512 devices in a mesh: tm: 4 (over y_hi, core), slab: 8 (over z), coarse: 16 (over x, y_lo).
Axes of the slice: x: 4, y: 8 (y_hi: 2, y_lo: 4; y = y_hi * 4 + y_lo), z: 8, core: 2. Of those that a mesh axis runs over, the one named last changes fastest.
Arguments:
- states: float32 [4, 32, 256, 256], P('tm', 'slab', 'coarse'), may hold values from -6 to 6
- diffusivity: float32 [32, 256, 256], P('slab', 'coarse'), may hold values from 0.25 to 2
- velocity: float32 [3, 32, 256, 256], P(None, 'slab', 'coarse'), may hold values from -0.5 to 0.5
Outputs:
- new_states: float32 [4, 32, 256, 256], P('tm', 'slab', 'coarse')
The draws below stay inside these ranges and needn't reach their ends.
All inputs are finite; a program needn't handle non-finite values.
Results may differ from the reference program's by a relative error of at most 0.0001.
Values sent between devices are 32-bit elements; how exact they have to be, the bound alone decides.
A program may use at most 64 MiB of HBM per device.

```python
import math
import jax
import jax.numpy as jnp

NY = 256
SECTIONS = 4
FINE_STEPS = 2
SPANS = 4
NZ = 32
NX = 256


def shard_levels(rng, extent, cuts, low, top_value):
    factor_of = 1.0
    for position, parts in cuts:
        heights = jax.random.uniform(jax.random.fold_in(jax.random.fold_in(rng, 6), position), (parts,), jnp.float32, low / len(cuts), top_value / len(cuts))
        factor_of = factor_of * jnp.repeat(jnp.exp(heights), extent[position] // parts).reshape((-1,) + (1,) * (len(extent) - 1 - position))
    return factor_of


def normal_values(own_key, shape, scale, limit, split=(), kind=jnp.bfloat16):
    array = scale * jax.random.normal(own_key, shape, jnp.float32)
    if split:
        array = array * shard_levels(own_key, shape, split, -0.22, 0.18)
    return jnp.clip(array, -limit, limit).astype(kind)


def setup_inputs(seed: int = 0) -> dict:
    key_list = jax.random.split(jax.random.key(seed), 4)
    return {
        "states": normal_values(key_list[0], (SPANS, NZ, NX, NY), 1.0, 6.0, ((0, 4), (1, 8), (2, 16)), jnp.float32),
        "diffusivity": jnp.clip(jnp.exp(math.log(2.0) - 2.0794415 * jax.random.uniform(key_list[1], (NZ, NX, NY), jnp.float32) ** shard_levels(key_list[1], (NZ, NX, NY), ((0, 8), (1, 16)), -0.2, 0.2)), 0.25, 2.0),
        "velocity": jnp.clip(jax.random.uniform(key_list[2], (3, NZ, NX, NY), jnp.float32, -0.5, 0.5) * shard_levels(key_list[2], (3, NZ, NX, NY), ((1, 8), (2, 16)), -0.4, 0.0), -0.5, 0.5),
    }


fine_step = 1.0
relaxation = 0.8


def chebyshev_coefficients(sections):
    damping = 0.05
    centre_point = 1.0 + damping / (sections * sections)
    chebyshev = [1.0, centre_point]
    slopes = [0.0, 1.0]
    for degree in range(2, sections + 1):
        chebyshev.append(2.0 * centre_point * chebyshev[degree - 1] - chebyshev[degree - 2])
        slopes.append(2.0 * chebyshev[degree - 1] + 2.0 * centre_point * slopes[degree - 1] - slopes[degree - 2])
    slope_ratio = chebyshev[sections] / slopes[sections]
    weights = [1.0 / entry for entry in chebyshev]
    scales = [0.0, 0.0]
    carries = [0.0, 0.0]
    tildes = [0.0, slope_ratio / centre_point]
    for degree in range(2, sections + 1):
        scales.append(2.0 * weights[degree] * centre_point / weights[degree - 1])
        carries.append(-weights[degree] / weights[degree - 2])
        tildes.append(2.0 * weights[degree] * slope_ratio / weights[degree - 1])
    return scales, carries, tildes


def stencil(padded, coeffs, spacing):
    centre = padded[1:-1, 1:-1, 1:-1]
    depth_after = padded[2:, 1:-1, 1:-1]
    depth_before = padded[:-2, 1:-1, 1:-1]
    row_after = padded[1:-1, 2:, 1:-1]
    row_before = padded[1:-1, :-2, 1:-1]
    column_after = padded[1:-1, 1:-1, 2:]
    column_before = padded[1:-1, 1:-1, :-2]
    beside_all = depth_after + depth_before + row_after + row_before + column_after + column_before
    spread = coeffs[0] * (beside_all - 6.0 * centre) / (spacing * spacing)
    drifts = (coeffs[1] * (depth_after - depth_before) + coeffs[2] * (row_after - row_before) + coeffs[3] * (column_after - column_before)) / (2.0 * spacing)
    return spread - drifts


def shrink(values):
    return values.reshape(values.shape[0] // 2, 2, values.shape[1] // 2, 2, values.shape[2] // 2, 2).mean(axis=(1, 3, 5))


def expand(values):
    return jnp.repeat(jnp.repeat(jnp.repeat(values, 2, 0), 2, 1), 2, 2)


def padding(values):
    return jnp.pad(values, 1)


def coarse_step(source, coeffs, coarse_coeffs):
    interval = FINE_STEPS * fine_step
    diagonal = 1.0 + 6.0 * interval * coeffs[0]

    def misfit(trial):
        return source - (trial - interval * stencil(padding(trial), coeffs, 1.0))

    smoothed = source + relaxation * misfit(source) / diagonal
    coarse_source = shrink(misfit(smoothed))
    coarse_diagonal = 1.0 + 6.0 * interval * coarse_coeffs[0] / 4.0
    guess_one = relaxation * coarse_source / coarse_diagonal
    coarse_misfit = coarse_source - (guess_one - interval * stencil(padding(guess_one), coarse_coeffs, 2.0))
    guess_two = guess_one + relaxation * coarse_misfit / coarse_diagonal
    second = smoothed + expand(guess_two)
    return second + relaxation * misfit(second) / diagonal


def fine_propagate(start_field, coeffs):
    scales, carries, tildes = chebyshev_coefficients(SECTIONS)
    for repeat in range(FINE_STEPS):
        before = start_field
        current = start_field + tildes[1] * fine_step * stencil(padding(start_field), coeffs, 1.0)
        for degree in range(2, SECTIONS + 1):
            update = scales[degree] * current + carries[degree] * before + tildes[degree] * fine_step * stencil(padding(current), coeffs, 1.0)
            before, current = current, update
        start_field = current
    return start_field


def reference(states, diffusivity, velocity):
    coeffs = jnp.concatenate([diffusivity[None], velocity], 0)
    coarse_coeffs = jnp.stack([shrink(coeffs[number]) for number in range(4)])
    corrections = []
    for period in range(SPANS):
        fine_end = fine_propagate(states[period], coeffs)
        corrections.append(fine_end - coarse_step(states[period], coeffs, coarse_coeffs))
    current = states[0]
    outputs = []
    for period in range(SPANS):
        current = coarse_step(current, coeffs, coarse_coeffs) + corrections[period]
        outputs.append(current)
    return jnp.stack(outputs)
```

```python
import jax
import jax.numpy as jnp
from jax import lax
from jax.experimental import pallas as pl
from jax.experimental.pallas import tpu as pltpu
from jax.sharding import PartitionSpec as P

MESH = pl.DeviceIdType.MESH
SECTIONS = 4
RELAX = 0.8


def chebyshev_coefficients(sections):
    damping = 0.05
    centre_point = 1.0 + damping / (sections * sections)
    chebyshev = [1.0, centre_point]
    slopes = [0.0, 1.0]
    for degree in range(2, sections + 1):
        chebyshev.append(2.0 * centre_point * chebyshev[degree - 1] - chebyshev[degree - 2])
        slopes.append(
            2.0 * chebyshev[degree - 1]
            + 2.0 * centre_point * slopes[degree - 1]
            - slopes[degree - 2]
        )
    slope_ratio = chebyshev[sections] / slopes[sections]
    weights = [1.0 / entry for entry in chebyshev]
    scales = [0.0, 0.0]
    carries = [0.0, 0.0]
    tildes = [0.0, slope_ratio / centre_point]
    for degree in range(2, sections + 1):
        scales.append(2.0 * weights[degree] * centre_point / weights[degree - 1])
        carries.append(-weights[degree] / weights[degree - 2])
        tildes.append(2.0 * weights[degree] * slope_ratio / weights[degree - 1])
    return (scales, carries, tildes)


DIRS = ((1, 0), (-1, 0), (0, 1), (0, -1), (1, 1), (1, -1), (-1, 1), (-1, -1))


def cuts(step, low, count, wide):
    if step == 0:
        return pl.ds(low, count), pl.ds(low, count)
    if step == 1:
        return pl.ds(low + count - wide, wide), pl.ds(low - wide, wide)
    return pl.ds(low, wide), pl.ds(low + count, wide)


def fine_box(d, deep, rows, corner):
    dz, dr = d
    hz, hr = (corner, corner) if dz and dr else (deep, rows)
    z_src, z_dst = cuts(dz, 4, 4, hz)
    every = pl.ds(0, 2)
    if dr == 0:
        box = (pl.ds(0, 4), every, pl.ds(2, 4))
        return (z_src, *box), (z_dst, *box)
    rows_at = pl.ds(4 - hr, hr) if dr == 1 else pl.ds(0, hr)
    s_src, s_dst = (5, 1) if dr == 1 else (2, 6)
    return (
        (z_src, rows_at, every, pl.ds(s_src, 1)),
        (z_dst, rows_at, every, pl.ds(s_dst, 1)),
    )


def coarse_box(d):
    dz, dr = d
    deep, rows = (1, 1) if dz and dr else (2, 2)
    z_src, z_dst = cuts(dz, 2, 2, deep)
    if dr == 0:
        return (z_src, pl.ds(0, 2), pl.ds(2, 4)), (z_dst, pl.ds(0, 2), pl.ds(2, 4))
    rows_at = pl.ds(2 - rows, rows) if dr == 1 else pl.ds(0, rows)
    s_src, s_dst = (5, 1) if dr == 1 else (2, 6)
    return (z_src, rows_at, pl.ds(s_src, 1)), (z_dst, rows_at, pl.ds(s_dst, 1))


def lanes(shape):
    return lax.broadcasted_iota(jnp.int32, shape, len(shape) - 1)


def around(centre, fine):
    axis = centre.ndim - 2
    row_after = jnp.concatenate([centre[1:], pltpu.roll(centre[:1], 7, axis)], 0)
    row_before = jnp.concatenate([pltpu.roll(centre[-1:], 1, axis), centre[:-1]], 0)
    if fine:
        even, odd = centre[:, 0], centre[:, 1]
    else:
        even, odd = centre, centre
    at = lanes(even.shape)
    last = even.ndim - 1
    shifted_up = jnp.where(at == 127, 0.0, pltpu.roll(even, 127, last))
    shifted_down = jnp.where(at == 0, 0.0, pltpu.roll(odd, 1, last))
    if not fine:
        return row_after, row_before, shifted_up, shifted_down
    return (
        row_after,
        row_before,
        jnp.stack([odd, shifted_up], 1),
        jnp.stack([shifted_down, even], 1),
    )


def operator(field, coeffs, z, fine=True):
    centre, after, before = field[z], field[z + 1], field[z - 1]
    ra, rb, ca, cb = around(centre, fine)
    spread = coeffs[0, z] * (after + before + ra + rb + ca + cb - 6.0 * centre)
    drift = coeffs[1, z] * (after - before) + coeffs[2, z] * (ra - rb) + coeffs[3, z] * (ca - cb)
    return centre, spread, drift


def spread_out(value):
    wide = jnp.concatenate([value[:1], value[:1], value[1:], value[1:]], 0)
    return jnp.stack([wide, wide], 1)


def gathered(value, index):
    return jnp.take_along_axis(value, index, axis=1, mode="promise_in_bounds")


def split_columns(rows):
    low, high = rows[:, :128], rows[:, 128:]
    at = lanes(low.shape)
    source = (2 * at) % 128
    first = at < 64
    even = jnp.where(first, gathered(low, source), gathered(high, source))
    odd = jnp.where(first, gathered(low, source + 1), gathered(high, source + 1))
    return even, odd


def join_columns(even, odd):
    at = lanes(even.shape)
    half = at // 2
    is_even = at % 2 == 0
    low = jnp.where(is_even, gathered(even, half), gathered(odd, half))
    high = jnp.where(is_even, gathered(even, half + 64), gathered(odd, half + 64))
    return low, high


def kernel(
    s_ref, d_ref, v_ref, o_ref,
    own, co, sa, sb, ta, ua, weight, fe, bb, v1, v2, e1, e2, cco, cweight,
    fx, sx, xin, xout, res, dealt,
    s_send, s_recv, c_send, c_recv, f_send, f_recv, b_send, b_recv, e_send, e_recv, m_send, m_recv,
):
    tm, slab, coarse = (lax.axis_index(a) for a in ("tm", "slab", "coarse"))
    slabs, coarses = lax.axis_size("slab"), lax.axis_size("coarse")

    def at(dz, dr):
        z, r = slab + dz, coarse + dr
        return z, r, (z >= 0) & (z < slabs) & (r >= 0) & (r < coarses)

    sibling = tm + 1 - 2 * lax.rem(tm, 2)
    barrier = pltpu.get_barrier_semaphore()
    count = jnp.int32(1)
    pl.semaphore_signal(barrier, inc=1, device_id=(sibling, slab, coarse), device_id_type=MESH)
    for dz, dr in DIRS:
        z, r, there = at(dz, dr)

        @pl.when(there)
        def _():
            for t in (tm, sibling):
                pl.semaphore_signal(barrier, inc=1, device_id=(t, z, r), device_id_type=MESH)

        count = count + 2 * there.astype(jnp.int32)
    for a, b in ((1, 2), (1, 3)):
        for me, other in ((a, b), (b, a)):
            here = tm == me

            @pl.when(here)
            def _():
                pl.semaphore_signal(
                    barrier, inc=1, device_id=(other, slab, coarse), device_id_type=MESH
                )

            count = count + here.astype(jnp.int32)

    def arrange(z, _):
        for source, target, scale in (
            (s_ref.at[z], own.at[z], None),
            (d_ref.at[z], co.at[0, z + 4], None),
            (v_ref.at[0, z], co.at[1, z + 4], 0.5),
            (v_ref.at[1, z], co.at[2, z + 4], 0.5),
            (v_ref.at[2, z], co.at[3, z + 4], 0.5),
        ):
            for p, part in enumerate(split_columns(source[...])):
                dealt[z, p] = part if scale is None else scale * part
                for i in range(4):
                    target[i, p, 2:6, :] = dealt[z, p, pl.ds(i, 4, stride=4), :]
        return 0

    lax.fori_loop(0, 4, arrange, 0)
    pl.semaphore_wait(barrier, count)

    def copy(src, dst, send, recv, device):
        return pltpu.make_async_remote_copy(
            src_ref=src, dst_ref=dst, send_sem=send, recv_sem=recv, device_id=device, device_id_type=MESH
        )

    def own_box(z):
        return (pl.ds(z, 4), pl.ds(0, 4), pl.ds(0, 2), pl.ds(2, 4))

    def state_copy(n):
        if n == 8:
            return copy(
                own.at[own_box(0)], sa.at[own_box(4)], s_send.at[8], s_recv.at[8],
                (sibling, slab, coarse),
            )
        z, r, _ = at(*DIRS[n])
        (zs, *src), dst = fine_box(DIRS[n], 4, 4, 3)
        src = (pl.ds(zs.start - 4, zs.size), *src)
        return copy(own.at[src], sa.at[dst], s_send.at[n], s_recv.at[n], (sibling, z, r))

    def coeff_copy(n):
        z, r, _ = at(*DIRS[n])
        src, dst = fine_box(DIRS[n], 3, 3, 2)
        every = pl.ds(0, 4)
        return copy(
            co.at[(every, *src)], co.at[(every, *dst)], c_send.at[n], c_recv.at[n], (tm, z, r)
        )

    def step_copy(n):
        z, r, _ = at(*DIRS[n])
        src, dst = fine_box(DIRS[n], 4, 4, 3)
        return copy(sb.at[src], sb.at[dst], f_send.at[n], f_recv.at[n], (tm, z, r))

    def solve_copy(k):
        def make(n):
            z, r, _ = at(*DIRS[n])
            src, dst = fine_box(DIRS[n], 2, 2, 1)
            return copy(
                bb.at[(k, *src)], bb.at[(k, *dst)], b_send.at[k, n], b_recv.at[k, n], (tm, z, r)
            )

        return make

    def guess_copy(k):
        def make(n):
            z, r, _ = at(*DIRS[n])
            src, dst = coarse_box(DIRS[n])
            return copy(
                e1.at[(k, *src)], e1.at[(k, *dst)], e_send.at[k, n], e_recv.at[k, n], (tm, z, r)
            )

        return make

    def start(make, order=range(8)):
        for n in order:
            _, _, there = at(*DIRS[n])
            pl.when(there)(lambda n=n: make(n).start())

    def arrive(make):
        for n in range(8):
            _, _, there = at(-DIRS[n][0], -DIRS[n][1])
            pl.when(there)(lambda n=n: make(n).wait_recv())

    def sent(make):
        for n in range(8):
            _, _, there = at(*DIRS[n])
            pl.when(there)(lambda n=n: make(n).wait_send())

    far = (4, 5, 6, 7, 2, 3, 0, 1)
    start(state_copy, far)
    state_copy(8).start()
    start(coeff_copy, far)

    here = (slab, coarse)
    window = copy(own.at[own_box(0)], sx.at[own_box(0)], m_send.at[0], m_recv.at[0], (1, *here))
    pl.when(tm == 2)(window.start)

    def outside(edge, layers, sublanes, coarse_layers):
        @pl.when(edge)
        def _():
            z, n = layers
            zero = jnp.zeros((4, 2, sublanes[1], 128), jnp.float32)
            s = pl.ds(*sublanes)

            def clear(q, _):
                for m in range(4):
                    co[m, z + q, :, :, s, :] = zero
                for field in (sa, sb, bb.at[0], bb.at[1], bb.at[2]):
                    field[z + q, :, :, s, :] = zero
                return 0

            lax.fori_loop(0, n, clear, 0)
            for k in range(3):
                for q in range(coarse_layers[0], coarse_layers[0] + coarse_layers[1]):
                    e1[k, q, :, s, :] = jnp.zeros((2, sublanes[1], 128), jnp.float32)

    outside(slab == 0, (0, 4), (0, 8), (0, 2))
    outside(slab == slabs - 1, (8, 4), (0, 8), (4, 2))
    outside(coarse == 0, (0, 12), (1, 1), (0, 6))
    outside(coarse == coarses - 1, (0, 12), (6, 1), (0, 6))

    arrive(state_copy)
    state_copy(8).wait_recv()
    arrive(coeff_copy)

    scales, carries, tildes = chebyshev_coefficients(SECTIONS)

    def loop(low, high, body):
        def wrapped(z, _):
            body(z)
            return 0

        lax.fori_loop(low, high, wrapped, 0, unroll=2)

    def fine_step(begin, finish):
        def first(z):
            centre, spread, drift = operator(begin, co, z)
            ta[z] = centre + tildes[1] * (spread - drift)

        def later(degree, current, before, put):
            def body(z):
                centre, spread, drift = operator(current, co, z)
                put(
                    z,
                    scales[degree] * centre
                    + carries[degree] * before[z]
                    + tildes[degree] * (spread - drift),
                )

            return body

        def put_to(ref):
            def put(z, value):
                ref[z] = value

            return put

        loop(1, 11, first)
        loop(2, 10, later(2, ta, begin, put_to(ua)))
        loop(3, 9, later(3, ua, ta, put_to(ta)))
        loop(4, 8, later(4, ta, ua, finish))

    def to_sb(z, value):
        sb[z, :, :, 2:6, :] = value[:, :, 2:6, :]

    def to_fe(z, value):
        fe[z - 4] = value

    fine_step(sa, to_sb)
    start(step_copy, far)

    def weigh(z):
        weight[z] = RELAX / (1.0 + 12.0 * co[0, z])

    loop(3, 9, weigh)

    def coarse_weigh(q):
        for m in range(4):
            total = co[m, 2 * q] + co[m, 2 * q + 1]
            total = total[:, 0] + total[:, 1]
            total = jnp.concatenate([total[0:1] + total[1:2], total[2:3] + total[3:4]], 0)
            mean = 0.125 * total
            cco[m, q] = mean
            if m == 0:
                cweight[q] = RELAX / (1.0 + 3.0 * mean)

    loop(1, 5, coarse_weigh)
    arrive(step_copy)
    fine_step(sb, to_fe)

    is_lead = lax.rem(tm, 2) == 1
    ends = copy(fe, fx, m_send.at[1], m_recv.at[1], (sibling, *here))
    ends_first = copy(fe, res, m_send.at[1], m_recv.at[1], (sibling, *here))
    crossing = copy(xout, xin, m_send.at[2], m_recv.at[2], (3, *here))
    third = copy(res, res, m_send.at[3], m_recv.at[3], (2, *here))
    pl.when(jnp.logical_not(is_lead))(ends.start)
    pl.when(tm == 1)(ends_first.start)

    def to_bb(k, z, value):
        bb[k, z + 4, :, :, 2:6, :] = value[:, :, 2:6, :]

    @pl.when(tm == 1)
    def _():
        for z in range(4):
            to_bb(0, z, fe[z] - own[z])

    @pl.when(tm == 3)
    def _():
        crossing.wait_recv()
        for z in range(4):
            value = fe[z] + xin[z]
            res[z] = value
            to_bb(2, z, value - own[z])
        third.start()

    def solve(k, _):
        b = bb.at[k]
        start(solve_copy(k), far)
        arrive(solve_copy(k))

        def smooth(z):
            centre, spread, drift = operator(b, co, z)
            v1[z] = centre + (2.0 * weight[z]) * (spread - drift)

        loop(3, 9, smooth)

        def restrict(q):
            total = None
            for z in (2 * q, 2 * q + 1):
                centre, spread, drift = operator(v1, co, z)
                misfit = b[z] - centre + 2.0 * (spread - drift)
                total = misfit if total is None else total + misfit
            total = total[:, 0] + total[:, 1]
            total = jnp.concatenate([total[0:1] + total[1:2], total[2:3] + total[3:4]], 0)
            guess = cweight[q] * (0.125 * total)
            e1[k, q, :, 2:6, :] = guess[:, 2:6, :]

        loop(2, 4, restrict)
        start(guess_copy(k), far)
        arrive(guess_copy(k))

        def correct(q):
            centre, spread, drift = operator(e1.at[k], cco, q, fine=False)
            w = cweight[q]
            second = (2.0 - w) * centre + w * (0.5 * spread - drift)
            wide = spread_out(second)
            for z in (2 * q, 2 * q + 1):
                v2[z] = v1[z] + wide

        loop(1, 5, correct)

        def finish(z):
            centre, spread, drift = operator(v2, co, z)
            xout[z - 4] = centre + weight[z] * (b[z] - centre + 2.0 * (spread - drift))

        loop(4, 8, finish)

        @pl.when(k == 0)
        def _():
            ends.wait_recv()
            window.wait_recv()
            for z in range(4):
                value = fx[z] + xout[z]
                res[z] = value
                to_bb(1, z, value - sx[z])

        @pl.when(k == 1)
        def _():
            crossing.start()

        sent(solve_copy(k))
        sent(guess_copy(k))
        return 0

    low = jnp.where(tm == 1, 0, 2)
    high = jnp.where(tm == 1, 2, jnp.where(tm == 3, 3, 2))
    lax.fori_loop(low, high, solve, 0)

    @pl.when(tm == 3)
    def _():
        ends.wait_recv()
        third.wait_send()
        for z in range(4):
            res[z] = fx[z] + xout[z]

    pl.when(tm == 0)(ends_first.wait_recv)
    pl.when(tm == 2)(third.wait_recv)

    def give(z, _):
        for p in range(2):
            for i in range(4):
                dealt[z, p, pl.ds(i, 4, stride=4), :] = res[z, i, p, 2:6, :]
        low_part, high_part = join_columns(dealt[z, 0], dealt[z, 1])
        o_ref[z, :, 0:128] = low_part
        o_ref[z, :, 128:256] = high_part
        return 0

    lax.fori_loop(0, 4, give, 0)

    sent(state_copy)
    state_copy(8).wait_send()
    sent(coeff_copy)
    sent(step_copy)
    pl.when(tm == 2)(window.wait_send)
    pl.when(jnp.logical_not(is_lead))(ends.wait_send)
    pl.when(tm == 1)(ends_first.wait_send)
    pl.when(tm == 1)(crossing.wait_send)


def per_device(states, diffusivity, velocity):
    def vmem(*shape):
        return pltpu.VMEM(shape + (8, 128), jnp.float32)

    dma = pltpu.SemaphoreType.DMA
    block = pl.BlockSpec(memory_space=pltpu.VMEM)
    out = pl.pallas_call(
        kernel,
        name="parareal",
        out_shape=jax.ShapeDtypeStruct(diffusivity.shape, jnp.float32),
        in_specs=[block] * 3,
        out_specs=block,
        scratch_shapes=[
            vmem(4, 4, 2),
            vmem(4, 12, 4, 2),
            vmem(12, 4, 2),
            vmem(12, 4, 2),
            vmem(12, 4, 2),
            vmem(12, 4, 2),
            vmem(12, 4, 2),
            vmem(4, 4, 2),
            vmem(3, 12, 4, 2),
            vmem(12, 4, 2),
            vmem(12, 4, 2),
            vmem(3, 6, 2),
            vmem(6, 2),
            vmem(4, 6, 2),
            vmem(6, 2),
            vmem(4, 4, 2),
            vmem(4, 4, 2),
            vmem(4, 4, 2),
            vmem(4, 4, 2),
            vmem(4, 4, 2),
            pltpu.VMEM((4, 2, 16, 128), jnp.float32),
            dma((9,)), dma((9,)), dma((8,)), dma((8,)), dma((8,)), dma((8,)),
            dma((3, 8)), dma((3, 8)), dma((3, 8)), dma((3, 8)), dma((4,)), dma((4,)),
        ],
        compiler_params=pltpu.CompilerParams(
            collective_id=0, has_side_effects=True, vmem_limit_bytes=32 * 1024 * 1024
        ),
    )(states[0], diffusivity, velocity)
    return out[None]


def solution(mesh):
    return jax.shard_map(
        per_device,
        mesh=mesh,
        in_specs=(
            P("tm", "slab", "coarse", None),
            P("slab", "coarse", None),
            P(None, "slab", "coarse", None),
        ),
        out_specs=P("tm", "slab", "coarse", None),
        check_vma=False,
    )
```

```python
import jax
import jax.numpy as jnp
from jax import lax
from jax.experimental import pallas as pl
from jax.experimental.pallas import tpu as pltpu
from jax.sharding import PartitionSpec as P

MESH = pl.DeviceIdType.MESH
SECTIONS = 4
RELAX = 0.8


def chebyshev_coefficients(sections):
    damping = 0.05
    centre_point = 1.0 + damping / (sections * sections)
    chebyshev = [1.0, centre_point]
    slopes = [0.0, 1.0]
    for degree in range(2, sections + 1):
        chebyshev.append(2.0 * centre_point * chebyshev[degree - 1] - chebyshev[degree - 2])
        slopes.append(
            2.0 * chebyshev[degree - 1]
            + 2.0 * centre_point * slopes[degree - 1]
            - slopes[degree - 2]
        )
    slope_ratio = chebyshev[sections] / slopes[sections]
    weights = [1.0 / entry for entry in chebyshev]
    scales = [0.0, 0.0]
    carries = [0.0, 0.0]
    tildes = [0.0, slope_ratio / centre_point]
    for degree in range(2, sections + 1):
        scales.append(2.0 * weights[degree] * centre_point / weights[degree - 1])
        carries.append(-weights[degree] / weights[degree - 2])
        tildes.append(2.0 * weights[degree] * slope_ratio / weights[degree - 1])
    return (scales, carries, tildes)


DIRS = ((1, 0), (-1, 0), (0, 1), (0, -1), (1, 1), (1, -1), (-1, 1), (-1, -1))


def cuts(step, low, count, wide):
    if step == 0:
        return pl.ds(low, count), pl.ds(low, count)
    if step == 1:
        return pl.ds(low + count - wide, wide), pl.ds(low - wide, wide)
    return pl.ds(low, wide), pl.ds(low + count, wide)


def fine_box(d, deep, rows, corner, blocks=1):
    dz, dr = d
    hz, hr = corner if dz and dr else (deep, rows)
    z_src, z_dst = cuts(dz, 4, 4, hz)
    every = pl.ds(0, 2)
    if dr == 0:
        box = (pl.ds(0, 4), every, pl.ds(2, 4))
        return (z_src, *box), (z_dst, *box)
    rows_at = pl.ds(4 - hr, hr) if dr == 1 else pl.ds(0, hr)
    s_src, s_dst = (6 - blocks, 2 - blocks) if dr == 1 else (2, 6)
    return (
        (z_src, rows_at, every, pl.ds(s_src, blocks)),
        (z_dst, rows_at, every, pl.ds(s_dst, blocks)),
    )


def coarse_box(d, blocks):
    dz, dr = d
    z_src, z_dst = cuts(dz, 2, 2, 2)
    every = pl.ds(0, 2)
    if dr == 0:
        return (z_src, every, pl.ds(2, 4)), (z_dst, every, pl.ds(2, 4))
    blocks = 1 if dz else blocks
    s_src, s_dst = (6 - blocks, 2 - blocks) if dr == 1 else (2, 6)
    return (z_src, every, pl.ds(s_src, blocks)), (z_dst, every, pl.ds(s_dst, blocks))


def lanes(shape):
    return lax.broadcasted_iota(jnp.int32, shape, len(shape) - 1)


def around(centre, fine):
    axis = centre.ndim - 2
    row_after = jnp.concatenate([centre[1:], pltpu.roll(centre[:1], 7, axis)], 0)
    row_before = jnp.concatenate([pltpu.roll(centre[-1:], 1, axis), centre[:-1]], 0)
    if fine:
        even, odd = centre[:, 0], centre[:, 1]
    else:
        even, odd = centre, centre
    at = lanes(even.shape)
    last = even.ndim - 1
    shifted_up = jnp.where(at == 127, 0.0, pltpu.roll(even, 127, last))
    shifted_down = jnp.where(at == 0, 0.0, pltpu.roll(odd, 1, last))
    if not fine:
        return row_after, row_before, shifted_up, shifted_down
    return (
        row_after,
        row_before,
        jnp.stack([odd, shifted_up], 1),
        jnp.stack([shifted_down, even], 1),
    )


def operator(field, coeffs, z, fine=True):
    centre, after, before = field[z], field[z + 1], field[z - 1]
    ra, rb, ca, cb = around(centre, fine)
    spread = coeffs[0, z] * (after + before + ra + rb + ca + cb - 6.0 * centre)
    drift = coeffs[1, z] * (after - before) + coeffs[2, z] * (ra - rb) + coeffs[3, z] * (ca - cb)
    return centre, spread, drift


def spread_out(value):
    wide = jnp.concatenate([value[:1], value[:1], value[1:], value[1:]], 0)
    return jnp.stack([wide, wide], 1)


def gathered(value, index):
    return jnp.take_along_axis(value, index, axis=1, mode="promise_in_bounds")


def split_columns(rows):
    low, high = rows[:, :128], rows[:, 128:]
    at = lanes(low.shape)
    source = (2 * at) % 128
    first = at < 64
    even = jnp.where(first, gathered(low, source), gathered(high, source))
    odd = jnp.where(first, gathered(low, source + 1), gathered(high, source + 1))
    return even, odd


def join_columns(even, odd):
    at = lanes(even.shape)
    half = at // 2
    is_even = at % 2 == 0
    low = jnp.where(is_even, gathered(even, half), gathered(odd, half))
    high = jnp.where(is_even, gathered(even, half + 64), gathered(odd, half + 64))
    return low, high


def kernel(
    s_hbm, d_hbm, v_hbm, o_ref,
    s_ref, d_ref, v_ref,
    own, co, cw, sa, sb, ta, ua, weight, fe, jo, jj, bb, v1, v2, vr, e1, cco, cweight,
    fx, sx, xout, res, dealt,
    in_sem, s_send, s_recv, c_send, c_recv, w_send, w_recv, g_send, g_recv,
    f_send, f_recv, b_send, b_recv, e_send, e_recv, r_send, r_recv, x_send, x_recv,
    m_send, m_recv,
):
    tm, slab, coarse = (lax.axis_index(a) for a in ("tm", "slab", "coarse"))
    slabs, coarses = lax.axis_size("slab"), lax.axis_size("coarse")
    loads = [
        pltpu.make_async_copy(src, dst, in_sem.at[n])
        for n, (src, dst) in enumerate(((s_hbm, s_ref), (d_hbm, d_ref), (v_hbm, v_ref)))
    ]
    for load in loads:
        load.start()

    def at(dz, dr):
        z, r = slab + dz, coarse + dr
        return z, r, (z >= 0) & (z < slabs) & (r >= 0) & (r < coarses)

    core = lax.rem(tm, 2)
    is_lead = core == 1
    sibling = tm + 1 - 2 * core
    across = lax.rem(tm + 2, 4)
    here = (slab, coarse)

    barrier = pltpu.get_barrier_semaphore()
    count = jnp.int32(2)
    for dz, dr in DIRS:
        z, r, there = at(dz, dr)

        @pl.when(there)
        def _():
            for t in (tm, sibling):
                pl.semaphore_signal(barrier, inc=1, device_id=(t, z, r), device_id_type=MESH)

        count = count + 2 * there.astype(jnp.int32)
    for t in (across, sibling):
        pl.semaphore_signal(barrier, inc=1, device_id=(t, *here), device_id_type=MESH)

    def arrange(z, _):
        for source, target, scale in (
            (s_ref.at[z], own.at[z], None),
            (d_ref.at[z], co.at[0, z + 4], None),
            (v_ref.at[0, z], co.at[1, z + 4], 0.5),
            (v_ref.at[1, z], co.at[2, z + 4], 0.5),
            (v_ref.at[2, z], co.at[3, z + 4], 0.5),
        ):
            for p, part in enumerate(split_columns(source[...])):
                dealt[z, p] = part if scale is None else scale * part
                for i in range(4):
                    target[i, p, 2:6, :] = dealt[z, p, pl.ds(i, 4, stride=4), :]
        return 0

    for load in loads:
        load.wait()
    lax.fori_loop(0, 4, arrange, 0)
    pl.semaphore_wait(barrier, count)

    def copy(src, dst, send, recv, device):
        return pltpu.make_async_remote_copy(
            src_ref=src, dst_ref=dst, send_sem=send, recv_sem=recv, device_id=device, device_id_type=MESH
        )

    def own_box(z):
        return (pl.ds(z, 4), pl.ds(0, 4), pl.ds(0, 2), pl.ds(2, 4))

    every = pl.ds(0, 4)
    both = pl.ds(0, 2)

    def state_copy(n):
        z, r, _ = at(*DIRS[n])
        (zs, *src), dst = fine_box(DIRS[n], 4, 4, (3, 3))
        src = (pl.ds(zs.start - 4, zs.size), *src)
        return copy(own.at[src], sa.at[dst], s_send.at[n], s_recv.at[n], (sibling, z, r))

    swap = copy(
        own.at[own_box(0)], sa.at[own_box(4)], s_send.at[8], s_recv.at[8], (sibling, *here)
    )

    def coeff_copy(n):
        z, r, _ = at(*DIRS[n])
        src, dst = fine_box(DIRS[n], 3, 3, (2, 2))
        return copy(
            co.at[(every, *src)], co.at[(every, *dst)], c_send.at[n], c_recv.at[n], (tm, z, r)
        )

    def coeff_pass(n):
        box = (every, *fine_box(DIRS[n], 3, 3, (2, 2))[1])
        return copy(co.at[box], co.at[box], w_send.at[n], w_recv.at[n], (sibling, *here))

    more = []
    for n, (dz, dr) in enumerate(DIRS):
        if dr == 0:
            continue
        z_src, z_dst = cuts(dz, 4, 4, 1 if dz else 4)
        near, away = ((5, 1), (4, 0)) if dr == 1 else ((2, 6), (3, 7))
        more.append((n, (z_src, every, both, pl.ds(away[0], 1)), (z_dst, every, both, pl.ds(away[1], 1))))
        if dz:
            part = pl.ds(0, 2) if dr == 1 else pl.ds(2, 2)
            more.append((n, (z_src, part, both, pl.ds(near[0], 1)), (z_dst, part, both, pl.ds(near[1], 1))))
        else:
            part = pl.ds(0, 1) if dr == 1 else pl.ds(3, 1)
            more.append((n, (z_src, part, both, pl.ds(near[0], 1)), (z_dst, part, both, pl.ds(near[1], 1))))
    more_dirs = [DIRS[n] for n, _, _ in more]

    def more_copy(q):
        n, src, dst = more[q]
        z, r, _ = at(*DIRS[n])
        return copy(
            co.at[(every, *src)], cw.at[(every, *dst)], g_send.at[q], g_recv.at[q], (tm, z, r)
        )

    def step_copy(n):
        z, r, _ = at(*DIRS[n])
        src, dst = fine_box(DIRS[n], 4, 4, (3, 3))
        return copy(sb.at[src], sb.at[dst], f_send.at[n], f_recv.at[n], (tm, z, r))

    def first_copy(n):
        z, r, _ = at(*DIRS[n])
        src, dst = fine_box(DIRS[n], 2, 4, (2, 4), blocks=2)
        return copy(bb.at[(0, *src)], bb.at[(0, *dst)], b_send.at[n], b_recv.at[n], (tm, z, r))

    def layer_copy(k):
        def make(n):
            z, r, _ = at(*DIRS[n])
            z_src, z_dst = cuts(DIRS[n][0], 4, 4, 2)
            box = (every, both, pl.ds(1, 6))
            sem = 8 * k + n
            return copy(
                bb.at[(k, z_src, *box)], bb.at[(k, z_dst, *box)], b_send.at[sem], b_recv.at[sem],
                (tm, z, r),
            )

        return make

    def flat_guess_copy(n):
        z, r, _ = at(*DIRS[n])
        z_src, z_dst = cuts(DIRS[n][0], 2, 2, 2)
        return copy(e1.at[0, z_src], e1.at[0, z_dst], e_send.at[n], e_recv.at[n], (tm, z, r))

    def guess_copy(n):
        z, r, _ = at(*DIRS[n])
        src, dst = coarse_box(DIRS[n], 2)
        return copy(
            e1.at[(1, *src)], e1.at[(1, *dst)], e_send.at[8 + n], e_recv.at[8 + n], (tm, z, r)
        )

    def last_guess_copy(n):
        if n == 8:
            box = (2, pl.ds(2, 2), both, pl.ds(2, 4))
            return copy(e1.at[box], e1.at[box], e_send.at[24], e_recv.at[24], (across, *here))
        z, r, _ = at(*DIRS[n])
        src, dst = coarse_box(DIRS[n], 1)
        return copy(
            e1.at[(2, *src)], e1.at[(2, *dst)], e_send.at[16 + n], e_recv.at[16 + n], (across, z, r)
        )

    def smooth_copy(n):
        z, r, _ = at(*DIRS[n])
        s_src, s_dst = (5, 1) if DIRS[n][1] == 1 else (2, 6)
        box = (pl.ds(3, 6), pl.ds(1, 2), both)
        return copy(
            v1.at[(*box, pl.ds(s_src, 1))], vr.at[(*box, pl.ds(s_dst, 1))],
            r_send.at[n], r_recv.at[n], (tm, z, r),
        )

    def jump_copy(field, n):
        z, r, _ = at(*DIRS[n])
        src, dst = fine_box(DIRS[n], 4, 2, (1, 1))
        return lambda target: copy(
            field.at[src], jj.at[(target, *dst)], r_send.at[n - 2], r_recv.at[n - 2 + 4 * target],
            ((sibling, z, r) if target == 0 else (tm, z, r)),
        )

    def start(make, order=range(8), dirs=DIRS):
        for n in order:
            _, _, there = at(*dirs[n])
            pl.when(there)(lambda n=n: make(n).start())

    def arrive(make, order=range(8), dirs=DIRS):
        for n in order:
            _, _, there = at(-dirs[n][0], -dirs[n][1])
            pl.when(there)(lambda n=n: make(n).wait_recv())

    def sent(make, order=range(8), dirs=DIRS):
        for n in order:
            _, _, there = at(*dirs[n])
            pl.when(there)(lambda n=n: make(n).wait_send())

    far = (4, 5, 6, 7, 2, 3, 0, 1)
    heavy = (0, 1, 4, 5, 6, 7, 2, 3)
    along = (0, 1)
    beside = (2, 3)
    pl.when(is_lead)(lambda: start(coeff_copy, heavy))
    start(state_copy, heavy)
    swap.start()

    window = copy(own, sx, m_send.at[0], m_recv.at[0], (across, *here))
    pl.when(tm == 2)(window.start)

    def zero(n):
        return jnp.zeros((4, 2, n, 128), jnp.float32)

    def loop(low, high, body, unroll=2):
        def wrapped(z, _):
            body(z)
            return 0

        lax.fori_loop(low, high, wrapped, 0, unroll=unroll)

    for edge, begin, begin_coarse in ((slab == 0, 0, 0), (slab == slabs - 1, 8, 4)):

        @pl.when(edge)
        def _():
            def clear(z):
                for m in range(4):
                    co[m, z] = zero(8)
                    cw[m, z] = zero(8)
                for field in (sa, sb, bb.at[0], bb.at[1], bb.at[2]):
                    field[z] = zero(8)

            loop(begin, begin + 4, clear)
            for k in range(3):
                for z in range(begin_coarse, begin_coarse + 2):
                    e1[k, z] = jnp.zeros((2, 8, 128), jnp.float32)

    for edge, begin in ((coarse == 0, 0), (coarse == coarses - 1, 6)):

        @pl.when(edge)
        def _():
            s = pl.ds(begin, 2)

            def clear(z):
                for m in range(4):
                    co[m, z, :, :, s, :] = zero(2)
                    cw[m, z, :, :, s, :] = zero(2)
                for field in (sa, sb, bb.at[0], vr):
                    field[z, :, :, s, :] = zero(2)

            loop(0, 12, clear)
            for k in range(2):

                @pl.when(tm == 1 + 2 * k)
                def _():
                    for z in range(4, 8):
                        jj[k, z, :, :, s, :] = zero(2)

            for k in (1, 2):
                for z in range(6):
                    e1[k, z, :, s, :] = jnp.zeros((2, 2, 128), jnp.float32)

    arrive(state_copy)
    swap.wait_recv()
    pl.when(is_lead)(lambda: arrive(coeff_copy))
    pl.when(jnp.logical_not(is_lead))(lambda: arrive(coeff_pass))

    scales, carries, tildes = chebyshev_coefficients(SECTIONS)

    def fine_step(begin, finish):
        def first(z):
            centre, spread, drift = operator(begin, co, z)
            ta[z] = centre + tildes[1] * (spread - drift)

        def later(degree, current, before, put):
            def body(z):
                centre, spread, drift = operator(current, co, z)
                put(
                    z,
                    scales[degree] * centre
                    + carries[degree] * before[z]
                    + tildes[degree] * (spread - drift),
                )

            return body

        def put_to(ref):
            def put(z, value):
                ref[z] = value

            return put

        loop(1, 11, first)
        loop(2, 10, later(2, ta, begin, put_to(ua)))
        loop(3, 9, later(3, ua, ta, put_to(ta)))
        loop(4, 8, later(4, ta, ua, finish))

    def to_own_rows(target, z, value):
        target[z, :, :, 2:6, :] = value[:, :, 2:6, :]

    def to_fe(z, value):
        fe[z - 4] = value

    fine_step(sa, lambda z, value: to_own_rows(sb, z, value))
    start(step_copy, far)

    @pl.when(is_lead)
    def _():
        for n in range(8):
            _, _, there = at(-DIRS[n][0], -DIRS[n][1])
            pl.when(there)(lambda n=n: coeff_pass(n).start())

    pl.when(tm == 1)(lambda: start(more_copy, range(len(more)), more_dirs))

    arrive(step_copy)
    fine_step(sb, to_fe)

    def weigh(z):
        weight[z] = RELAX / (1.0 + 12.0 * co[0, z])

    def halves(value):
        value = value[:, 0] + value[:, 1]
        return 0.125 * jnp.concatenate([value[0:1] + value[1:2], value[2:3] + value[3:4]], 0)

    def coarse_weigh(q):
        for m in range(4):
            mean = halves(co[m, 2 * q] + co[m, 2 * q + 1])
            cco[m, q] = mean
            if m == 0:
                cweight[q] = RELAX / (1.0 + 3.0 * mean)

    def merge(low, high, first, last):
        def body(z):
            for m in range(4):
                for part, sub in ((every, 0), (every, 7), (first, 1), (last, 6)):
                    at_rows = (m, z, part, slice(None), pl.ds(sub, 1), slice(None))
                    co[at_rows] = cw[at_rows]

        for z in range(low, high):
            body(z)

    def weights():
        loop(3, 9, weigh)
        loop(1, 5, coarse_weigh)

    ends = copy(fe, fx, m_send.at[1], m_recv.at[1], (sibling, *here))
    ends_first = copy(fe, res, m_send.at[1], m_recv.at[1], (sibling, *here))
    jump = copy(
        jo.at[own_box(4)], jj.at[(0, *own_box(4))], m_send.at[2], m_recv.at[2], (sibling, *here)
    )
    jump_box = (1, pl.ds(4, 4), every, both, pl.ds(1, 6))
    last_jump = copy(jj.at[jump_box], jj.at[jump_box], m_send.at[4], m_recv.at[4], (across, *here))
    third = copy(res, res, m_send.at[3], m_recv.at[3], (sibling, *here))
    cross_boxes = [(2, pl.ds(low, n), every, both, pl.ds(1, 6)) for low, n in ((4, 4), (2, 2), (8, 2))]

    def cross(n):
        box = cross_boxes[n]
        return copy(bb.at[box], bb.at[box], x_send.at[n], x_recv.at[n], (across, *here))

    @pl.when(tm == 0)
    def _():
        window.wait_recv()
        for z in range(4):
            jo[z + 4] = fe[z] - sx[z]
        start(lambda n: jump_copy(jo, n)(0), beside)
        jump.start()
        ends.start()
        ends_first.wait_recv()

    @pl.when(tm == 2)
    def _():
        ends.start()
        third.wait_recv()

    def solve_smooth(b):
        def smooth(z):
            centre, spread, drift = operator(b, co, z)
            v1[z] = centre + (2.0 * weight[z]) * (spread - drift)

        loop(3, 9, smooth)

    def solve_restrict(b, put):
        def restrict(q):
            total = None
            for z in (2 * q, 2 * q + 1):
                centre, spread, drift = operator(v1, co, z)
                misfit = b[z] - centre + 2.0 * (spread - drift)
                total = misfit if total is None else total + misfit
            put(q, cweight[q] * halves(total))

        loop(2, 4, restrict)

    def solve_correct(e, base):
        def correct(q):
            centre, spread, drift = operator(e, cco, q, fine=False)
            w = cweight[q]
            wide = spread_out((2.0 - w) * centre + w * (0.5 * spread - drift))
            for z in (2 * q, 2 * q + 1):
                v2[z] = base(z) + wide

        loop(1, 5, correct)

    def solve_finish(b, put):
        def finish(z):
            centre, spread, drift = operator(v2, co, z)
            put(z, centre + weight[z] * (b[z] - centre + 2.0 * (spread - drift)))

        loop(4, 8, finish)

    def put_guess(k):
        def put(q, value):
            e1[k, q, :, 2:6, :] = value[:, 2:6, :]

        return put

    @pl.when(tm == 1)
    def _():
        b = bb.at[0]
        for z in range(4):
            b[z + 4, :, :, 2:6, :] = (fe[z] - own[z])[:, :, 2:6, :]
        start(first_copy, far)
        ends_first.start()
        arrive(more_copy, range(len(more)), more_dirs)
        merge(4, 8, pl.ds(0, 1), pl.ds(3, 1))
        for z in (3, 8):
            merge(z, z + 1, pl.ds(0, 2), pl.ds(2, 2))
        weights()
        arrive(first_copy)
        solve_smooth(b)

        def put_flat(q, value):
            e1[0, q] = value

        solve_restrict(b, put_flat)
        start(flat_guess_copy, along)
        arrive(flat_guess_copy, along)
        solve_correct(e1.at[0], lambda z: v1[z])
        arrive(lambda n: jump_copy(jo, n)(0), beside)
        jump.wait_recv()
        b = bb.at[1]

        def put_first(z, value):
            bb[1, z] = value + jj[0, z]
            xout[z - 4] = value

        solve_finish(bb.at[0], put_first)
        start(layer_copy(1), along)
        ends.wait_recv()
        for z in range(4):
            res[z] = fx[z] + xout[z]

        arrive(layer_copy(1), along)
        solve_smooth(b)
        start(smooth_copy, beside)
        solve_restrict(b, put_guess(1))
        start(guess_copy, far)
        shape = (4, 2, 8, 128)
        i = lax.broadcasted_iota(jnp.int32, shape, 0)
        sub = lax.broadcasted_iota(jnp.int32, shape, 2)
        given = ((sub == 1) | (sub == 6)) & ((i == 1) | (i == 2))
        arrive(smooth_copy, beside)
        arrive(guess_copy)
        solve_correct(e1.at[1], lambda z: jnp.where(given, vr[z], v1[z]))
        last_jump.wait_recv()

        def put_second(z, value):
            bb[2, z] = value + jj[1, z]

        solve_finish(b, put_second)

        b = bb.at[2]
        start(layer_copy(2), along)
        cross(0).start()
        arrive(layer_copy(2), along)
        sent(smooth_copy, beside)
        solve_smooth(b)
        solve_restrict(b, put_guess(2))
        start(last_guess_copy, far)
        last_guess_copy(8).start()
        cross(1).start()
        cross(2).start()

    @pl.when(tm == 3)
    def _():
        for z in range(4):
            value = fe[z] - own[z]
            jo[z + 4] = value
            to_own_rows(jj.at[1], z + 4, value)
        start(lambda n: jump_copy(jo, n)(1), beside)
        weights()
        arrive(lambda n: jump_copy(jo, n)(1), beside)
        last_jump.start()
        b = bb.at[2]
        cross(0).wait_recv()
        for z in range(4):
            res[z] = b[z + 4] + own[z]
        third.start()
        cross(1).wait_recv()
        cross(2).wait_recv()
        solve_smooth(b)
        arrive(last_guess_copy)
        last_guess_copy(8).wait_recv()
        solve_correct(e1.at[2], lambda z: v1[z])
        ends.wait_recv()
        third.wait_send()

        def put_last(z, value):
            res[z - 4] = fx[z - 4] + value

        solve_finish(b, put_last)

    def give(z, _):
        for p in range(2):
            for i in range(4):
                dealt[z, p, pl.ds(i, 4, stride=4), :] = res[z, i, p, 2:6, :]
        low_part, high_part = join_columns(dealt[z, 0], dealt[z, 1])
        o_ref[z, :, 0:128] = low_part
        o_ref[z, :, 128:256] = high_part
        return 0

    lax.fori_loop(0, 4, give, 0)

    sent(state_copy)
    swap.wait_send()
    sent(step_copy)

    @pl.when(is_lead)
    def _():
        sent(coeff_copy)
        for n in range(8):
            _, _, there = at(-DIRS[n][0], -DIRS[n][1])
            pl.when(there)(lambda n=n: coeff_pass(n).wait_send())

    @pl.when(tm == 0)
    def _():
        sent(lambda n: jump_copy(jo, n)(0), beside)
        jump.wait_send()
        ends.wait_send()

    @pl.when(tm == 2)
    def _():
        window.wait_send()
        ends.wait_send()

    @pl.when(tm == 1)
    def _():
        sent(more_copy, range(len(more)), more_dirs)
        sent(first_copy)
        ends_first.wait_send()
        sent(flat_guess_copy, along)
        sent(layer_copy(1), along)
        sent(guess_copy)
        sent(layer_copy(2), along)
        sent(last_guess_copy)
        last_guess_copy(8).wait_send()
        for n in range(3):
            cross(n).wait_send()

    @pl.when(tm == 3)
    def _():
        sent(lambda n: jump_copy(jo, n)(1), beside)
        last_jump.wait_send()


def per_device(states, diffusivity, velocity):
    def vmem(*shape):
        return pltpu.VMEM(shape + (8, 128), jnp.float32)

    dma = pltpu.SemaphoreType.DMA
    block = pl.BlockSpec(memory_space=pl.ANY)
    raw = (states[0], diffusivity, velocity)
    counts = (9, 8, 8, 12, 8, 24, 25, 8, 3, 5)
    out = pl.pallas_call(
        kernel,
        name="parareal",
        out_shape=jax.ShapeDtypeStruct(diffusivity.shape, jnp.float32),
        in_specs=[block] * 3,
        out_specs=pl.BlockSpec(memory_space=pltpu.VMEM),
        scratch_shapes=[pltpu.VMEM(array.shape, jnp.float32) for array in raw]
        + [
            vmem(4, 4, 2),
            vmem(4, 12, 4, 2),
            vmem(4, 12, 4, 2),
            vmem(12, 4, 2),
            vmem(12, 4, 2),
            vmem(12, 4, 2),
            vmem(12, 4, 2),
            vmem(12, 4, 2),
            vmem(4, 4, 2),
            vmem(12, 4, 2),
            vmem(2, 12, 4, 2),
            vmem(3, 12, 4, 2),
            vmem(12, 4, 2),
            vmem(12, 4, 2),
            vmem(12, 4, 2),
            vmem(3, 6, 2),
            vmem(4, 6, 2),
            vmem(6, 2),
            vmem(4, 4, 2),
            vmem(4, 4, 2),
            vmem(4, 4, 2),
            vmem(4, 4, 2),
            pltpu.VMEM((4, 2, 16, 128), jnp.float32),
            dma((3,)),
        ]
        + [dma((n,)) for n in counts for _ in range(2)],
        compiler_params=pltpu.CompilerParams(
            collective_id=0, has_side_effects=True, vmem_limit_bytes=56 * 1024 * 1024
        ),
    )(*raw)
    return out[None]


def solution(mesh):
    return jax.shard_map(
        per_device,
        mesh=mesh,
        in_specs=(
            P("tm", "slab", "coarse", None),
            P("slab", "coarse", None),
            P(None, "slab", "coarse", None),
        ),
        out_specs=P("tm", "slab", "coarse", None),
        check_vma=False,
    )
```

```python
import jax
import jax.numpy as jnp
from jax import lax
from jax.experimental import pallas as pl
from jax.experimental.pallas import tpu as pltpu
from jax.sharding import PartitionSpec as P

MESH = pl.DeviceIdType.MESH
SECTIONS = 4
RELAX = 0.8


def chebyshev_coefficients(sections):
    damping = 0.05
    centre_point = 1.0 + damping / (sections * sections)
    chebyshev = [1.0, centre_point]
    slopes = [0.0, 1.0]
    for degree in range(2, sections + 1):
        chebyshev.append(2.0 * centre_point * chebyshev[degree - 1] - chebyshev[degree - 2])
        slopes.append(
            2.0 * chebyshev[degree - 1]
            + 2.0 * centre_point * slopes[degree - 1]
            - slopes[degree - 2]
        )
    slope_ratio = chebyshev[sections] / slopes[sections]
    weights = [1.0 / entry for entry in chebyshev]
    scales = [0.0, 0.0]
    carries = [0.0, 0.0]
    tildes = [0.0, slope_ratio / centre_point]
    for degree in range(2, sections + 1):
        scales.append(2.0 * weights[degree] * centre_point / weights[degree - 1])
        carries.append(-weights[degree] / weights[degree - 2])
        tildes.append(2.0 * weights[degree] * slope_ratio / weights[degree - 1])
    return (scales, carries, tildes)


DIRS = ((1, 0), (-1, 0), (0, 1), (0, -1), (1, 1), (1, -1), (-1, 1), (-1, -1))


def cuts(step, low, count, wide):
    if step == 0:
        return pl.ds(low, count), pl.ds(low, count)
    if step == 1:
        return pl.ds(low + count - wide, wide), pl.ds(low - wide, wide)
    return pl.ds(low, wide), pl.ds(low + count, wide)


def fine_box(d, deep, rows, corner, blocks=1):
    dz, dr = d
    hz, hr = corner if dz and dr else (deep, rows)
    z_src, z_dst = cuts(dz, 4, 4, hz)
    every = pl.ds(0, 2)
    if dr == 0:
        box = (pl.ds(0, 4), every, pl.ds(2, 4))
        return (z_src, *box), (z_dst, *box)
    rows_at = pl.ds(4 - hr, hr) if dr == 1 else pl.ds(0, hr)
    s_src, s_dst = (6 - blocks, 2 - blocks) if dr == 1 else (2, 6)
    return (
        (z_src, rows_at, every, pl.ds(s_src, blocks)),
        (z_dst, rows_at, every, pl.ds(s_dst, blocks)),
    )


def coarse_box(d, blocks):
    dz, dr = d
    z_src, z_dst = cuts(dz, 2, 2, 2)
    every = pl.ds(0, 2)
    if dr == 0:
        return (z_src, every, pl.ds(2, 4)), (z_dst, every, pl.ds(2, 4))
    blocks = 1 if dz else blocks
    s_src, s_dst = (6 - blocks, 2 - blocks) if dr == 1 else (2, 6)
    return (z_src, every, pl.ds(s_src, blocks)), (z_dst, every, pl.ds(s_dst, blocks))


def lanes(shape):
    return lax.broadcasted_iota(jnp.int32, shape, len(shape) - 1)


def around(centre, fine):
    axis = centre.ndim - 2
    row_after = jnp.concatenate([centre[1:], pltpu.roll(centre[:1], 7, axis)], 0)
    row_before = jnp.concatenate([pltpu.roll(centre[-1:], 1, axis), centre[:-1]], 0)
    if fine:
        even, odd = centre[:, 0], centre[:, 1]
    else:
        even, odd = centre, centre
    at = lanes(even.shape)
    last = even.ndim - 1
    shifted_up = jnp.where(at == 127, 0.0, pltpu.roll(even, 127, last))
    shifted_down = jnp.where(at == 0, 0.0, pltpu.roll(odd, 1, last))
    if not fine:
        return row_after, row_before, shifted_up, shifted_down
    return (
        row_after,
        row_before,
        jnp.stack([odd, shifted_up], 1),
        jnp.stack([shifted_down, even], 1),
    )


def operator(field, coeffs, z, fine=True):
    centre, after, before = field[z], field[z + 1], field[z - 1]
    ra, rb, ca, cb = around(centre, fine)
    spread = coeffs[0, z] * (after + before + ra + rb + ca + cb - 6.0 * centre)
    drift = coeffs[1, z] * (after - before) + coeffs[2, z] * (ra - rb) + coeffs[3, z] * (ca - cb)
    return centre, spread, drift


def spread_out(value):
    wide = jnp.concatenate([value[:1], value[:1], value[1:], value[1:]], 0)
    return jnp.stack([wide, wide], 1)


def gathered(value, index):
    return jnp.take_along_axis(value, index, axis=1, mode="promise_in_bounds")


def split_columns(rows):
    low, high = rows[:, :128], rows[:, 128:]
    at = lanes(low.shape)
    source = (2 * at) % 128
    first = at < 64
    even = jnp.where(first, gathered(low, source), gathered(high, source))
    odd = jnp.where(first, gathered(low, source + 1), gathered(high, source + 1))
    return even, odd


def join_columns(even, odd):
    at = lanes(even.shape)
    half = at // 2
    is_even = at % 2 == 0
    low = jnp.where(is_even, gathered(even, half), gathered(odd, half))
    high = jnp.where(is_even, gathered(even, half + 64), gathered(odd, half + 64))
    return low, high


def kernel(
    s_hbm, d_hbm, v_hbm, o_ref,
    s_ref, d_ref, v_ref,
    own, co, cw, sa, sb, ta, ua, weight, fe, jo, jj, bb, v1, v2, vr, e1, cco, cweight,
    fx, sx, xout, res, dealt,
    in_sem, s_send, s_recv, c_send, c_recv, w_send, w_recv, g_send, g_recv,
    f_send, f_recv, b_send, b_recv, e_send, e_recv, r_send, r_recv, x_send, x_recv,
    m_send, m_recv,
):
    tm, slab, coarse = (lax.axis_index(a) for a in ("tm", "slab", "coarse"))
    slabs, coarses = lax.axis_size("slab"), lax.axis_size("coarse")
    loads = [
        pltpu.make_async_copy(src, dst, in_sem.at[n])
        for n, (src, dst) in enumerate(((s_hbm, s_ref), (d_hbm, d_ref), (v_hbm, v_ref)))
    ]
    for load in loads:
        load.start()

    def at(dz, dr):
        z, r = slab + dz, coarse + dr
        return z, r, (z >= 0) & (z < slabs) & (r >= 0) & (r < coarses)

    core = lax.rem(tm, 2)
    is_lead = core == 1
    sibling = tm + 1 - 2 * core
    across = lax.rem(tm + 2, 4)
    here = (slab, coarse)

    barrier = pltpu.get_barrier_semaphore()
    count = jnp.int32(2)
    for dz, dr in DIRS:
        z, r, there = at(dz, dr)

        @pl.when(there)
        def _():
            for t in (tm, sibling):
                pl.semaphore_signal(barrier, inc=1, device_id=(t, z, r), device_id_type=MESH)

        count = count + 2 * there.astype(jnp.int32)
    for t in (across, sibling):
        pl.semaphore_signal(barrier, inc=1, device_id=(t, *here), device_id_type=MESH)

    def arrange(z, _):
        for source, target, scale in (
            (s_ref.at[z], own.at[z], None),
            (d_ref.at[z], co.at[0, z + 4], None),
            (v_ref.at[0, z], co.at[1, z + 4], 0.5),
            (v_ref.at[1, z], co.at[2, z + 4], 0.5),
            (v_ref.at[2, z], co.at[3, z + 4], 0.5),
        ):
            for p, part in enumerate(split_columns(source[...])):
                dealt[z, p] = part if scale is None else scale * part
                for i in range(4):
                    target[i, p, 2:6, :] = dealt[z, p, pl.ds(i, 4, stride=4), :]
        return 0

    for load in loads:
        load.wait()
    lax.fori_loop(0, 4, arrange, 0)
    pl.semaphore_wait(barrier, count)

    def copy(src, dst, send, recv, device):
        return pltpu.make_async_remote_copy(
            src_ref=src, dst_ref=dst, send_sem=send, recv_sem=recv, device_id=device, device_id_type=MESH
        )

    def own_box(z):
        return (pl.ds(z, 4), pl.ds(0, 4), pl.ds(0, 2), pl.ds(2, 4))

    every = pl.ds(0, 4)
    both = pl.ds(0, 2)

    def state_copy(n):
        z, r, _ = at(*DIRS[n])
        (zs, *src), dst = fine_box(DIRS[n], 4, 4, (3, 3))
        src = (pl.ds(zs.start - 4, zs.size), *src)
        return copy(own.at[src], sa.at[dst], s_send.at[n], s_recv.at[n], (sibling, z, r))

    swap = copy(
        own.at[own_box(0)], sa.at[own_box(4)], s_send.at[8], s_recv.at[8], (sibling, *here)
    )

    def coeff_copy(n):
        z, r, _ = at(*DIRS[n])
        src, dst = fine_box(DIRS[n], 3, 3, (2, 2))
        return copy(
            co.at[(every, *src)], co.at[(every, *dst)], c_send.at[n], c_recv.at[n], (tm, z, r)
        )

    def coeff_pass(n):
        box = (every, *fine_box(DIRS[n], 3, 3, (2, 2))[1])
        return copy(co.at[box], co.at[box], w_send.at[n], w_recv.at[n], (sibling, *here))

    more = []
    for n, (dz, dr) in enumerate(DIRS):
        if dr == 0:
            continue
        z_src, z_dst = cuts(dz, 4, 4, 1 if dz else 4)
        near, away = ((5, 1), (4, 0)) if dr == 1 else ((2, 6), (3, 7))
        more.append((n, (z_src, every, both, pl.ds(away[0], 1)), (z_dst, every, both, pl.ds(away[1], 1))))
        if dz:
            part = pl.ds(0, 2) if dr == 1 else pl.ds(2, 2)
            more.append((n, (z_src, part, both, pl.ds(near[0], 1)), (z_dst, part, both, pl.ds(near[1], 1))))
        else:
            part = pl.ds(0, 1) if dr == 1 else pl.ds(3, 1)
            more.append((n, (z_src, part, both, pl.ds(near[0], 1)), (z_dst, part, both, pl.ds(near[1], 1))))
    more_dirs = [DIRS[n] for n, _, _ in more]

    def more_copy(q):
        n, src, dst = more[q]
        z, r, _ = at(*DIRS[n])
        return copy(
            co.at[(every, *src)], cw.at[(every, *dst)], g_send.at[q], g_recv.at[q], (tm, z, r)
        )

    def step_copy(n):
        z, r, _ = at(*DIRS[n])
        src, dst = fine_box(DIRS[n], 4, 4, (3, 3))
        return copy(sb.at[src], sb.at[dst], f_send.at[n], f_recv.at[n], (tm, z, r))

    def first_copy(n):
        z, r, _ = at(*DIRS[n])
        src, dst = fine_box(DIRS[n], 2, 4, (2, 4), blocks=2)
        return copy(bb.at[(0, *src)], bb.at[(0, *dst)], b_send.at[n], b_recv.at[n], (tm, z, r))

    def layer_copy(k):
        def make(n):
            z, r, _ = at(*DIRS[n])
            z_src, z_dst = cuts(DIRS[n][0], 4, 4, 2)
            box = (every, both, pl.ds(1, 6))
            sem = 8 * k + n
            return copy(
                bb.at[(k, z_src, *box)], bb.at[(k, z_dst, *box)], b_send.at[sem], b_recv.at[sem],
                (tm, z, r),
            )

        return make

    def flat_guess_copy(n):
        z, r, _ = at(*DIRS[n])
        z_src, z_dst = cuts(DIRS[n][0], 2, 2, 2)
        return copy(e1.at[0, z_src], e1.at[0, z_dst], e_send.at[n], e_recv.at[n], (tm, z, r))

    def guess_copy(n):
        z, r, _ = at(*DIRS[n])
        src, dst = coarse_box(DIRS[n], 2)
        return copy(
            e1.at[(1, *src)], e1.at[(1, *dst)], e_send.at[8 + n], e_recv.at[8 + n], (tm, z, r)
        )

    def last_guess_copy(n):
        if n == 8:
            box = (2, pl.ds(2, 2), both, pl.ds(2, 4))
            return copy(e1.at[box], e1.at[box], e_send.at[24], e_recv.at[24], (across, *here))
        z, r, _ = at(*DIRS[n])
        src, dst = coarse_box(DIRS[n], 1)
        return copy(
            e1.at[(2, *src)], e1.at[(2, *dst)], e_send.at[16 + n], e_recv.at[16 + n], (across, z, r)
        )

    def smooth_copy(n):
        z, r, _ = at(*DIRS[n])
        s_src, s_dst = (5, 1) if DIRS[n][1] == 1 else (2, 6)
        box = (pl.ds(3, 6), pl.ds(1, 2), both)
        return copy(
            v1.at[(*box, pl.ds(s_src, 1))], vr.at[(*box, pl.ds(s_dst, 1))],
            r_send.at[n], r_recv.at[n], (tm, z, r),
        )

    def jump_copy(field, n):
        z, r, _ = at(*DIRS[n])
        src, dst = fine_box(DIRS[n], 4, 2, (1, 1))
        return lambda target: copy(
            field.at[src], jj.at[(target, *dst)], r_send.at[n - 2], r_recv.at[n - 2 + 4 * target],
            ((sibling, z, r) if target == 0 else (tm, z, r)),
        )

    def start(make, order=range(8), dirs=DIRS):
        for n in order:
            _, _, there = at(*dirs[n])
            pl.when(there)(lambda n=n: make(n).start())

    def arrive(make, order=range(8), dirs=DIRS):
        for n in order:
            _, _, there = at(-dirs[n][0], -dirs[n][1])
            pl.when(there)(lambda n=n: make(n).wait_recv())

    def sent(make, order=range(8), dirs=DIRS):
        for n in order:
            _, _, there = at(*dirs[n])
            pl.when(there)(lambda n=n: make(n).wait_send())

    far = (4, 5, 6, 7, 2, 3, 0, 1)
    heavy = (0, 1, 4, 5, 6, 7, 2, 3)
    along = (0, 1)
    beside = (2, 3)
    pl.when(is_lead)(lambda: start(coeff_copy, heavy))
    start(state_copy, heavy)
    swap.start()

    window = copy(own, sx, m_send.at[0], m_recv.at[0], (across, *here))
    pl.when(tm == 2)(window.start)

    def zero(n):
        return jnp.zeros((4, 2, n, 128), jnp.float32)

    def loop(low, high, body, unroll=True):
        def wrapped(z, _):
            body(z)
            return 0

        lax.fori_loop(low, high, wrapped, 0, unroll=unroll)

    for edge, begin, begin_coarse in ((slab == 0, 0, 0), (slab == slabs - 1, 8, 4)):

        @pl.when(edge)
        def _():
            def clear(z):
                for m in range(4):
                    co[m, z] = zero(8)
                    cw[m, z] = zero(8)
                for field in (sa, sb, bb.at[0], bb.at[1], bb.at[2]):
                    field[z] = zero(8)

            loop(begin, begin + 4, clear)
            for k in range(3):
                for z in range(begin_coarse, begin_coarse + 2):
                    e1[k, z] = jnp.zeros((2, 8, 128), jnp.float32)

    for edge, begin in ((coarse == 0, 0), (coarse == coarses - 1, 6)):

        @pl.when(edge)
        def _():
            s = pl.ds(begin, 2)

            def clear(z):
                for m in range(4):
                    co[m, z, :, :, s, :] = zero(2)
                    cw[m, z, :, :, s, :] = zero(2)
                for field in (sa, sb, bb.at[0], vr):
                    field[z, :, :, s, :] = zero(2)

            loop(0, 12, clear)
            for k in range(2):

                @pl.when(tm == 1 + 2 * k)
                def _():
                    for z in range(4, 8):
                        jj[k, z, :, :, s, :] = zero(2)

            for k in (1, 2):
                for z in range(6):
                    e1[k, z, :, s, :] = jnp.zeros((2, 2, 128), jnp.float32)

    arrive(state_copy)
    swap.wait_recv()
    pl.when(is_lead)(lambda: arrive(coeff_copy))
    pl.when(jnp.logical_not(is_lead))(lambda: arrive(coeff_pass))

    scales, carries, tildes = chebyshev_coefficients(SECTIONS)

    def fine_step(begin, finish):
        def first(z):
            centre, spread, drift = operator(begin, co, z)
            ta[z] = centre + tildes[1] * (spread - drift)

        def later(degree, current, before, put):
            def body(z):
                centre, spread, drift = operator(current, co, z)
                put(
                    z,
                    scales[degree] * centre
                    + carries[degree] * before[z]
                    + tildes[degree] * (spread - drift),
                )

            return body

        def put_to(ref):
            def put(z, value):
                ref[z] = value

            return put

        loop(1, 11, first)
        loop(2, 10, later(2, ta, begin, put_to(ua)))
        loop(3, 9, later(3, ua, ta, put_to(ta)))
        loop(4, 8, later(4, ta, ua, finish))

    def to_own_rows(target, z, value):
        target[z, :, :, 2:6, :] = value[:, :, 2:6, :]

    def to_fe(z, value):
        fe[z - 4] = value

    fine_step(sa, lambda z, value: to_own_rows(sb, z, value))
    start(step_copy, far)

    @pl.when(is_lead)
    def _():
        for n in range(8):
            _, _, there = at(-DIRS[n][0], -DIRS[n][1])
            pl.when(there)(lambda n=n: coeff_pass(n).start())

    pl.when(tm == 1)(lambda: start(more_copy, range(len(more)), more_dirs))

    arrive(step_copy)
    fine_step(sb, to_fe)

    def weigh(z):
        weight[z] = RELAX / (1.0 + 12.0 * co[0, z])

    def halves(value):
        value = value[:, 0] + value[:, 1]
        return 0.125 * jnp.concatenate([value[0:1] + value[1:2], value[2:3] + value[3:4]], 0)

    def coarse_weigh(q):
        for m in range(4):
            mean = halves(co[m, 2 * q] + co[m, 2 * q + 1])
            cco[m, q] = mean
            if m == 0:
                cweight[q] = RELAX / (1.0 + 3.0 * mean)

    def merge(low, high, first, last):
        def body(z):
            for m in range(4):
                for part, sub in ((every, 0), (every, 7), (first, 1), (last, 6)):
                    at_rows = (m, z, part, slice(None), pl.ds(sub, 1), slice(None))
                    co[at_rows] = cw[at_rows]

        for z in range(low, high):
            body(z)

    def weights():
        loop(3, 9, weigh)
        loop(1, 5, coarse_weigh)

    ends = copy(fe, fx, m_send.at[1], m_recv.at[1], (sibling, *here))
    ends_first = copy(fe, res, m_send.at[1], m_recv.at[1], (sibling, *here))
    jump = copy(
        jo.at[own_box(4)], jj.at[(0, *own_box(4))], m_send.at[2], m_recv.at[2], (sibling, *here)
    )
    jump_box = (1, pl.ds(4, 4), every, both, pl.ds(1, 6))
    last_jump = copy(jj.at[jump_box], jj.at[jump_box], m_send.at[4], m_recv.at[4], (across, *here))
    third = copy(res, res, m_send.at[3], m_recv.at[3], (sibling, *here))
    cross_boxes = [(2, pl.ds(low, n), every, both, pl.ds(1, 6)) for low, n in ((4, 4), (2, 2), (8, 2))]

    def cross(n):
        box = cross_boxes[n]
        return copy(bb.at[box], bb.at[box], x_send.at[n], x_recv.at[n], (across, *here))

    @pl.when(tm == 0)
    def _():
        window.wait_recv()
        for z in range(4):
            jo[z + 4] = fe[z] - sx[z]
        start(lambda n: jump_copy(jo, n)(0), beside)
        jump.start()
        ends.start()
        ends_first.wait_recv()

    @pl.when(tm == 2)
    def _():
        ends.start()
        third.wait_recv()

    def solve_smooth(b):
        def smooth(z):
            centre, spread, drift = operator(b, co, z)
            v1[z] = centre + (2.0 * weight[z]) * (spread - drift)

        loop(3, 9, smooth)

    def solve_restrict(b, put):
        def restrict(q):
            total = None
            for z in (2 * q, 2 * q + 1):
                centre, spread, drift = operator(v1, co, z)
                misfit = b[z] - centre + 2.0 * (spread - drift)
                total = misfit if total is None else total + misfit
            put(q, cweight[q] * halves(total))

        loop(2, 4, restrict)

    def solve_correct(e, base):
        def correct(q):
            centre, spread, drift = operator(e, cco, q, fine=False)
            w = cweight[q]
            wide = spread_out((2.0 - w) * centre + w * (0.5 * spread - drift))
            for z in (2 * q, 2 * q + 1):
                v2[z] = base(z) + wide

        loop(1, 5, correct)

    def solve_finish(b, put):
        def finish(z):
            centre, spread, drift = operator(v2, co, z)
            put(z, centre + weight[z] * (b[z] - centre + 2.0 * (spread - drift)))

        loop(4, 8, finish)

    def put_guess(k):
        def put(q, value):
            e1[k, q, :, 2:6, :] = value[:, 2:6, :]

        return put

    @pl.when(tm == 1)
    def _():
        b = bb.at[0]
        for z in range(4):
            b[z + 4, :, :, 2:6, :] = (fe[z] - own[z])[:, :, 2:6, :]
        start(first_copy, far)
        ends_first.start()
        arrive(more_copy, range(len(more)), more_dirs)
        merge(4, 8, pl.ds(0, 1), pl.ds(3, 1))
        for z in (3, 8):
            merge(z, z + 1, pl.ds(0, 2), pl.ds(2, 2))
        weights()
        arrive(first_copy)
        solve_smooth(b)

        def put_flat(q, value):
            e1[0, q] = value

        solve_restrict(b, put_flat)
        start(flat_guess_copy, along)
        arrive(flat_guess_copy, along)
        solve_correct(e1.at[0], lambda z: v1[z])
        arrive(lambda n: jump_copy(jo, n)(0), beside)
        jump.wait_recv()
        b = bb.at[1]

        def put_first(z, value):
            bb[1, z] = value + jj[0, z]
            xout[z - 4] = value

        solve_finish(bb.at[0], put_first)
        start(layer_copy(1), along)
        ends.wait_recv()
        for z in range(4):
            res[z] = fx[z] + xout[z]

        arrive(layer_copy(1), along)
        solve_smooth(b)
        start(smooth_copy, beside)
        solve_restrict(b, put_guess(1))
        start(guess_copy, far)
        shape = (4, 2, 8, 128)
        i = lax.broadcasted_iota(jnp.int32, shape, 0)
        sub = lax.broadcasted_iota(jnp.int32, shape, 2)
        given = ((sub == 1) | (sub == 6)) & ((i == 1) | (i == 2))
        arrive(smooth_copy, beside)
        arrive(guess_copy)
        solve_correct(e1.at[1], lambda z: jnp.where(given, vr[z], v1[z]))
        last_jump.wait_recv()

        def put_second(z, value):
            bb[2, z] = value + jj[1, z]

        solve_finish(b, put_second)

        b = bb.at[2]
        start(layer_copy(2), along)
        cross(0).start()
        arrive(layer_copy(2), along)
        sent(smooth_copy, beside)
        solve_smooth(b)
        solve_restrict(b, put_guess(2))
        start(last_guess_copy, far)
        last_guess_copy(8).start()
        cross(1).start()
        cross(2).start()

    @pl.when(tm == 3)
    def _():
        for z in range(4):
            value = fe[z] - own[z]
            jo[z + 4] = value
            to_own_rows(jj.at[1], z + 4, value)
        start(lambda n: jump_copy(jo, n)(1), beside)
        weights()
        arrive(lambda n: jump_copy(jo, n)(1), beside)
        last_jump.start()
        b = bb.at[2]
        cross(0).wait_recv()
        for z in range(4):
            res[z] = b[z + 4] + own[z]
        third.start()
        cross(1).wait_recv()
        cross(2).wait_recv()
        solve_smooth(b)
        arrive(last_guess_copy)
        last_guess_copy(8).wait_recv()
        solve_correct(e1.at[2], lambda z: v1[z])
        ends.wait_recv()
        third.wait_send()

        def put_last(z, value):
            res[z - 4] = fx[z - 4] + value

        solve_finish(b, put_last)

    def give(z, _):
        for p in range(2):
            for i in range(4):
                dealt[z, p, pl.ds(i, 4, stride=4), :] = res[z, i, p, 2:6, :]
        low_part, high_part = join_columns(dealt[z, 0], dealt[z, 1])
        o_ref[z, :, 0:128] = low_part
        o_ref[z, :, 128:256] = high_part
        return 0

    lax.fori_loop(0, 4, give, 0)

    sent(state_copy)
    swap.wait_send()
    sent(step_copy)

    @pl.when(is_lead)
    def _():
        sent(coeff_copy)
        for n in range(8):
            _, _, there = at(-DIRS[n][0], -DIRS[n][1])
            pl.when(there)(lambda n=n: coeff_pass(n).wait_send())

    @pl.when(tm == 0)
    def _():
        sent(lambda n: jump_copy(jo, n)(0), beside)
        jump.wait_send()
        ends.wait_send()

    @pl.when(tm == 2)
    def _():
        window.wait_send()
        ends.wait_send()

    @pl.when(tm == 1)
    def _():
        sent(more_copy, range(len(more)), more_dirs)
        sent(first_copy)
        ends_first.wait_send()
        sent(flat_guess_copy, along)
        sent(layer_copy(1), along)
        sent(guess_copy)
        sent(layer_copy(2), along)
        sent(last_guess_copy)
        last_guess_copy(8).wait_send()
        for n in range(3):
            cross(n).wait_send()

    @pl.when(tm == 3)
    def _():
        sent(lambda n: jump_copy(jo, n)(1), beside)
        last_jump.wait_send()


def per_device(states, diffusivity, velocity):
    def vmem(*shape):
        return pltpu.VMEM(shape + (8, 128), jnp.float32)

    dma = pltpu.SemaphoreType.DMA
    block = pl.BlockSpec(memory_space=pl.ANY)
    raw = (states[0], diffusivity, velocity)
    counts = (9, 8, 8, 12, 8, 24, 25, 8, 3, 5)
    out = pl.pallas_call(
        kernel,
        name="parareal",
        out_shape=jax.ShapeDtypeStruct(diffusivity.shape, jnp.float32),
        in_specs=[block] * 3,
        out_specs=pl.BlockSpec(memory_space=pltpu.VMEM),
        scratch_shapes=[pltpu.VMEM(array.shape, jnp.float32) for array in raw]
        + [
            vmem(4, 4, 2),
            vmem(4, 12, 4, 2),
            vmem(4, 12, 4, 2),
            vmem(12, 4, 2),
            vmem(12, 4, 2),
            vmem(12, 4, 2),
            vmem(12, 4, 2),
            vmem(12, 4, 2),
            vmem(4, 4, 2),
            vmem(12, 4, 2),
            vmem(2, 12, 4, 2),
            vmem(3, 12, 4, 2),
            vmem(12, 4, 2),
            vmem(12, 4, 2),
            vmem(12, 4, 2),
            vmem(3, 6, 2),
            vmem(4, 6, 2),
            vmem(6, 2),
            vmem(4, 4, 2),
            vmem(4, 4, 2),
            vmem(4, 4, 2),
            vmem(4, 4, 2),
            pltpu.VMEM((4, 2, 16, 128), jnp.float32),
            dma((3,)),
        ]
        + [dma((n,)) for n in counts for _ in range(2)],
        compiler_params=pltpu.CompilerParams(
            collective_id=0, has_side_effects=True, vmem_limit_bytes=56 * 1024 * 1024
        ),
    )(*raw)
    return out[None]


def solution(mesh):
    return jax.shard_map(
        per_device,
        mesh=mesh,
        in_specs=(
            P("tm", "slab", "coarse", None),
            P("slab", "coarse", None),
            P(None, "slab", "coarse", None),
        ),
        out_specs=P("tm", "slab", "coarse", None),
        check_vma=False,
    )
```

```python
import jax
import jax.numpy as jnp
from jax import lax
from jax.experimental import pallas as pl
from jax.experimental.pallas import tpu as pltpu
from jax.sharding import PartitionSpec as P

MESH = pl.DeviceIdType.MESH
SECTIONS = 4
RELAX = 0.8


def chebyshev_coefficients(sections):
    damping = 0.05
    centre_point = 1.0 + damping / (sections * sections)
    chebyshev = [1.0, centre_point]
    slopes = [0.0, 1.0]
    for degree in range(2, sections + 1):
        chebyshev.append(2.0 * centre_point * chebyshev[degree - 1] - chebyshev[degree - 2])
        slopes.append(
            2.0 * chebyshev[degree - 1]
            + 2.0 * centre_point * slopes[degree - 1]
            - slopes[degree - 2]
        )
    slope_ratio = chebyshev[sections] / slopes[sections]
    weights = [1.0 / entry for entry in chebyshev]
    scales = [0.0, 0.0]
    carries = [0.0, 0.0]
    tildes = [0.0, slope_ratio / centre_point]
    for degree in range(2, sections + 1):
        scales.append(2.0 * weights[degree] * centre_point / weights[degree - 1])
        carries.append(-weights[degree] / weights[degree - 2])
        tildes.append(2.0 * weights[degree] * slope_ratio / weights[degree - 1])
    return (scales, carries, tildes)


DIRS = ((1, 0), (-1, 0), (0, 1), (0, -1), (1, 1), (1, -1), (-1, 1), (-1, -1))


def cuts(step, low, count, wide):
    if step == 0:
        return pl.ds(low, count), pl.ds(low, count)
    if step == 1:
        return pl.ds(low + count - wide, wide), pl.ds(low - wide, wide)
    return pl.ds(low, wide), pl.ds(low + count, wide)


def fine_box(d, deep, rows, corner, blocks=1):
    dz, dr = d
    hz, hr = corner if dz and dr else (deep, rows)
    z_src, z_dst = cuts(dz, 4, 4, hz)
    every = pl.ds(0, 2)
    if dr == 0:
        box = (pl.ds(0, 4), every, pl.ds(2, 4))
        return (z_src, *box), (z_dst, *box)
    rows_at = pl.ds(4 - hr, hr) if dr == 1 else pl.ds(0, hr)
    s_src, s_dst = (6 - blocks, 2 - blocks) if dr == 1 else (2, 6)
    return (
        (z_src, rows_at, every, pl.ds(s_src, blocks)),
        (z_dst, rows_at, every, pl.ds(s_dst, blocks)),
    )


def coarse_box(d, blocks):
    dz, dr = d
    z_src, z_dst = cuts(dz, 2, 2, 2)
    every = pl.ds(0, 2)
    if dr == 0:
        return (z_src, every, pl.ds(2, 4)), (z_dst, every, pl.ds(2, 4))
    blocks = 1 if dz else blocks
    s_src, s_dst = (6 - blocks, 2 - blocks) if dr == 1 else (2, 6)
    return (z_src, every, pl.ds(s_src, blocks)), (z_dst, every, pl.ds(s_dst, blocks))


def lanes(shape):
    return lax.broadcasted_iota(jnp.int32, shape, len(shape) - 1)


def around(centre, fine):
    axis = centre.ndim - 2
    row_after = jnp.concatenate([centre[1:], pltpu.roll(centre[:1], 7, axis)], 0)
    row_before = jnp.concatenate([pltpu.roll(centre[-1:], 1, axis), centre[:-1]], 0)
    if fine:
        even, odd = centre[:, 0], centre[:, 1]
    else:
        even, odd = centre, centre
    at = lanes(even.shape)
    last = even.ndim - 1
    shifted_up = jnp.where(at == 127, 0.0, pltpu.roll(even, 127, last))
    shifted_down = jnp.where(at == 0, 0.0, pltpu.roll(odd, 1, last))
    if not fine:
        return row_after, row_before, shifted_up, shifted_down
    return (
        row_after,
        row_before,
        jnp.stack([odd, shifted_up], 1),
        jnp.stack([shifted_down, even], 1),
    )


def operator(field, coeffs, z, fine=True):
    centre, after, before = field[z], field[z + 1], field[z - 1]
    ra, rb, ca, cb = around(centre, fine)
    spread = coeffs[0, z] * (after + before + ra + rb + ca + cb - 6.0 * centre)
    drift = coeffs[1, z] * (after - before) + coeffs[2, z] * (ra - rb) + coeffs[3, z] * (ca - cb)
    return centre, spread, drift


def spread_out(value):
    wide = jnp.concatenate([value[:1], value[:1], value[1:], value[1:]], 0)
    return jnp.stack([wide, wide], 1)


def gathered(value, index):
    return jnp.take_along_axis(value, index, axis=1, mode="promise_in_bounds")


def split_columns(rows):
    low, high = rows[:, :128], rows[:, 128:]
    at = lanes(low.shape)
    source = (2 * at) % 128
    first = at < 64
    even = jnp.where(first, gathered(low, source), gathered(high, source))
    odd = jnp.where(first, gathered(low, source + 1), gathered(high, source + 1))
    return even, odd


def join_columns(even, odd):
    at = lanes(even.shape)
    half = at // 2
    is_even = at % 2 == 0
    low = jnp.where(is_even, gathered(even, half), gathered(odd, half))
    high = jnp.where(is_even, gathered(even, half + 64), gathered(odd, half + 64))
    return low, high


def kernel(
    s_hbm, d_hbm, v_hbm, o_ref,
    s_ref, d_ref, v_ref,
    own, co, cw, sa, sb, ta, ua, weight, fe, jo, jj, bb, v1, v2, vr, e1, cco, cweight,
    fx, sx, xout, res, dealt,
    in_sem, s_send, s_recv, c_send, c_recv, w_send, w_recv, g_send, g_recv,
    f_send, f_recv, b_send, b_recv, e_send, e_recv, r_send, r_recv, x_send, x_recv,
    m_send, m_recv,
):
    tm, slab, coarse = (lax.axis_index(a) for a in ("tm", "slab", "coarse"))
    slabs, coarses = lax.axis_size("slab"), lax.axis_size("coarse")
    loads = [
        pltpu.make_async_copy(src, dst, in_sem.at[n])
        for n, (src, dst) in enumerate(((s_hbm, s_ref), (d_hbm, d_ref), (v_hbm, v_ref)))
    ]
    for load in loads:
        load.start()

    def at(dz, dr):
        z, r = slab + dz, coarse + dr
        return z, r, (z >= 0) & (z < slabs) & (r >= 0) & (r < coarses)

    core = lax.rem(tm, 2)
    is_lead = core == 1
    sibling = tm + 1 - 2 * core
    across = lax.rem(tm + 2, 4)
    here = (slab, coarse)

    barrier = pltpu.get_barrier_semaphore()
    count = jnp.int32(2)
    for dz, dr in DIRS:
        z, r, there = at(dz, dr)

        @pl.when(there)
        def _():
            for t in (tm, sibling):
                pl.semaphore_signal(barrier, inc=1, device_id=(t, z, r), device_id_type=MESH)

        count = count + 2 * there.astype(jnp.int32)
    for t in (across, sibling):
        pl.semaphore_signal(barrier, inc=1, device_id=(t, *here), device_id_type=MESH)

    def arrange(m):
        if m < 3:
            loads[m].wait()
        for z in range(4):
            source = (s_ref, d_ref, v_ref.at[0], v_ref.at[1], v_ref.at[2])[m]
            target = own.at[z] if m == 0 else co.at[m - 1, z + 4]
            for p, part in enumerate(split_columns(source[z])):
                dealt[m, z, p] = 0.5 * part if m > 1 else part
                for i in range(4):
                    target[i, p, 2:6, :] = dealt[m, z, p, pl.ds(i, 4, stride=4), :]

    def arrange_coeffs():
        for m in range(1, 5):
            arrange(m)

    pl.when(is_lead)(arrange_coeffs)
    pl.when(jnp.logical_not(is_lead))(lambda: arrange(0))
    pl.semaphore_wait(barrier, count)

    def copy(src, dst, send, recv, device):
        return pltpu.make_async_remote_copy(
            src_ref=src, dst_ref=dst, send_sem=send, recv_sem=recv, device_id=device, device_id_type=MESH
        )

    def own_box(z):
        return (pl.ds(z, 4), pl.ds(0, 4), pl.ds(0, 2), pl.ds(2, 4))

    every = pl.ds(0, 4)
    both = pl.ds(0, 2)

    def state_copy(n):
        z, r, _ = at(*DIRS[n])
        (zs, *src), dst = fine_box(DIRS[n], 4, 4, (3, 3))
        src = (pl.ds(zs.start - 4, zs.size), *src)
        return copy(own.at[src], sa.at[dst], s_send.at[n], s_recv.at[n], (sibling, z, r))

    swap = copy(
        own.at[own_box(0)], sa.at[own_box(4)], s_send.at[8], s_recv.at[8], (sibling, *here)
    )

    def coeff_copy(n):
        z, r, _ = at(*DIRS[n])
        src, dst = fine_box(DIRS[n], 3, 3, (2, 2))
        return copy(
            co.at[(every, *src)], co.at[(every, *dst)], c_send.at[n], c_recv.at[n], (tm, z, r)
        )

    def coeff_pass(n):
        box = (every, *fine_box(DIRS[n], 3, 3, (2, 2))[1])
        return copy(co.at[box], co.at[box], w_send.at[n], w_recv.at[n], (sibling, *here))

    more = []
    for n, (dz, dr) in enumerate(DIRS):
        if dr == 0:
            continue
        z_src, z_dst = cuts(dz, 4, 4, 1 if dz else 4)
        near, away = ((5, 1), (4, 0)) if dr == 1 else ((2, 6), (3, 7))
        more.append((n, (z_src, every, both, pl.ds(away[0], 1)), (z_dst, every, both, pl.ds(away[1], 1))))
        if dz:
            part = pl.ds(0, 2) if dr == 1 else pl.ds(2, 2)
            more.append((n, (z_src, part, both, pl.ds(near[0], 1)), (z_dst, part, both, pl.ds(near[1], 1))))
        else:
            part = pl.ds(0, 1) if dr == 1 else pl.ds(3, 1)
            more.append((n, (z_src, part, both, pl.ds(near[0], 1)), (z_dst, part, both, pl.ds(near[1], 1))))
    more_dirs = [DIRS[n] for n, _, _ in more]

    def more_copy(q):
        n, src, dst = more[q]
        z, r, _ = at(*DIRS[n])
        return copy(
            co.at[(every, *src)], cw.at[(every, *dst)], g_send.at[q], g_recv.at[q], (tm, z, r)
        )

    def step_copy(n):
        z, r, _ = at(*DIRS[n])
        src, dst = fine_box(DIRS[n], 4, 4, (3, 3))
        return copy(sb.at[src], sb.at[dst], f_send.at[n], f_recv.at[n], (tm, z, r))

    def first_copy(n):
        z, r, _ = at(*DIRS[n])
        src, dst = fine_box(DIRS[n], 2, 4, (2, 4), blocks=2)
        return copy(bb.at[(0, *src)], bb.at[(0, *dst)], b_send.at[n], b_recv.at[n], (tm, z, r))

    def layer_copy(k):
        def make(n):
            z, r, _ = at(*DIRS[n])
            z_src, z_dst = cuts(DIRS[n][0], 4, 4, 2)
            box = (every, both, pl.ds(1, 6))
            sem = 8 * k + n
            return copy(
                bb.at[(k, z_src, *box)], bb.at[(k, z_dst, *box)], b_send.at[sem], b_recv.at[sem],
                (tm, z, r),
            )

        return make

    def flat_guess_copy(n):
        z, r, _ = at(*DIRS[n])
        z_src, z_dst = cuts(DIRS[n][0], 2, 2, 2)
        return copy(e1.at[0, z_src], e1.at[0, z_dst], e_send.at[n], e_recv.at[n], (tm, z, r))

    def guess_copy(n):
        z, r, _ = at(*DIRS[n])
        src, dst = coarse_box(DIRS[n], 2)
        return copy(
            e1.at[(1, *src)], e1.at[(1, *dst)], e_send.at[8 + n], e_recv.at[8 + n], (tm, z, r)
        )

    def last_guess_copy(n):
        if n == 8:
            box = (2, pl.ds(2, 2), both, pl.ds(2, 4))
            return copy(e1.at[box], e1.at[box], e_send.at[24], e_recv.at[24], (across, *here))
        z, r, _ = at(*DIRS[n])
        src, dst = coarse_box(DIRS[n], 1)
        return copy(
            e1.at[(2, *src)], e1.at[(2, *dst)], e_send.at[16 + n], e_recv.at[16 + n], (across, z, r)
        )

    def smooth_copy(n):
        z, r, _ = at(*DIRS[n])
        s_src, s_dst = (5, 1) if DIRS[n][1] == 1 else (2, 6)
        box = (pl.ds(3, 6), pl.ds(1, 2), both)
        return copy(
            v1.at[(*box, pl.ds(s_src, 1))], vr.at[(*box, pl.ds(s_dst, 1))],
            r_send.at[n], r_recv.at[n], (tm, z, r),
        )

    def jump_copy(field, n):
        z, r, _ = at(*DIRS[n])
        src, dst = fine_box(DIRS[n], 4, 2, (1, 1))
        return lambda target: copy(
            field.at[src], jj.at[(target, *dst)], r_send.at[n - 2], r_recv.at[n - 2 + 4 * target],
            ((sibling, z, r) if target == 0 else (tm, z, r)),
        )

    def start(make, order=range(8), dirs=DIRS):
        for n in order:
            _, _, there = at(*dirs[n])
            pl.when(there)(lambda n=n: make(n).start())

    def arrive(make, order=range(8), dirs=DIRS):
        for n in order:
            _, _, there = at(-dirs[n][0], -dirs[n][1])
            pl.when(there)(lambda n=n: make(n).wait_recv())

    def sent(make, order=range(8), dirs=DIRS):
        for n in order:
            _, _, there = at(*dirs[n])
            pl.when(there)(lambda n=n: make(n).wait_send())

    far = (4, 5, 6, 7, 2, 3, 0, 1)
    heavy = (0, 1, 4, 5, 6, 7, 2, 3)
    along = (0, 1)
    beside = (2, 3)

    @pl.when(is_lead)
    def _():
        start(coeff_copy, heavy)
        arrange(0)

    start(state_copy, heavy)
    swap.start()
    pl.when(jnp.logical_not(is_lead))(arrange_coeffs)

    window = copy(own, sx, m_send.at[0], m_recv.at[0], (across, *here))
    pl.when(tm == 2)(window.start)

    def zero(n):
        return jnp.zeros((4, 2, n, 128), jnp.float32)

    def loop(low, high, body, unroll=True):
        def wrapped(z, _):
            body(z)
            return 0

        lax.fori_loop(low, high, wrapped, 0, unroll=unroll)

    for edge, begin, begin_coarse in ((slab == 0, 0, 0), (slab == slabs - 1, 8, 4)):

        @pl.when(edge)
        def _():
            def clear(z):
                for m in range(4):
                    co[m, z] = zero(8)
                    cw[m, z] = zero(8)
                for field in (sa, sb, bb.at[0], bb.at[1], bb.at[2]):
                    field[z] = zero(8)

            loop(begin, begin + 4, clear)
            for k in range(3):
                for z in range(begin_coarse, begin_coarse + 2):
                    e1[k, z] = jnp.zeros((2, 8, 128), jnp.float32)

    for edge, begin in ((coarse == 0, 0), (coarse == coarses - 1, 6)):

        @pl.when(edge)
        def _():
            s = pl.ds(begin, 2)

            def clear(z):
                for m in range(4):
                    co[m, z, :, :, s, :] = zero(2)
                    cw[m, z, :, :, s, :] = zero(2)
                for field in (sa, sb, bb.at[0], vr):
                    field[z, :, :, s, :] = zero(2)

            loop(0, 12, clear)
            for k in range(2):

                @pl.when(tm == 1 + 2 * k)
                def _():
                    for z in range(4, 8):
                        jj[k, z, :, :, s, :] = zero(2)

            for k in (1, 2):
                for z in range(6):
                    e1[k, z, :, s, :] = jnp.zeros((2, 2, 128), jnp.float32)

    arrive(state_copy)
    swap.wait_recv()
    pl.when(is_lead)(lambda: arrive(coeff_copy))
    pl.when(jnp.logical_not(is_lead))(lambda: arrive(coeff_pass))

    scales, carries, tildes = chebyshev_coefficients(SECTIONS)

    def fine_step(begin, finish):
        def first(z):
            centre, spread, drift = operator(begin, co, z)
            ta[z] = centre + tildes[1] * (spread - drift)

        def later(degree, current, before, put):
            def body(z):
                centre, spread, drift = operator(current, co, z)
                put(
                    z,
                    scales[degree] * centre
                    + carries[degree] * before[z]
                    + tildes[degree] * (spread - drift),
                )

            return body

        def put_to(ref):
            def put(z, value):
                ref[z] = value

            return put

        loop(1, 11, first)
        loop(2, 10, later(2, ta, begin, put_to(ua)))
        loop(3, 9, later(3, ua, ta, put_to(ta)))
        loop(4, 8, later(4, ta, ua, finish))

    def to_own_rows(target, z, value):
        target[z, :, :, 2:6, :] = value[:, :, 2:6, :]

    def to_fe(z, value):
        fe[z - 4] = value

    fine_step(sa, lambda z, value: to_own_rows(sb, z, value))
    start(step_copy, far)

    @pl.when(is_lead)
    def _():
        for n in range(8):
            _, _, there = at(-DIRS[n][0], -DIRS[n][1])
            pl.when(there)(lambda n=n: coeff_pass(n).start())

    pl.when(tm == 1)(lambda: start(more_copy, range(len(more)), more_dirs))

    arrive(step_copy)
    fine_step(sb, to_fe)

    def weigh(z):
        weight[z] = RELAX / (1.0 + 12.0 * co[0, z])

    def halves(value):
        value = value[:, 0] + value[:, 1]
        return 0.125 * jnp.concatenate([value[0:1] + value[1:2], value[2:3] + value[3:4]], 0)

    def coarse_weigh(q):
        for m in range(4):
            mean = halves(co[m, 2 * q] + co[m, 2 * q + 1])
            cco[m, q] = mean
            if m == 0:
                cweight[q] = RELAX / (1.0 + 3.0 * mean)

    def merge(low, high, first, last):
        def body(z):
            for m in range(4):
                for part, sub in ((every, 0), (every, 7), (first, 1), (last, 6)):
                    at_rows = (m, z, part, slice(None), pl.ds(sub, 1), slice(None))
                    co[at_rows] = cw[at_rows]

        for z in range(low, high):
            body(z)

    def weights():
        loop(3, 9, weigh)
        loop(1, 5, coarse_weigh)

    ends = copy(fe, fx, m_send.at[1], m_recv.at[1], (sibling, *here))
    ends_first = copy(fe, res, m_send.at[1], m_recv.at[1], (sibling, *here))
    jump = copy(
        jo.at[own_box(4)], jj.at[(0, *own_box(4))], m_send.at[2], m_recv.at[2], (sibling, *here)
    )
    jump_box = (1, pl.ds(4, 4), every, both, pl.ds(1, 6))
    last_jump = copy(jj.at[jump_box], jj.at[jump_box], m_send.at[4], m_recv.at[4], (across, *here))
    third = copy(res, res, m_send.at[3], m_recv.at[3], (sibling, *here))
    cross_boxes = [(2, pl.ds(low, n), every, both, pl.ds(1, 6)) for low, n in ((4, 4), (2, 2), (8, 2))]

    def cross(n):
        box = cross_boxes[n]
        return copy(bb.at[box], bb.at[box], x_send.at[n], x_recv.at[n], (across, *here))

    @pl.when(tm == 0)
    def _():
        window.wait_recv()
        for z in range(4):
            jo[z + 4] = fe[z] - sx[z]
        start(lambda n: jump_copy(jo, n)(0), beside)
        jump.start()
        ends.start()
        ends_first.wait_recv()

    @pl.when(tm == 2)
    def _():
        ends.start()
        third.wait_recv()

    def solve_smooth(b):
        def smooth(z):
            centre, spread, drift = operator(b, co, z)
            v1[z] = centre + (2.0 * weight[z]) * (spread - drift)

        loop(3, 9, smooth)

    def solve_restrict(b, put):
        def restrict(q):
            total = None
            for z in (2 * q, 2 * q + 1):
                centre, spread, drift = operator(v1, co, z)
                misfit = b[z] - centre + 2.0 * (spread - drift)
                total = misfit if total is None else total + misfit
            put(q, cweight[q] * halves(total))

        loop(2, 4, restrict)

    def solve_correct(e, base):
        def correct(q):
            centre, spread, drift = operator(e, cco, q, fine=False)
            w = cweight[q]
            wide = spread_out((2.0 - w) * centre + w * (0.5 * spread - drift))
            for z in (2 * q, 2 * q + 1):
                v2[z] = base(z) + wide

        loop(1, 5, correct)

    def solve_finish(b, put):
        def finish(z):
            centre, spread, drift = operator(v2, co, z)
            put(z, centre + weight[z] * (b[z] - centre + 2.0 * (spread - drift)))

        loop(4, 8, finish)

    def put_guess(k):
        def put(q, value):
            e1[k, q, :, 2:6, :] = value[:, 2:6, :]

        return put

    @pl.when(tm == 1)
    def _():
        b = bb.at[0]
        for z in range(4):
            b[z + 4, :, :, 2:6, :] = (fe[z] - own[z])[:, :, 2:6, :]
        start(first_copy, far)
        ends_first.start()
        arrive(more_copy, range(len(more)), more_dirs)
        merge(4, 8, pl.ds(0, 1), pl.ds(3, 1))
        for z in (3, 8):
            merge(z, z + 1, pl.ds(0, 2), pl.ds(2, 2))
        weights()
        arrive(first_copy)
        solve_smooth(b)

        def put_flat(q, value):
            e1[0, q] = value

        solve_restrict(b, put_flat)
        start(flat_guess_copy, along)
        arrive(flat_guess_copy, along)
        solve_correct(e1.at[0], lambda z: v1[z])
        arrive(lambda n: jump_copy(jo, n)(0), beside)
        jump.wait_recv()
        b = bb.at[1]

        def put_first(z, value):
            bb[1, z] = value + jj[0, z]
            xout[z - 4] = value

        solve_finish(bb.at[0], put_first)
        start(layer_copy(1), along)
        ends.wait_recv()
        for z in range(4):
            res[z] = fx[z] + xout[z]

        arrive(layer_copy(1), along)
        solve_smooth(b)
        start(smooth_copy, beside)
        solve_restrict(b, put_guess(1))
        start(guess_copy, far)
        shape = (4, 2, 8, 128)
        i = lax.broadcasted_iota(jnp.int32, shape, 0)
        sub = lax.broadcasted_iota(jnp.int32, shape, 2)
        given = ((sub == 1) | (sub == 6)) & ((i == 1) | (i == 2))
        arrive(smooth_copy, beside)
        arrive(guess_copy)
        solve_correct(e1.at[1], lambda z: jnp.where(given, vr[z], v1[z]))
        last_jump.wait_recv()

        def put_second(z, value):
            bb[2, z] = value + jj[1, z]

        solve_finish(b, put_second)

        b = bb.at[2]
        start(layer_copy(2), along)
        cross(0).start()
        arrive(layer_copy(2), along)
        cross(1).start()
        cross(2).start()
        sent(smooth_copy, beside)
        solve_smooth(b)
        solve_restrict(b, put_guess(2))
        start(last_guess_copy, far)
        last_guess_copy(8).start()

    @pl.when(tm == 3)
    def _():
        for z in range(4):
            value = fe[z] - own[z]
            jo[z + 4] = value
            to_own_rows(jj.at[1], z + 4, value)
        start(lambda n: jump_copy(jo, n)(1), beside)
        weights()
        arrive(lambda n: jump_copy(jo, n)(1), beside)
        last_jump.start()
        b = bb.at[2]
        cross(0).wait_recv()
        for z in range(4):
            res[z] = b[z + 4] + own[z]
        third.start()
        cross(1).wait_recv()
        cross(2).wait_recv()
        solve_smooth(b)
        arrive(last_guess_copy)
        last_guess_copy(8).wait_recv()
        solve_correct(e1.at[2], lambda z: v1[z])
        ends.wait_recv()
        third.wait_send()

        def put_last(z, value):
            res[z - 4] = fx[z - 4] + value

        solve_finish(b, put_last)

    for z in range(4):
        for p in range(2):
            for i in range(4):
                dealt[0, z, p, pl.ds(i, 4, stride=4), :] = res[z, i, p, 2:6, :]
        low_part, high_part = join_columns(dealt[0, z, 0], dealt[0, z, 1])
        o_ref[z, :, 0:128] = low_part
        o_ref[z, :, 128:256] = high_part

    sent(state_copy)
    swap.wait_send()
    sent(step_copy)

    @pl.when(is_lead)
    def _():
        sent(coeff_copy)
        for n in range(8):
            _, _, there = at(-DIRS[n][0], -DIRS[n][1])
            pl.when(there)(lambda n=n: coeff_pass(n).wait_send())

    @pl.when(tm == 0)
    def _():
        sent(lambda n: jump_copy(jo, n)(0), beside)
        jump.wait_send()
        ends.wait_send()

    @pl.when(tm == 2)
    def _():
        window.wait_send()
        ends.wait_send()

    @pl.when(tm == 1)
    def _():
        sent(more_copy, range(len(more)), more_dirs)
        sent(first_copy)
        ends_first.wait_send()
        sent(flat_guess_copy, along)
        sent(layer_copy(1), along)
        sent(guess_copy)
        sent(layer_copy(2), along)
        sent(last_guess_copy)
        last_guess_copy(8).wait_send()
        for n in range(3):
            cross(n).wait_send()

    @pl.when(tm == 3)
    def _():
        sent(lambda n: jump_copy(jo, n)(1), beside)
        last_jump.wait_send()


def per_device(states, diffusivity, velocity):
    def vmem(*shape):
        return pltpu.VMEM(shape + (8, 128), jnp.float32)

    dma = pltpu.SemaphoreType.DMA
    block = pl.BlockSpec(memory_space=pltpu.HBM)
    raw = (states[0], diffusivity, velocity)
    counts = (9, 8, 8, 12, 8, 24, 25, 8, 3, 5)
    out = pl.pallas_call(
        kernel,
        name="parareal",
        out_shape=jax.ShapeDtypeStruct(diffusivity.shape, jnp.float32),
        in_specs=[block] * 3,
        out_specs=pl.BlockSpec(memory_space=pltpu.VMEM),
        scratch_shapes=[pltpu.VMEM(array.shape, jnp.float32) for array in raw]
        + [
            vmem(4, 4, 2),
            vmem(4, 12, 4, 2),
            vmem(4, 12, 4, 2),
            vmem(12, 4, 2),
            vmem(12, 4, 2),
            vmem(12, 4, 2),
            vmem(12, 4, 2),
            vmem(12, 4, 2),
            vmem(4, 4, 2),
            vmem(12, 4, 2),
            vmem(2, 12, 4, 2),
            vmem(3, 12, 4, 2),
            vmem(12, 4, 2),
            vmem(12, 4, 2),
            vmem(12, 4, 2),
            vmem(3, 6, 2),
            vmem(4, 6, 2),
            vmem(6, 2),
            vmem(4, 4, 2),
            vmem(4, 4, 2),
            vmem(4, 4, 2),
            vmem(4, 4, 2),
            pltpu.VMEM((5, 4, 2, 16, 128), jnp.float32),
            dma((3,)),
        ]
        + [dma((n,)) for n in counts for _ in range(2)],
        compiler_params=pltpu.CompilerParams(
            collective_id=0, has_side_effects=True, vmem_limit_bytes=55168 * 1024
        ),
    )(*raw)
    return out[None]


def solution(mesh):
    return jax.shard_map(
        per_device,
        mesh=mesh,
        in_specs=(
            P("tm", "slab", "coarse", None),
            P("slab", "coarse", None),
            P(None, "slab", "coarse", None),
        ),
        out_specs=P("tm", "slab", "coarse", None),
        check_vma=False,
    )
```

```python
import jax
import jax.numpy as jnp
from jax import lax
from jax.experimental import pallas as pl
from jax.experimental.pallas import tpu as pltpu
from jax.sharding import PartitionSpec as P

MESH = pl.DeviceIdType.MESH
SECTIONS = 4
RELAX = 0.8


def chebyshev_coefficients(sections):
    damping = 0.05
    centre_point = 1.0 + damping / (sections * sections)
    chebyshev = [1.0, centre_point]
    slopes = [0.0, 1.0]
    for degree in range(2, sections + 1):
        chebyshev.append(2.0 * centre_point * chebyshev[degree - 1] - chebyshev[degree - 2])
        slopes.append(
            2.0 * chebyshev[degree - 1]
            + 2.0 * centre_point * slopes[degree - 1]
            - slopes[degree - 2]
        )
    slope_ratio = chebyshev[sections] / slopes[sections]
    weights = [1.0 / entry for entry in chebyshev]
    scales = [0.0, 0.0]
    carries = [0.0, 0.0]
    tildes = [0.0, slope_ratio / centre_point]
    for degree in range(2, sections + 1):
        scales.append(2.0 * weights[degree] * centre_point / weights[degree - 1])
        carries.append(-weights[degree] / weights[degree - 2])
        tildes.append(2.0 * weights[degree] * slope_ratio / weights[degree - 1])
    return (scales, carries, tildes)


TWO = ((2, 0), (-2, 0))
DIRS = ((1, 0), (-1, 0), (0, 1), (0, -1), (1, 1), (1, -1), (-1, 1), (-1, -1))


def cuts(step, low, count, wide):
    if step == 0:
        return pl.ds(low, count), pl.ds(low, count)
    if step == 1:
        return pl.ds(low + count - wide, wide), pl.ds(low - wide, wide)
    return pl.ds(low, wide), pl.ds(low + count, wide)


def fine_box(d, deep, rows, corner, blocks=1):
    dz, dr = d
    hz, hr = corner if dz and dr else (deep, rows)
    z_src, z_dst = cuts(dz, 4, 4, hz)
    every = pl.ds(0, 2)
    if dr == 0:
        box = (pl.ds(0, 4), every, pl.ds(2, 4))
        return (z_src, *box), (z_dst, *box)
    rows_at = pl.ds(4 - hr, hr) if dr == 1 else pl.ds(0, hr)
    s_src, s_dst = (6 - blocks, 2 - blocks) if dr == 1 else (2, 6)
    return (
        (z_src, rows_at, every, pl.ds(s_src, blocks)),
        (z_dst, rows_at, every, pl.ds(s_dst, blocks)),
    )


def coarse_box(d, blocks):
    dz, dr = d
    z_src, z_dst = cuts(dz, 3, 2, 2)
    every = pl.ds(0, 2)
    if dr == 0:
        return (z_src, every, pl.ds(2, 4)), (z_dst, every, pl.ds(2, 4))
    blocks = 1 if dz else blocks
    s_src, s_dst = (6 - blocks, 2 - blocks) if dr == 1 else (2, 6)
    return (z_src, every, pl.ds(s_src, blocks)), (z_dst, every, pl.ds(s_dst, blocks))


def lanes(shape):
    return lax.broadcasted_iota(jnp.int32, shape, len(shape) - 1)


def around(centre, fine):
    axis = centre.ndim - 2
    row_after = jnp.concatenate([centre[1:], pltpu.roll(centre[:1], 7, axis)], 0)
    row_before = jnp.concatenate([pltpu.roll(centre[-1:], 1, axis), centre[:-1]], 0)
    if fine:
        even, odd = centre[:, 0], centre[:, 1]
    else:
        even, odd = centre, centre
    at = lanes(even.shape)
    last = even.ndim - 1
    shifted_up = jnp.where(at == 127, 0.0, pltpu.roll(even, 127, last))
    shifted_down = jnp.where(at == 0, 0.0, pltpu.roll(odd, 1, last))
    if not fine:
        return row_after, row_before, shifted_up, shifted_down
    return (
        row_after,
        row_before,
        jnp.stack([odd, shifted_up], 1),
        jnp.stack([shifted_down, even], 1),
    )


def operator(field, coeffs, z, fine=True):
    centre, after, before = field[z], field[z + 1], field[z - 1]
    ra, rb, ca, cb = around(centre, fine)
    spread = coeffs[0, z] * (after + before + ra + rb + ca + cb - 6.0 * centre)
    drift = coeffs[1, z] * (after - before) + coeffs[2, z] * (ra - rb) + coeffs[3, z] * (ca - cb)
    return centre, spread, drift


def spread_out(value):
    wide = jnp.concatenate([value[:1], value[:1], value[1:], value[1:]], 0)
    return jnp.stack([wide, wide], 1)


def gathered(value, index):
    return jnp.take_along_axis(value, index, axis=1, mode="promise_in_bounds")


def split_columns(rows):
    low, high = rows[:, :128], rows[:, 128:]
    at = lanes(low.shape)
    source = (2 * at) % 128
    first = at < 64
    even = jnp.where(first, gathered(low, source), gathered(high, source))
    odd = jnp.where(first, gathered(low, source + 1), gathered(high, source + 1))
    return even, odd


def join_columns(even, odd):
    at = lanes(even.shape)
    half = at // 2
    is_even = at % 2 == 0
    low = jnp.where(is_even, gathered(even, half), gathered(odd, half))
    high = jnp.where(is_even, gathered(even, half + 64), gathered(odd, half + 64))
    return low, high


def kernel(
    s_hbm, d_hbm, v_hbm, o_ref,
    s_ref, d_ref, v_ref,
    own, co, cw, sa, sb, ta, ua, weight, fe, jo, jj, bb, v1, v2, vr, e1, cco, cweight,
    fx, sx, xout, res, dealt,
    in_sem, s_send, s_recv, c_send, c_recv, w_send, w_recv, g_send, g_recv,
    f_send, f_recv, b_send, b_recv, e_send, e_recv, r_send, r_recv, x_send, x_recv,
    m_send, m_recv,
):
    tm, slab, coarse = (lax.axis_index(a) for a in ("tm", "slab", "coarse"))
    slabs, coarses = lax.axis_size("slab"), lax.axis_size("coarse")
    loads = [
        pltpu.make_async_copy(src, dst, in_sem.at[n])
        for n, (src, dst) in enumerate(((s_hbm, s_ref), (d_hbm, d_ref), (v_hbm, v_ref)))
    ]
    for load in loads:
        load.start()

    def at(dz, dr):
        z, r = slab + dz, coarse + dr
        return z, r, (z >= 0) & (z < slabs) & (r >= 0) & (r < coarses)

    core = lax.rem(tm, 2)
    is_lead = core == 1
    sibling = tm + 1 - 2 * core
    across = lax.rem(tm + 2, 4)
    here = (slab, coarse)

    barrier = pltpu.get_barrier_semaphore()
    count = jnp.int32(2)
    for dz, dr in DIRS:
        z, r, there = at(dz, dr)

        @pl.when(there)
        def _():
            for t in (tm, sibling):
                pl.semaphore_signal(barrier, inc=1, device_id=(t, z, r), device_id_type=MESH)

        count = count + 2 * there.astype(jnp.int32)
    for t in (across, sibling):
        pl.semaphore_signal(barrier, inc=1, device_id=(t, *here), device_id_type=MESH)

    def arrange(m):
        if m < 3:
            loads[m].wait()
        for z in range(4):
            source = (s_ref, d_ref, v_ref.at[0], v_ref.at[1], v_ref.at[2])[m]
            target = own.at[z] if m == 0 else co.at[m - 1, z + 4]
            for p, part in enumerate(split_columns(source[z])):
                dealt[m, z, p] = 0.5 * part if m > 1 else part
                for i in range(4):
                    target[i, p, 2:6, :] = dealt[m, z, p, pl.ds(i, 4, stride=4), :]

    def arrange_coeffs():
        for m in range(1, 5):
            arrange(m)

    pl.when(is_lead)(arrange_coeffs)
    pl.when(jnp.logical_not(is_lead))(lambda: arrange(0))
    pl.semaphore_wait(barrier, count)

    def copy(src, dst, send, recv, device):
        return pltpu.make_async_remote_copy(
            src_ref=src, dst_ref=dst, send_sem=send, recv_sem=recv, device_id=device, device_id_type=MESH
        )

    def own_box(z):
        return (pl.ds(z, 4), pl.ds(0, 4), pl.ds(0, 2), pl.ds(2, 4))

    every = pl.ds(0, 4)
    both = pl.ds(0, 2)

    def state_copy(n):
        z, r, _ = at(*DIRS[n])
        (zs, *src), dst = fine_box(DIRS[n], 4, 4, (3, 3))
        src = (pl.ds(zs.start - 4, zs.size), *src)
        return copy(own.at[src], sa.at[dst], s_send.at[n], s_recv.at[n], (sibling, z, r))

    swap = copy(
        own.at[own_box(0)], sa.at[own_box(4)], s_send.at[8], s_recv.at[8], (sibling, *here)
    )

    def coeff_copy(n):
        z, r, _ = at(*DIRS[n])
        src, dst = fine_box(DIRS[n], 3, 3, (2, 2))
        return copy(
            co.at[(every, *src)], co.at[(every, *dst)], c_send.at[n], c_recv.at[n], (tm, z, r)
        )

    def coeff_pass(n):
        box = (every, *fine_box(DIRS[n], 3, 3, (2, 2))[1])
        return copy(co.at[box], co.at[box], w_send.at[n], w_recv.at[n], (sibling, *here))

    more = []
    for n, (dz, dr) in enumerate(DIRS):
        if dr == 0:
            continue
        z_src, z_dst = cuts(dz, 4, 4, 1 if dz else 4)
        near, away = ((5, 1), (4, 0)) if dr == 1 else ((2, 6), (3, 7))
        more.append((n, (z_src, every, both, pl.ds(away[0], 1)), (z_dst, every, both, pl.ds(away[1], 1))))
        if dz:
            part = pl.ds(0, 2) if dr == 1 else pl.ds(2, 2)
            more.append((n, (z_src, part, both, pl.ds(near[0], 1)), (z_dst, part, both, pl.ds(near[1], 1))))
        else:
            part = pl.ds(0, 1) if dr == 1 else pl.ds(3, 1)
            more.append((n, (z_src, part, both, pl.ds(near[0], 1)), (z_dst, part, both, pl.ds(near[1], 1))))
    for n, z_src, z_dst in ((0, 4, 0), (1, 7, 11)):
        box = (every, both, pl.ds(2, 4))
        more.append((n, (pl.ds(z_src, 1), *box), (pl.ds(z_dst, 1), *box)))
    more_dirs = [DIRS[n] for n, _, _ in more]

    def more_copy(q):
        n, src, dst = more[q]
        z, r, _ = at(*DIRS[n])
        return copy(
            co.at[(every, *src)], cw.at[(every, *dst)], g_send.at[q], g_recv.at[q], (tm, z, r)
        )

    def step_copy(n):
        z, r, _ = at(*DIRS[n])
        src, dst = fine_box(DIRS[n], 4, 4, (3, 3))
        return copy(sb.at[src], sb.at[dst], f_send.at[n], f_recv.at[n], (tm, z, r))

    def first_copy(n):
        z, r, _ = at(*DIRS[n])
        src, dst = fine_box(DIRS[n], 2, 4, (2, 4), blocks=2)
        return copy(bb.at[(0, *src)], bb.at[(0, *dst)], b_send.at[n], b_recv.at[n], (tm, z, r))

    def flat_guess_copy(n):
        z, r, _ = at(*DIRS[n])
        z_src, z_dst = cuts(DIRS[n][0], 3, 2, 2)
        return copy(e1.at[0, z_src], e1.at[0, z_dst], e_send.at[n], e_recv.at[n], (tm, z, r))

    def far_guess_copy(k):
        def make(n):
            z, r, _ = at(*TWO[n])
            z_src, z_dst = ((4, 0), (3, 7))[n]
            box = (both, pl.ds(0, 8) if k == 0 else pl.ds(2, 4))
            sem = 2 + 2 * k + n
            return copy(
                e1.at[(k, pl.ds(z_src, 1), *box)], e1.at[(k, pl.ds(z_dst, 1), *box)],
                e_send.at[sem], e_recv.at[sem], (tm, z, r),
            )

        return make

    def smooth_layer_copy(k):
        def make(n):
            z, r, _ = at(*DIRS[n])
            box = (every, both, pl.ds(0, 8) if k == 0 else pl.ds(1, 6))
            sem = 4 + 2 * k + n
            return copy(
                v1.at[(pl.ds(5, 2), *box)], vr.at[(k, pl.ds((1, 9)[n], 2), *box)],
                r_send.at[sem], r_recv.at[sem], (tm, z, r),
            )

        return make

    def guess_copy(n):
        z, r, _ = at(*DIRS[n])
        src, dst = coarse_box(DIRS[n], 2)
        return copy(
            e1.at[(1, *src)], e1.at[(1, *dst)], e_send.at[8 + n], e_recv.at[8 + n], (tm, z, r)
        )

    def last_guess_copy(n):
        if n == 8:
            box = (2, pl.ds(3, 2), both, pl.ds(2, 4))
            return copy(e1.at[box], e1.at[box], e_send.at[24], e_recv.at[24], (across, *here))
        z, r, _ = at(*DIRS[n])
        src, dst = coarse_box(DIRS[n], 1)
        return copy(
            e1.at[(2, *src)], e1.at[(2, *dst)], e_send.at[16 + n], e_recv.at[16 + n], (across, z, r)
        )

    def smooth_copy(n):
        z, r, _ = at(*DIRS[n])
        s_src, s_dst = (5, 1) if DIRS[n][1] == 1 else (2, 6)
        box = (pl.ds(3, 6), pl.ds(1 if DIRS[n][1] == 1 else 0, 3), both)
        return copy(
            v1.at[(*box, pl.ds(s_src, 1))], vr.at[(1, *box, pl.ds(s_dst, 1))],
            r_send.at[n], r_recv.at[n], (tm, z, r),
        )

    def jump_copy(field, n):
        z, r, _ = at(*DIRS[n])
        src, dst = fine_box(DIRS[n], 2, 2, (1, 1))
        return lambda target: copy(
            field.at[src], jj.at[(target, *dst)], r_send.at[n + 8], r_recv.at[n + 8 + 8 * target],
            ((sibling, z, r) if target == 0 else (tm, z, r)),
        )

    def start(make, order=range(8), dirs=DIRS):
        for n in order:
            _, _, there = at(*dirs[n])
            pl.when(there)(lambda n=n: make(n).start())

    def arrive(make, order=range(8), dirs=DIRS):
        for n in order:
            _, _, there = at(-dirs[n][0], -dirs[n][1])
            pl.when(there)(lambda n=n: make(n).wait_recv())

    def sent(make, order=range(8), dirs=DIRS):
        for n in order:
            _, _, there = at(*dirs[n])
            pl.when(there)(lambda n=n: make(n).wait_send())

    far = (4, 5, 6, 7, 2, 3, 0, 1)
    heavy = (0, 1, 4, 5, 6, 7, 2, 3)
    along = (0, 1)
    beside = (2, 3)

    @pl.when(is_lead)
    def _():
        start(coeff_copy, heavy)
        arrange(0)

    start(state_copy, heavy)
    swap.start()
    pl.when(jnp.logical_not(is_lead))(arrange_coeffs)

    window = copy(own, sx, m_send.at[0], m_recv.at[0], (across, *here))
    pl.when(tm == 2)(window.start)

    def zero(n):
        return jnp.zeros((4, 2, n, 128), jnp.float32)

    def loop(low, high, body, unroll=True):
        def wrapped(z, _):
            body(z)
            return 0

        lax.fori_loop(low, high, wrapped, 0, unroll=unroll)

    for edge, begin, begin_coarse in ((slab == 0, 0, 0), (slab == slabs - 1, 8, 5)):

        @pl.when(edge)
        def _():
            def clear(z):
                for m in range(4):
                    co[m, z] = zero(8)
                    cw[m, z] = zero(8)
                for field in (sa, sb, bb.at[0], vr.at[0], vr.at[1]):
                    field[z] = zero(8)

            loop(begin, begin + 4, clear)
            for k in range(3):
                for z in range(begin_coarse, begin_coarse + 3):
                    e1[k, z] = jnp.zeros((2, 8, 128), jnp.float32)
            for k in range(2):

                @pl.when(tm == 1 + 2 * k)
                def _():
                    for z in (2, 3) if begin == 0 else (8, 9):
                        jj[k, z] = zero(8)

    for edge, z in ((slab == 1, 0), (slab == slabs - 2, 7)):

        @pl.when(edge)
        def _():
            for k in range(2):
                e1[k, z] = jnp.zeros((2, 8, 128), jnp.float32)

    for edge, begin in ((coarse == 0, 0), (coarse == coarses - 1, 6)):

        @pl.when(edge)
        def _():
            s = pl.ds(begin, 2)

            def clear(z):
                for m in range(4):
                    co[m, z, :, :, s, :] = zero(2)
                    cw[m, z, :, :, s, :] = zero(2)
                for field in (sa, sb, bb.at[0]):
                    field[z, :, :, s, :] = zero(2)

            loop(0, 12, clear)
            for z in range(3, 9):
                vr[1, z, :, :, s, :] = zero(2)
            for k in range(2):

                @pl.when(tm == 1 + 2 * k)
                def _():
                    for z in range(2, 10):
                        jj[k, z, :, :, s, :] = zero(2)

            for k in (1, 2):
                for z in range(8):
                    e1[k, z, :, s, :] = jnp.zeros((2, 2, 128), jnp.float32)

    arrive(state_copy)
    swap.wait_recv()
    pl.when(is_lead)(lambda: arrive(coeff_copy))
    pl.when(jnp.logical_not(is_lead))(lambda: arrive(coeff_pass))

    scales, carries, tildes = chebyshev_coefficients(SECTIONS)

    def fine_step(begin, finish):
        def first(z):
            centre, spread, drift = operator(begin, co, z)
            ta[z] = centre + tildes[1] * (spread - drift)

        def later(degree, current, before, put):
            def body(z):
                centre, spread, drift = operator(current, co, z)
                put(
                    z,
                    scales[degree] * centre
                    + carries[degree] * before[z]
                    + tildes[degree] * (spread - drift),
                )

            return body

        def put_to(ref):
            def put(z, value):
                ref[z] = value

            return put

        loop(1, 11, first)
        loop(2, 10, later(2, ta, begin, put_to(ua)))
        loop(3, 9, later(3, ua, ta, put_to(ta)))
        loop(4, 8, later(4, ta, ua, finish))

    def to_own_rows(target, z, value):
        target[z, :, :, 2:6, :] = value[:, :, 2:6, :]

    def to_fe(z, value):
        fe[z - 4] = value

    fine_step(sa, lambda z, value: to_own_rows(sb, z, value))
    start(step_copy, far)

    @pl.when(is_lead)
    def _():
        for n in range(8):
            _, _, there = at(-DIRS[n][0], -DIRS[n][1])
            pl.when(there)(lambda n=n: coeff_pass(n).start())

    pl.when(tm == 1)(lambda: start(more_copy, range(len(more)), more_dirs))

    arrive(step_copy)
    fine_step(sb, to_fe)

    def weigh(z):
        weight[z] = RELAX / (1.0 + 12.0 * co[0, z])

    def halves(value):
        value = value[:, 0] + value[:, 1]
        return 0.125 * jnp.concatenate([value[0:1] + value[1:2], value[2:3] + value[3:4]], 0)

    def coarse_weigh(q):
        for m in range(4):
            mean = halves(co[m, 2 * q - 2] + co[m, 2 * q - 1])
            cco[m, q] = mean
            if m == 0:
                cweight[q] = RELAX / (1.0 + 3.0 * mean)

    def merge(low, high, first, last):
        def body(z):
            for m in range(4):
                for part, sub in ((every, 0), (every, 7), (first, 1), (last, 6)):
                    at_rows = (m, z, part, slice(None), pl.ds(sub, 1), slice(None))
                    co[at_rows] = cw[at_rows]

        for z in range(low, high):
            body(z)

    def weights():
        loop(2, 10, weigh)
        loop(1, 7, coarse_weigh)

    ends = copy(fe, fx, m_send.at[1], m_recv.at[1], (sibling, *here))
    ends_first = copy(fe, res, m_send.at[1], m_recv.at[1], (sibling, *here))
    jump = copy(
        jo.at[own_box(4)], jj.at[(0, *own_box(4))], m_send.at[2], m_recv.at[2], (sibling, *here)
    )
    jump_box = (1, pl.ds(2, 8), every, both, pl.ds(1, 6))
    last_jump = copy(jj.at[jump_box], jj.at[jump_box], m_send.at[4], m_recv.at[4], (across, *here))
    third = copy(res, res, m_send.at[3], m_recv.at[3], (sibling, *here))
    cross_box = (2, pl.ds(2, 8), every, both, pl.ds(1, 6))
    cross = copy(
        bb.at[cross_box], bb.at[cross_box], x_send.at[0], x_recv.at[0], (across, *here)
    )

    @pl.when(tm == 0)
    def _():
        window.wait_recv()
        for z in range(4):
            jo[z + 4] = fe[z] - sx[z]
        start(lambda n: jump_copy(jo, n)(0), far)
        jump.start()
        ends.start()
        ends_first.wait_recv()

    @pl.when(tm == 2)
    def _():
        ends.start()
        third.wait_recv()

    def solve_smooth(b):
        def smooth(z):
            centre, spread, drift = operator(b, co, z)
            v1[z] = centre + (2.0 * weight[z]) * (spread - drift)

        loop(3, 9, smooth)

    def solve_restrict(b, put):
        def restrict(q):
            total = None
            for z in (2 * q - 2, 2 * q - 1):
                centre, spread, drift = operator(v1, co, z)
                misfit = b[z] - centre + 2.0 * (spread - drift)
                total = misfit if total is None else total + misfit
            put(q, cweight[q] * halves(total))

        loop(3, 5, restrict)

    def solve_correct(e, base, reach):
        for q in range(3 - reach, 5 + reach):
            centre, spread, drift = operator(e, cco, q, fine=False)
            w = cweight[q]
            wide = spread_out((2.0 - w) * centre + w * (0.5 * spread - drift))
            for z in (2 * q - 2, 2 * q - 1):
                if z >= 4 - 2 * reach + (reach - 1) and z < 8 + 2 * reach - (reach - 1):
                    v2[z] = base(z) + wide

    def solve_finish(b, put, reach):
        def finish(z):
            centre, spread, drift = operator(v2, co, z)
            put(z, centre + weight[z] * (b[z] - centre + 2.0 * (spread - drift)))

        loop(4 - reach, 8 + reach, finish)

    def put_guess(k):
        def put(q, value):
            e1[k, q, :, 2:6, :] = value[:, 2:6, :]

        return put

    @pl.when(tm == 1)
    def _():
        b = bb.at[0]
        for z in range(4):
            b[z + 4, :, :, 2:6, :] = (fe[z] - own[z])[:, :, 2:6, :]
        start(first_copy, far)
        ends_first.start()
        arrive(more_copy, range(len(more)), more_dirs)
        merge(4, 8, pl.ds(0, 1), pl.ds(3, 1))
        for z in (3, 8):
            merge(z, z + 1, pl.ds(0, 2), pl.ds(2, 2))
        for z in (0, 11):
            for m in range(4):
                co[m, z, :, :, 2:6, :] = cw[m, z, :, :, 2:6, :]
        weights()
        arrive(first_copy)
        solve_smooth(b)
        start(smooth_layer_copy(0), along)

        def put_flat(q, value):
            e1[0, q] = value

        solve_restrict(b, put_flat)
        start(far_guess_copy(0), along, TWO)
        start(flat_guess_copy, along)
        arrive(smooth_layer_copy(0), along)
        arrive(flat_guess_copy, along)
        arrive(far_guess_copy(0), along, TWO)
        solve_correct(e1.at[0], lambda z: v1[z] if 3 <= z < 9 else vr[0, z], 2)
        arrive(lambda n: jump_copy(jo, n)(0))
        jump.wait_recv()
        b = bb.at[1]

        def put_first(z, value):
            bb[1, z] = value + jj[0, z]

        solve_finish(bb.at[0], put_first, 2)

        sent(smooth_layer_copy(0), along)
        solve_smooth(b)
        start(smooth_copy, beside)
        start(smooth_layer_copy(1), along)
        solve_restrict(b, put_guess(1))
        start(guess_copy, (4, 5, 6, 7, 2, 3))
        start(far_guess_copy(1), along, TWO)
        start(guess_copy, along)
        ends.wait_recv()
        for z in range(4):
            res[z] = fx[z] + (b[z + 4] - jj[0, z + 4])
        shape = (4, 2, 8, 128)
        i = lax.broadcasted_iota(jnp.int32, shape, 0)
        sub = lax.broadcasted_iota(jnp.int32, shape, 2)
        given = ((sub == 1) & (i > 0)) | ((sub == 6) & (i < 3))
        arrive(smooth_copy, beside)
        arrive(smooth_layer_copy(1), along)
        arrive(guess_copy)
        arrive(far_guess_copy(1), along, TWO)
        solve_correct(
            e1.at[1],
            lambda z: jnp.where(given, vr[1, z], v1[z]) if 3 <= z < 9 else vr[1, z],
            2,
        )
        last_jump.wait_recv()

        def put_second(z, value):
            bb[2, z] = value + jj[1, z]

        solve_finish(b, put_second, 2)

        b = bb.at[2]
        cross.start()
        sent(smooth_copy, beside)
        sent(smooth_layer_copy(1), along)
        solve_smooth(b)
        solve_restrict(b, put_guess(2))
        start(last_guess_copy, far)
        last_guess_copy(8).start()

    @pl.when(tm == 3)
    def _():
        for z in range(4):
            value = fe[z] - own[z]
            jo[z + 4] = value
            to_own_rows(jj.at[1], z + 4, value)
        start(lambda n: jump_copy(jo, n)(1), far)
        weights()
        arrive(lambda n: jump_copy(jo, n)(1))
        last_jump.start()
        b = bb.at[2]
        cross.wait_recv()
        for z in range(4):
            res[z] = b[z + 4] + own[z]
        third.start()
        solve_smooth(b)
        arrive(last_guess_copy)
        last_guess_copy(8).wait_recv()
        solve_correct(e1.at[2], lambda z: v1[z], 1)
        ends.wait_recv()
        third.wait_send()

        def put_last(z, value):
            res[z - 4] = fx[z - 4] + value

        solve_finish(b, put_last, 0)

    for z in range(4):
        for p in range(2):
            for i in range(4):
                dealt[0, z, p, pl.ds(i, 4, stride=4), :] = res[z, i, p, 2:6, :]
        low_part, high_part = join_columns(dealt[0, z, 0], dealt[0, z, 1])
        o_ref[z, :, 0:128] = low_part
        o_ref[z, :, 128:256] = high_part

    sent(state_copy)
    swap.wait_send()
    sent(step_copy)

    @pl.when(is_lead)
    def _():
        sent(coeff_copy)
        for n in range(8):
            _, _, there = at(-DIRS[n][0], -DIRS[n][1])
            pl.when(there)(lambda n=n: coeff_pass(n).wait_send())

    @pl.when(tm == 0)
    def _():
        sent(lambda n: jump_copy(jo, n)(0))
        jump.wait_send()
        ends.wait_send()

    @pl.when(tm == 2)
    def _():
        window.wait_send()
        ends.wait_send()

    @pl.when(tm == 1)
    def _():
        sent(more_copy, range(len(more)), more_dirs)
        sent(first_copy)
        ends_first.wait_send()
        sent(flat_guess_copy, along)
        sent(far_guess_copy(0), along, TWO)
        sent(guess_copy)
        sent(far_guess_copy(1), along, TWO)
        sent(last_guess_copy)
        last_guess_copy(8).wait_send()
        cross.wait_send()

    @pl.when(tm == 3)
    def _():
        sent(lambda n: jump_copy(jo, n)(1))
        last_jump.wait_send()


def per_device(states, diffusivity, velocity):
    def vmem(*shape):
        return pltpu.VMEM(shape + (8, 128), jnp.float32)

    dma = pltpu.SemaphoreType.DMA
    block = pl.BlockSpec(memory_space=pltpu.HBM)
    raw = (states[0], diffusivity, velocity)
    counts = (9, 8, 8, 14, 8, 8, 25, 24, 1, 5)
    out = pl.pallas_call(
        kernel,
        name="parareal",
        out_shape=jax.ShapeDtypeStruct(diffusivity.shape, jnp.float32),
        in_specs=[block] * 3,
        out_specs=pl.BlockSpec(memory_space=pltpu.VMEM),
        scratch_shapes=[pltpu.VMEM(array.shape, jnp.float32) for array in raw]
        + [
            vmem(4, 4, 2),
            vmem(4, 12, 4, 2),
            vmem(4, 12, 4, 2),
            vmem(12, 4, 2),
            vmem(12, 4, 2),
            vmem(12, 4, 2),
            vmem(12, 4, 2),
            vmem(12, 4, 2),
            vmem(4, 4, 2),
            vmem(12, 4, 2),
            vmem(2, 12, 4, 2),
            vmem(3, 12, 4, 2),
            vmem(12, 4, 2),
            vmem(12, 4, 2),
            vmem(2, 12, 4, 2),
            vmem(3, 8, 2),
            vmem(4, 8, 2),
            vmem(8, 2),
            vmem(4, 4, 2),
            vmem(4, 4, 2),
            vmem(4, 4, 2),
            vmem(4, 4, 2),
            pltpu.VMEM((5, 4, 2, 16, 128), jnp.float32),
            dma((3,)),
        ]
        + [dma((n,)) for n in counts for _ in range(2)],
        compiler_params=pltpu.CompilerParams(
            collective_id=0, has_side_effects=True, vmem_limit_bytes=55168 * 1024
        ),
    )(*raw)
    return out[None]


def solution(mesh):
    return jax.shard_map(
        per_device,
        mesh=mesh,
        in_specs=(
            P("tm", "slab", "coarse", None),
            P("slab", "coarse", None),
            P(None, "slab", "coarse", None),
        ),
        out_specs=P("tm", "slab", "coarse", None),
        check_vma=False,
    )
```

```python
import jax
import jax.numpy as jnp
from jax import lax
from jax.experimental import pallas as pl
from jax.experimental.pallas import tpu as pltpu
from jax.sharding import PartitionSpec as P

MESH = pl.DeviceIdType.MESH
SECTIONS = 4
RELAX = 0.8


def chebyshev_coefficients(sections):
    damping = 0.05
    centre_point = 1.0 + damping / (sections * sections)
    chebyshev = [1.0, centre_point]
    slopes = [0.0, 1.0]
    for degree in range(2, sections + 1):
        chebyshev.append(2.0 * centre_point * chebyshev[degree - 1] - chebyshev[degree - 2])
        slopes.append(
            2.0 * chebyshev[degree - 1]
            + 2.0 * centre_point * slopes[degree - 1]
            - slopes[degree - 2]
        )
    slope_ratio = chebyshev[sections] / slopes[sections]
    weights = [1.0 / entry for entry in chebyshev]
    scales = [0.0, 0.0]
    carries = [0.0, 0.0]
    tildes = [0.0, slope_ratio / centre_point]
    for degree in range(2, sections + 1):
        scales.append(2.0 * weights[degree] * centre_point / weights[degree - 1])
        carries.append(-weights[degree] / weights[degree - 2])
        tildes.append(2.0 * weights[degree] * slope_ratio / weights[degree - 1])
    return (scales, carries, tildes)


TWO = ((2, 0), (-2, 0))
DIRS = ((1, 0), (-1, 0), (0, 1), (0, -1), (1, 1), (1, -1), (-1, 1), (-1, -1))


def cuts(step, low, count, wide):
    if step == 0:
        return pl.ds(low, count), pl.ds(low, count)
    if step == 1:
        return pl.ds(low + count - wide, wide), pl.ds(low - wide, wide)
    return pl.ds(low, wide), pl.ds(low + count, wide)


def fine_box(d, deep, rows, corner, blocks=1):
    dz, dr = d
    hz, hr = corner if dz and dr else (deep, rows)
    z_src, z_dst = cuts(dz, 4, 4, hz)
    every = pl.ds(0, 2)
    if dr == 0:
        box = (pl.ds(0, 4), every, pl.ds(2, 4))
        return (z_src, *box), (z_dst, *box)
    rows_at = pl.ds(4 - hr, hr) if dr == 1 else pl.ds(0, hr)
    s_src, s_dst = (6 - blocks, 2 - blocks) if dr == 1 else (2, 6)
    return (
        (z_src, rows_at, every, pl.ds(s_src, blocks)),
        (z_dst, rows_at, every, pl.ds(s_dst, blocks)),
    )


def coarse_box(d, blocks):
    dz, dr = d
    z_src, z_dst = cuts(dz, 3, 2, 2)
    every = pl.ds(0, 2)
    if dr == 0:
        return (z_src, every, pl.ds(2, 4)), (z_dst, every, pl.ds(2, 4))
    blocks = 1 if dz else blocks
    s_src, s_dst = (6 - blocks, 2 - blocks) if dr == 1 else (2, 6)
    return (z_src, every, pl.ds(s_src, blocks)), (z_dst, every, pl.ds(s_dst, blocks))


def lanes(shape):
    return lax.broadcasted_iota(jnp.int32, shape, len(shape) - 1)


def around(centre, fine):
    axis = centre.ndim - 2
    row_after = jnp.concatenate([centre[1:], pltpu.roll(centre[:1], 7, axis)], 0)
    row_before = jnp.concatenate([pltpu.roll(centre[-1:], 1, axis), centre[:-1]], 0)
    if fine:
        even, odd = centre[:, 0], centre[:, 1]
    else:
        even, odd = centre, centre
    at = lanes(even.shape)
    last = even.ndim - 1
    shifted_up = jnp.where(at == 127, 0.0, pltpu.roll(even, 127, last))
    shifted_down = jnp.where(at == 0, 0.0, pltpu.roll(odd, 1, last))
    if not fine:
        return row_after, row_before, shifted_up, shifted_down
    return (
        row_after,
        row_before,
        jnp.stack([odd, shifted_up], 1),
        jnp.stack([shifted_down, even], 1),
    )


def operator(field, coeffs, z, fine=True):
    centre, after, before = field[z], field[z + 1], field[z - 1]
    ra, rb, ca, cb = around(centre, fine)
    spread = coeffs[0, z] * (after + before + ra + rb + ca + cb - 6.0 * centre)
    drift = coeffs[1, z] * (after - before) + coeffs[2, z] * (ra - rb) + coeffs[3, z] * (ca - cb)
    return centre, spread, drift


def spread_out(value):
    wide = jnp.concatenate([value[:1], value[:1], value[1:], value[1:]], 0)
    return jnp.stack([wide, wide], 1)


def gathered(value, index):
    return jnp.take_along_axis(value, index, axis=1, mode="promise_in_bounds")


def split_columns(rows):
    low, high = rows[:, :128], rows[:, 128:]
    at = lanes(low.shape)
    source = (2 * at) % 128
    first = at < 64
    even = jnp.where(first, gathered(low, source), gathered(high, source))
    odd = jnp.where(first, gathered(low, source + 1), gathered(high, source + 1))
    return even, odd


def join_columns(even, odd):
    at = lanes(even.shape)
    half = at // 2
    is_even = at % 2 == 0
    low = jnp.where(is_even, gathered(even, half), gathered(odd, half))
    high = jnp.where(is_even, gathered(even, half + 64), gathered(odd, half + 64))
    return low, high


def kernel(
    s_hbm, d_hbm, v_hbm, o_ref,
    s_ref, d_ref, v_ref,
    own, co, cw, sa, sb, ta, ua, weight, fe, jo, jj, bb, v1, v2, vr, e1, cco, cweight,
    fx, sx, xout, res, dealt,
    in_sem, s_send, s_recv, c_send, c_recv, w_send, w_recv, g_send, g_recv,
    f_send, f_recv, b_send, b_recv, e_send, e_recv, r_send, r_recv, x_send, x_recv,
    m_send, m_recv,
):
    tm, slab, coarse = (lax.axis_index(a) for a in ("tm", "slab", "coarse"))
    slabs, coarses = lax.axis_size("slab"), lax.axis_size("coarse")
    loads = [
        pltpu.make_async_copy(src, dst, in_sem.at[n])
        for n, (src, dst) in enumerate(((s_hbm, s_ref), (d_hbm, d_ref), (v_hbm, v_ref)))
    ]
    for load in loads:
        load.start()

    def at(dz, dr):
        z, r = slab + dz, coarse + dr
        return z, r, (z >= 0) & (z < slabs) & (r >= 0) & (r < coarses)

    core = lax.rem(tm, 2)
    is_lead = core == 1
    sibling = tm + 1 - 2 * core
    across = lax.rem(tm + 2, 4)
    here = (slab, coarse)

    barrier = pltpu.get_barrier_semaphore()
    count = jnp.int32(2)
    for dz, dr in DIRS:
        z, r, there = at(dz, dr)

        @pl.when(there)
        def _():
            for t in (tm, sibling):
                pl.semaphore_signal(barrier, inc=1, device_id=(t, z, r), device_id_type=MESH)

        count = count + 2 * there.astype(jnp.int32)
    for t in (across, sibling):
        pl.semaphore_signal(barrier, inc=1, device_id=(t, *here), device_id_type=MESH)

    def arrange(m):
        if m < 3:
            loads[m].wait()
        for z in range(4):
            source = (s_ref, d_ref, v_ref.at[0], v_ref.at[1], v_ref.at[2])[m]
            target = own.at[z] if m == 0 else co.at[m - 1, z + 4]
            for p, part in enumerate(split_columns(source[z])):
                dealt[m, z, p] = 0.5 * part if m > 1 else part
                for i in range(4):
                    target[i, p, 2:6, :] = dealt[m, z, p, pl.ds(i, 4, stride=4), :]

    def arrange_coeffs():
        for m in range(1, 5):
            arrange(m)

    pl.when(is_lead)(arrange_coeffs)
    pl.when(jnp.logical_not(is_lead))(lambda: arrange(0))
    pl.semaphore_wait(barrier, count)

    def copy(src, dst, send, recv, device):
        return pltpu.make_async_remote_copy(
            src_ref=src, dst_ref=dst, send_sem=send, recv_sem=recv, device_id=device, device_id_type=MESH
        )

    def own_box(z):
        return (pl.ds(z, 4), pl.ds(0, 4), pl.ds(0, 2), pl.ds(2, 4))

    every = pl.ds(0, 4)
    both = pl.ds(0, 2)

    def state_copy(n):
        z, r, _ = at(*DIRS[n])
        (zs, *src), dst = fine_box(DIRS[n], 4, 4, (3, 3))
        src = (pl.ds(zs.start - 4, zs.size), *src)
        return copy(own.at[src], sa.at[dst], s_send.at[n], s_recv.at[n], (sibling, z, r))

    swap = copy(
        own.at[own_box(0)], sa.at[own_box(4)], s_send.at[8], s_recv.at[8], (sibling, *here)
    )

    def coeff_copy(n):
        z, r, _ = at(*DIRS[n])
        src, dst = fine_box(DIRS[n], 3, 3, (2, 2))
        return copy(
            co.at[(every, *src)], co.at[(every, *dst)], c_send.at[n], c_recv.at[n], (tm, z, r)
        )

    def coeff_pass(n):
        box = (every, *fine_box(DIRS[n], 3, 3, (2, 2))[1])
        return copy(co.at[box], co.at[box], w_send.at[n], w_recv.at[n], (sibling, *here))

    more = []
    for n, (dz, dr) in enumerate(DIRS):
        if dr == 0:
            continue
        z_src, z_dst = cuts(dz, 4, 4, 1 if dz else 4)
        near, away = ((5, 1), (4, 0)) if dr == 1 else ((2, 6), (3, 7))
        more.append((n, (z_src, every, both, pl.ds(away[0], 1)), (z_dst, every, both, pl.ds(away[1], 1))))
        if dz:
            part = pl.ds(0, 2) if dr == 1 else pl.ds(2, 2)
            more.append((n, (z_src, part, both, pl.ds(near[0], 1)), (z_dst, part, both, pl.ds(near[1], 1))))
        else:
            part = pl.ds(0, 1) if dr == 1 else pl.ds(3, 1)
            more.append((n, (z_src, part, both, pl.ds(near[0], 1)), (z_dst, part, both, pl.ds(near[1], 1))))
    for n, z_src, z_dst in ((0, 4, 0), (1, 7, 11)):
        box = (every, both, pl.ds(2, 4))
        more.append((n, (pl.ds(z_src, 1), *box), (pl.ds(z_dst, 1), *box)))
    more_dirs = [DIRS[n] for n, _, _ in more]

    def more_copy(q):
        n, src, dst = more[q]
        z, r, _ = at(*DIRS[n])
        return copy(
            co.at[(every, *src)], cw.at[(every, *dst)], g_send.at[q], g_recv.at[q], (tm, z, r)
        )

    def step_copy(n):
        z, r, _ = at(*DIRS[n])
        src, dst = fine_box(DIRS[n], 4, 4, (3, 3))
        return copy(sb.at[src], sb.at[dst], f_send.at[n], f_recv.at[n], (tm, z, r))

    def first_copy(n):
        z, r, _ = at(*DIRS[n])
        src, dst = fine_box(DIRS[n], 2, 4, (2, 4), blocks=2)
        return copy(bb.at[(0, *src)], bb.at[(0, *dst)], b_send.at[n], b_recv.at[n], (tm, z, r))

    def flat_guess_copy(n):
        z, r, _ = at(*DIRS[n])
        z_src, z_dst = cuts(DIRS[n][0], 3, 2, 2)
        return copy(e1.at[0, z_src], e1.at[0, z_dst], e_send.at[n], e_recv.at[n], (tm, z, r))

    def far_guess_copy(k):
        def make(n):
            z, r, _ = at(*TWO[n])
            z_src, z_dst = ((4, 0), (3, 7))[n]
            box = (both, pl.ds(0, 8) if k == 0 else pl.ds(2, 4))
            sem = 2 + 2 * k + n
            return copy(
                e1.at[(k, pl.ds(z_src, 1), *box)], e1.at[(k, pl.ds(z_dst, 1), *box)],
                e_send.at[sem], e_recv.at[sem], (tm, z, r),
            )

        return make

    def smooth_layer_copy(k):
        def make(n):
            z, r, _ = at(*DIRS[n])
            box = (every, both, pl.ds(1, 6))
            sem = 4 + 2 * k + n
            return copy(
                v1.at[(pl.ds(5, 2), *box)], vr.at[(k, pl.ds((1, 9)[n], 2), *box)],
                r_send.at[sem], r_recv.at[sem], (tm, z, r),
            )

        return make

    def guess_copy(n):
        z, r, _ = at(*DIRS[n])
        src, dst = coarse_box(DIRS[n], 2)
        return copy(
            e1.at[(1, *src)], e1.at[(1, *dst)], e_send.at[8 + n], e_recv.at[8 + n], (tm, z, r)
        )

    def last_guess_copy(n):
        if n == 8:
            box = (2, pl.ds(3, 2), both, pl.ds(2, 4))
            return copy(e1.at[box], e1.at[box], e_send.at[24], e_recv.at[24], (across, *here))
        z, r, _ = at(*DIRS[n])
        src, dst = coarse_box(DIRS[n], 1)
        return copy(
            e1.at[(2, *src)], e1.at[(2, *dst)], e_send.at[16 + n], e_recv.at[16 + n], (across, z, r)
        )

    def smooth_copy(n):
        z, r, _ = at(*DIRS[n])
        s_src, s_dst = (5, 1) if DIRS[n][1] == 1 else (2, 6)
        box = (pl.ds(3, 6), pl.ds(1 if DIRS[n][1] == 1 else 0, 3), both)
        return copy(
            v1.at[(*box, pl.ds(s_src, 1))], vr.at[(1, *box, pl.ds(s_dst, 1))],
            r_send.at[n], r_recv.at[n], (tm, z, r),
        )

    def jump_copy(field, n):
        z, r, _ = at(*DIRS[n])
        src, dst = fine_box(DIRS[n], 2, 2, (1, 1))
        return lambda target: copy(
            field.at[src], jj.at[(target, *dst)], r_send.at[n + 8], r_recv.at[n + 8 + 8 * target],
            ((sibling, z, r) if target == 0 else (tm, z, r)),
        )

    def start(make, order=range(8), dirs=DIRS):
        for n in order:
            _, _, there = at(*dirs[n])
            pl.when(there)(lambda n=n: make(n).start())

    def arrive(make, order=range(8), dirs=DIRS):
        for n in order:
            _, _, there = at(-dirs[n][0], -dirs[n][1])
            pl.when(there)(lambda n=n: make(n).wait_recv())

    def sent(make, order=range(8), dirs=DIRS):
        for n in order:
            _, _, there = at(*dirs[n])
            pl.when(there)(lambda n=n: make(n).wait_send())

    far = (4, 5, 6, 7, 2, 3, 0, 1)
    heavy = (0, 1, 4, 5, 6, 7, 2, 3)
    along = (0, 1)
    beside = (2, 3)

    @pl.when(is_lead)
    def _():
        start(coeff_copy, heavy)
        arrange(0)

    start(state_copy, heavy)
    swap.start()
    pl.when(jnp.logical_not(is_lead))(arrange_coeffs)

    window = copy(own, sx, m_send.at[0], m_recv.at[0], (across, *here))
    pl.when(tm == 2)(window.start)

    def zero(n):
        return jnp.zeros((4, 2, n, 128), jnp.float32)

    def loop(low, high, body, unroll=True):
        def wrapped(z, _):
            body(z)
            return 0

        lax.fori_loop(low, high, wrapped, 0, unroll=unroll)

    for edge, begin, begin_coarse in ((slab == 0, 0, 0), (slab == slabs - 1, 8, 5)):

        @pl.when(edge)
        def _():
            def clear(z):
                for m in range(4):
                    co[m, z] = zero(8)
                    cw[m, z] = zero(8)
                for field in (sa, sb, bb.at[0], vr.at[0], vr.at[1]):
                    field[z] = zero(8)

            loop(begin, begin + 4, clear)
            for k in range(3):
                for z in range(begin_coarse, begin_coarse + 3):
                    e1[k, z] = jnp.zeros((2, 8, 128), jnp.float32)
            for k in range(2):

                @pl.when(tm == 1 + 2 * k)
                def _():
                    for z in (2, 3) if begin == 0 else (8, 9):
                        jj[k, z] = zero(8)

    for edge, z in ((slab == 1, 0), (slab == slabs - 2, 7)):

        @pl.when(edge)
        def _():
            for k in range(2):
                e1[k, z] = jnp.zeros((2, 8, 128), jnp.float32)

    for edge, begin in ((coarse == 0, 0), (coarse == coarses - 1, 6)):

        @pl.when(edge)
        def _():
            s = pl.ds(begin, 2)

            def clear(z):
                for m in range(4):
                    co[m, z, :, :, s, :] = zero(2)
                    cw[m, z, :, :, s, :] = zero(2)
                for field in (sa, sb, bb.at[0]):
                    field[z, :, :, s, :] = zero(2)

            loop(0, 12, clear)
            for z in range(3, 9):
                vr[1, z, :, :, s, :] = zero(2)
            for k in range(2):

                @pl.when(tm == 1 + 2 * k)
                def _():
                    for z in range(2, 10):
                        jj[k, z, :, :, s, :] = zero(2)

            for k in (1, 2):
                for z in range(8):
                    e1[k, z, :, s, :] = jnp.zeros((2, 2, 128), jnp.float32)

    arrive(state_copy)
    swap.wait_recv()
    pl.when(is_lead)(lambda: arrive(coeff_copy))
    pl.when(jnp.logical_not(is_lead))(lambda: arrive(coeff_pass))

    scales, carries, tildes = chebyshev_coefficients(SECTIONS)

    def fine_step(begin, finish):
        def first(z):
            centre, spread, drift = operator(begin, co, z)
            ta[z] = centre + tildes[1] * (spread - drift)

        def later(degree, current, before, put):
            def body(z):
                centre, spread, drift = operator(current, co, z)
                put(
                    z,
                    scales[degree] * centre
                    + carries[degree] * before[z]
                    + tildes[degree] * (spread - drift),
                )

            return body

        def put_to(ref):
            def put(z, value):
                ref[z] = value

            return put

        loop(1, 11, first)
        loop(2, 10, later(2, ta, begin, put_to(ua)))
        loop(3, 9, later(3, ua, ta, put_to(ta)))
        loop(4, 8, later(4, ta, ua, finish))

    def to_own_rows(target, z, value):
        target[z, :, :, 2:6, :] = value[:, :, 2:6, :]

    def to_fe(z, value):
        fe[z - 4] = value

    fine_step(sa, lambda z, value: to_own_rows(sb, z, value))
    start(step_copy, far)

    @pl.when(is_lead)
    def _():
        for n in range(8):
            _, _, there = at(-DIRS[n][0], -DIRS[n][1])
            pl.when(there)(lambda n=n: coeff_pass(n).start())

    pl.when(tm == 1)(lambda: start(more_copy, range(len(more)), more_dirs))

    arrive(step_copy)
    fine_step(sb, to_fe)

    def weigh(z):
        weight[z] = RELAX / (1.0 + 12.0 * co[0, z])

    def halves(value):
        value = value[:, 0] + value[:, 1]
        return 0.125 * jnp.concatenate([value[0:1] + value[1:2], value[2:3] + value[3:4]], 0)

    def coarse_weigh(q):
        for m in range(4):
            mean = halves(co[m, 2 * q - 2] + co[m, 2 * q - 1])
            cco[m, q] = mean
            if m == 0:
                cweight[q] = RELAX / (1.0 + 3.0 * mean)

    def merge(low, high, first, last):
        def body(z):
            for m in range(4):
                for part, sub in ((every, 0), (every, 7), (first, 1), (last, 6)):
                    at_rows = (m, z, part, slice(None), pl.ds(sub, 1), slice(None))
                    co[at_rows] = cw[at_rows]

        for z in range(low, high):
            body(z)

    def weights():
        loop(2, 10, weigh)
        loop(1, 7, coarse_weigh)

    ends = copy(fe, fx, m_send.at[1], m_recv.at[1], (sibling, *here))
    ends_first = copy(fe, res, m_send.at[1], m_recv.at[1], (sibling, *here))
    jump = copy(
        jo.at[own_box(4)], jj.at[(0, *own_box(4))], m_send.at[2], m_recv.at[2], (sibling, *here)
    )
    jump_box = (1, pl.ds(2, 8), every, both, pl.ds(1, 6))
    last_jump = copy(jj.at[jump_box], jj.at[jump_box], m_send.at[4], m_recv.at[4], (across, *here))
    third = copy(res, res, m_send.at[3], m_recv.at[3], (sibling, *here))
    cross_boxes = (
        (2, pl.ds(2, 8), every, both, pl.ds(2, 4)),
        (2, pl.ds(3, 6), pl.ds(2, 2), both, pl.ds(1, 1)),
        (2, pl.ds(3, 6), pl.ds(0, 2), both, pl.ds(6, 1)),
    )
    cross = [
        copy(bb.at[box], bb.at[box], x_send.at[n], x_recv.at[n], (across, *here))
        for n, box in enumerate(cross_boxes)
    ]

    @pl.when(tm == 0)
    def _():
        window.wait_recv()
        for z in range(4):
            jo[z + 4] = fe[z] - sx[z]
        start(lambda n: jump_copy(jo, n)(0), far)
        jump.start()
        ends.start()
        ends_first.wait_recv()

    @pl.when(tm == 2)
    def _():
        ends.start()
        third.wait_recv()

    def solve_smooth(b):
        def smooth(z):
            centre, spread, drift = operator(b, co, z)
            v1[z] = centre + (2.0 * weight[z]) * (spread - drift)

        loop(3, 9, smooth)

    def solve_restrict(b, put):
        def restrict(q):
            total = None
            for z in (2 * q - 2, 2 * q - 1):
                centre, spread, drift = operator(v1, co, z)
                misfit = b[z] - centre + 2.0 * (spread - drift)
                total = misfit if total is None else total + misfit
            put(q, cweight[q] * halves(total))

        loop(3, 5, restrict)

    def solve_correct(e, base, reach):
        for q in range(3 - reach, 5 + reach):
            centre, spread, drift = operator(e, cco, q, fine=False)
            w = cweight[q]
            wide = spread_out((2.0 - w) * centre + w * (0.5 * spread - drift))
            for z in (2 * q - 2, 2 * q - 1):
                if z >= 4 - 2 * reach + (reach - 1) and z < 8 + 2 * reach - (reach - 1):
                    v2[z] = base(z) + wide

    def solve_finish(b, put, reach):
        def finish(z):
            centre, spread, drift = operator(v2, co, z)
            put(z, centre + weight[z] * (b[z] - centre + 2.0 * (spread - drift)))

        loop(4 - reach, 8 + reach, finish)

    def put_guess(k):
        def put(q, value):
            e1[k, q, :, 2:6, :] = value[:, 2:6, :]

        return put

    @pl.when(tm == 1)
    def _():
        b = bb.at[0]
        for z in range(4):
            b[z + 4, :, :, 2:6, :] = (fe[z] - own[z])[:, :, 2:6, :]
        start(first_copy, far)
        ends_first.start()
        arrive(more_copy, range(len(more)), more_dirs)
        merge(4, 8, pl.ds(0, 1), pl.ds(3, 1))
        for z in (3, 8):
            merge(z, z + 1, pl.ds(0, 2), pl.ds(2, 2))
        for z in (0, 11):
            for m in range(4):
                co[m, z, :, :, 2:6, :] = cw[m, z, :, :, 2:6, :]
        weights()
        arrive(first_copy)
        solve_smooth(b)
        start(smooth_layer_copy(0), along)

        def put_flat(q, value):
            e1[0, q] = value

        solve_restrict(b, put_flat)
        start(far_guess_copy(0), along, TWO)
        start(flat_guess_copy, along)
        arrive(smooth_layer_copy(0), along)
        arrive(flat_guess_copy, along)
        arrive(far_guess_copy(0), along, TWO)
        solve_correct(e1.at[0], lambda z: v1[z] if 3 <= z < 9 else vr[0, z], 2)
        arrive(lambda n: jump_copy(jo, n)(0))
        jump.wait_recv()
        b = bb.at[1]

        def put_first(z, value):
            bb[1, z] = value + jj[0, z]

        solve_finish(bb.at[0], put_first, 2)

        sent(smooth_layer_copy(0), along)
        solve_smooth(b)
        start(smooth_copy, beside)
        start(smooth_layer_copy(1), along)
        solve_restrict(b, put_guess(1))
        start(guess_copy, (4, 5, 6, 7, 2, 3))
        start(far_guess_copy(1), along, TWO)
        start(guess_copy, along)
        ends.wait_recv()
        for z in range(4):
            res[z] = fx[z] + (b[z + 4] - jj[0, z + 4])
        shape = (4, 2, 8, 128)
        i = lax.broadcasted_iota(jnp.int32, shape, 0)
        sub = lax.broadcasted_iota(jnp.int32, shape, 2)
        given = ((sub == 1) & (i > 0)) | ((sub == 6) & (i < 3))
        arrive(smooth_copy, beside)
        arrive(smooth_layer_copy(1), along)
        arrive(guess_copy)
        arrive(far_guess_copy(1), along, TWO)
        solve_correct(
            e1.at[1],
            lambda z: jnp.where(given, vr[1, z], v1[z]) if 3 <= z < 9 else vr[1, z],
            2,
        )
        last_jump.wait_recv()

        def put_second(z, value):
            bb[2, z] = value + jj[1, z]

        solve_finish(b, put_second, 2)

        b = bb.at[2]
        for part in cross:
            part.start()
        sent(smooth_copy, beside)
        sent(smooth_layer_copy(1), along)
        solve_smooth(b)
        solve_restrict(b, put_guess(2))
        start(last_guess_copy, far)
        last_guess_copy(8).start()

    @pl.when(tm == 3)
    def _():
        for z in range(4):
            value = fe[z] - own[z]
            jo[z + 4] = value
            to_own_rows(jj.at[1], z + 4, value)
        start(lambda n: jump_copy(jo, n)(1), far)
        weights()
        arrive(lambda n: jump_copy(jo, n)(1))
        last_jump.start()
        b = bb.at[2]
        for part in cross:
            part.wait_recv()
        for z in range(4):
            res[z] = b[z + 4] + own[z]
        third.start()
        solve_smooth(b)
        arrive(last_guess_copy)
        last_guess_copy(8).wait_recv()
        solve_correct(e1.at[2], lambda z: v1[z], 1)
        ends.wait_recv()
        third.wait_send()

        def put_last(z, value):
            res[z - 4] = fx[z - 4] + value

        solve_finish(b, put_last, 0)

    for z in range(4):
        for p in range(2):
            for i in range(4):
                dealt[0, z, p, pl.ds(i, 4, stride=4), :] = res[z, i, p, 2:6, :]
        low_part, high_part = join_columns(dealt[0, z, 0], dealt[0, z, 1])
        o_ref[z, :, 0:128] = low_part
        o_ref[z, :, 128:256] = high_part

    sent(state_copy)
    swap.wait_send()
    sent(step_copy)

    @pl.when(is_lead)
    def _():
        sent(coeff_copy)
        for n in range(8):
            _, _, there = at(-DIRS[n][0], -DIRS[n][1])
            pl.when(there)(lambda n=n: coeff_pass(n).wait_send())

    @pl.when(tm == 0)
    def _():
        sent(lambda n: jump_copy(jo, n)(0))
        jump.wait_send()
        ends.wait_send()

    @pl.when(tm == 2)
    def _():
        window.wait_send()
        ends.wait_send()

    @pl.when(tm == 1)
    def _():
        sent(more_copy, range(len(more)), more_dirs)
        sent(first_copy)
        ends_first.wait_send()
        sent(flat_guess_copy, along)
        sent(far_guess_copy(0), along, TWO)
        sent(guess_copy)
        sent(far_guess_copy(1), along, TWO)
        sent(last_guess_copy)
        last_guess_copy(8).wait_send()
        for part in cross:
            part.wait_send()

    @pl.when(tm == 3)
    def _():
        sent(lambda n: jump_copy(jo, n)(1))
        last_jump.wait_send()


def per_device(states, diffusivity, velocity):
    def vmem(*shape):
        return pltpu.VMEM(shape + (8, 128), jnp.float32)

    dma = pltpu.SemaphoreType.DMA
    block = pl.BlockSpec(memory_space=pltpu.HBM)
    raw = (states[0], diffusivity, velocity)
    counts = (9, 8, 8, 14, 8, 8, 25, 24, 3, 5)
    out = pl.pallas_call(
        kernel,
        name="parareal",
        out_shape=jax.ShapeDtypeStruct(diffusivity.shape, jnp.float32),
        in_specs=[block] * 3,
        out_specs=pl.BlockSpec(memory_space=pltpu.VMEM),
        scratch_shapes=[pltpu.VMEM(array.shape, jnp.float32) for array in raw]
        + [
            vmem(4, 4, 2),
            vmem(4, 12, 4, 2),
            vmem(4, 12, 4, 2),
            vmem(12, 4, 2),
            vmem(12, 4, 2),
            vmem(12, 4, 2),
            vmem(12, 4, 2),
            vmem(12, 4, 2),
            vmem(4, 4, 2),
            vmem(12, 4, 2),
            vmem(2, 12, 4, 2),
            vmem(3, 12, 4, 2),
            vmem(12, 4, 2),
            vmem(12, 4, 2),
            vmem(2, 12, 4, 2),
            vmem(3, 8, 2),
            vmem(4, 8, 2),
            vmem(8, 2),
            vmem(4, 4, 2),
            vmem(4, 4, 2),
            vmem(4, 4, 2),
            vmem(4, 4, 2),
            pltpu.VMEM((5, 4, 2, 16, 128), jnp.float32),
            dma((3,)),
        ]
        + [dma((n,)) for n in counts for _ in range(2)],
        compiler_params=pltpu.CompilerParams(
            collective_id=0, has_side_effects=True, vmem_limit_bytes=55168 * 1024
        ),
    )(*raw)
    return out[None]


def solution(mesh):
    return jax.shard_map(
        per_device,
        mesh=mesh,
        in_specs=(
            P("tm", "slab", "coarse", None),
            P("slab", "coarse", None),
            P(None, "slab", "coarse", None),
        ),
        out_specs=P("tm", "slab", "coarse", None),
        check_vma=False,
    )
```

```python
import jax
import jax.numpy as jnp
from jax import lax
from jax.experimental import pallas as pl
from jax.experimental.pallas import tpu as pltpu
from jax.sharding import PartitionSpec as P

MESH = pl.DeviceIdType.MESH
SECTIONS = 4
RELAX = 0.8


def chebyshev_coefficients(sections):
    damping = 0.05
    centre_point = 1.0 + damping / (sections * sections)
    chebyshev = [1.0, centre_point]
    slopes = [0.0, 1.0]
    for degree in range(2, sections + 1):
        chebyshev.append(2.0 * centre_point * chebyshev[degree - 1] - chebyshev[degree - 2])
        slopes.append(
            2.0 * chebyshev[degree - 1]
            + 2.0 * centre_point * slopes[degree - 1]
            - slopes[degree - 2]
        )
    slope_ratio = chebyshev[sections] / slopes[sections]
    weights = [1.0 / entry for entry in chebyshev]
    scales = [0.0, 0.0]
    carries = [0.0, 0.0]
    tildes = [0.0, slope_ratio / centre_point]
    for degree in range(2, sections + 1):
        scales.append(2.0 * weights[degree] * centre_point / weights[degree - 1])
        carries.append(-weights[degree] / weights[degree - 2])
        tildes.append(2.0 * weights[degree] * slope_ratio / weights[degree - 1])
    return (scales, carries, tildes)


TWO = ((2, 0), (-2, 0))
DIRS = ((1, 0), (-1, 0), (0, 1), (0, -1), (1, 1), (1, -1), (-1, 1), (-1, -1))


def cuts(step, low, count, wide):
    if step == 0:
        return pl.ds(low, count), pl.ds(low, count)
    if step == 1:
        return pl.ds(low + count - wide, wide), pl.ds(low - wide, wide)
    return pl.ds(low, wide), pl.ds(low + count, wide)


def fine_box(d, deep, rows, corner, blocks=1):
    dz, dr = d
    hz, hr = corner if dz and dr else (deep, rows)
    z_src, z_dst = cuts(dz, 4, 4, hz)
    every = pl.ds(0, 2)
    if dr == 0:
        box = (pl.ds(0, 4), every, pl.ds(2, 4))
        return (z_src, *box), (z_dst, *box)
    rows_at = pl.ds(4 - hr, hr) if dr == 1 else pl.ds(0, hr)
    s_src, s_dst = (6 - blocks, 2 - blocks) if dr == 1 else (2, 6)
    return (
        (z_src, rows_at, every, pl.ds(s_src, blocks)),
        (z_dst, rows_at, every, pl.ds(s_dst, blocks)),
    )


def coarse_box(d, blocks):
    dz, dr = d
    z_src, z_dst = cuts(dz, 3, 2, 2)
    every = pl.ds(0, 2)
    if dr == 0:
        return (z_src, every, pl.ds(2, 4)), (z_dst, every, pl.ds(2, 4))
    blocks = 1 if dz else blocks
    s_src, s_dst = (6 - blocks, 2 - blocks) if dr == 1 else (2, 6)
    return (z_src, every, pl.ds(s_src, blocks)), (z_dst, every, pl.ds(s_dst, blocks))


def lanes(shape):
    return lax.broadcasted_iota(jnp.int32, shape, len(shape) - 1)


def around(centre, fine):
    axis = centre.ndim - 2
    row_after = jnp.concatenate([centre[1:], pltpu.roll(centre[:1], 7, axis)], 0)
    row_before = jnp.concatenate([pltpu.roll(centre[-1:], 1, axis), centre[:-1]], 0)
    if fine:
        even, odd = centre[:, 0], centre[:, 1]
    else:
        even, odd = centre, centre
    at = lanes(even.shape)
    last = even.ndim - 1
    shifted_up = jnp.where(at == 127, 0.0, pltpu.roll(even, 127, last))
    shifted_down = jnp.where(at == 0, 0.0, pltpu.roll(odd, 1, last))
    if not fine:
        return row_after, row_before, shifted_up, shifted_down
    return (
        row_after,
        row_before,
        jnp.stack([odd, shifted_up], 1),
        jnp.stack([shifted_down, even], 1),
    )


def operator(field, coeffs, z, fine=True):
    centre, after, before = field[z], field[z + 1], field[z - 1]
    ra, rb, ca, cb = around(centre, fine)
    spread = coeffs[0, z] * (after + before + ra + rb + ca + cb - 6.0 * centre)
    drift = coeffs[1, z] * (after - before) + coeffs[2, z] * (ra - rb) + coeffs[3, z] * (ca - cb)
    return centre, spread, drift


def spread_out(value):
    wide = jnp.concatenate([value[:1], value[:1], value[1:], value[1:]], 0)
    return jnp.stack([wide, wide], 1)


def gathered(value, index):
    return jnp.take_along_axis(value, index, axis=1, mode="promise_in_bounds")


def split_columns(rows):
    low, high = rows[:, :128], rows[:, 128:]
    at = lanes(low.shape)
    source = (2 * at) % 128
    first = at < 64
    even = jnp.where(first, gathered(low, source), gathered(high, source))
    odd = jnp.where(first, gathered(low, source + 1), gathered(high, source + 1))
    return even, odd


def join_columns(even, odd):
    at = lanes(even.shape)
    half = at // 2
    is_even = at % 2 == 0
    low = jnp.where(is_even, gathered(even, half), gathered(odd, half))
    high = jnp.where(is_even, gathered(even, half + 64), gathered(odd, half + 64))
    return low, high


def kernel(
    s_hbm, d_hbm, v_hbm, o_ref,
    s_ref, d_ref, v_ref,
    own, co, cw, sa, sb, ta, ua, weight, fe, jo, jj, bb, v1, v2, vr, e1, cco, cweight,
    fx, sx, xout, res, dealt,
    in_sem, s_send, s_recv, c_send, c_recv, w_send, w_recv, g_send, g_recv,
    f_send, f_recv, b_send, b_recv, e_send, e_recv, r_send, r_recv, x_send, x_recv,
    m_send, m_recv,
):
    tm, slab, coarse = (lax.axis_index(a) for a in ("tm", "slab", "coarse"))
    slabs, coarses = lax.axis_size("slab"), lax.axis_size("coarse")
    loads = [
        pltpu.make_async_copy(src, dst, in_sem.at[n])
        for n, (src, dst) in enumerate(((s_hbm, s_ref), (d_hbm, d_ref), (v_hbm, v_ref)))
    ]
    for load in loads:
        load.start()

    def at(dz, dr):
        z, r = slab + dz, coarse + dr
        return z, r, (z >= 0) & (z < slabs) & (r >= 0) & (r < coarses)

    core = lax.rem(tm, 2)
    is_lead = core == 1
    sibling = tm + 1 - 2 * core
    across = lax.rem(tm + 2, 4)
    here = (slab, coarse)

    barrier = pltpu.get_barrier_semaphore()
    count = jnp.int32(2)
    for dz, dr in DIRS:
        z, r, there = at(dz, dr)

        @pl.when(there)
        def _():
            for t in (tm, sibling):
                pl.semaphore_signal(barrier, inc=1, device_id=(t, z, r), device_id_type=MESH)

        count = count + 2 * there.astype(jnp.int32)
    for t in (across, sibling):
        pl.semaphore_signal(barrier, inc=1, device_id=(t, *here), device_id_type=MESH)

    def arrange(m):
        if m < 3:
            loads[m].wait()
        for z in range(4):
            source = (s_ref, d_ref, v_ref.at[0], v_ref.at[1], v_ref.at[2])[m]
            target = own.at[z] if m == 0 else co.at[m - 1, z + 4]
            for p, part in enumerate(split_columns(source[z])):
                dealt[m, z, p] = 0.5 * part if m > 1 else part
                for i in range(4):
                    target[i, p, 2:6, :] = dealt[m, z, p, pl.ds(i, 4, stride=4), :]

    def arrange_coeffs():
        for m in range(1, 5):
            arrange(m)

    pl.when(is_lead)(arrange_coeffs)
    pl.when(jnp.logical_not(is_lead))(lambda: arrange(0))
    pl.semaphore_wait(barrier, count)

    def copy(src, dst, send, recv, device):
        return pltpu.make_async_remote_copy(
            src_ref=src, dst_ref=dst, send_sem=send, recv_sem=recv, device_id=device, device_id_type=MESH
        )

    def own_box(z):
        return (pl.ds(z, 4), pl.ds(0, 4), pl.ds(0, 2), pl.ds(2, 4))

    every = pl.ds(0, 4)
    both = pl.ds(0, 2)

    def state_copy(n):
        z, r, _ = at(*DIRS[n])
        (zs, *src), dst = fine_box(DIRS[n], 4, 4, (3, 3))
        src = (pl.ds(zs.start - 4, zs.size), *src)
        return copy(own.at[src], sa.at[dst], s_send.at[n], s_recv.at[n], (sibling, z, r))

    swap = copy(
        own.at[own_box(0)], sa.at[own_box(4)], s_send.at[8], s_recv.at[8], (sibling, *here)
    )

    def coeff_copy(n):
        z, r, _ = at(*DIRS[n])
        src, dst = fine_box(DIRS[n], 3, 3, (2, 2))
        return copy(
            co.at[(every, *src)], co.at[(every, *dst)], c_send.at[n], c_recv.at[n], (tm, z, r)
        )

    def coeff_pass(n):
        box = (every, *fine_box(DIRS[n], 3, 3, (2, 2))[1])
        return copy(co.at[box], co.at[box], w_send.at[n], w_recv.at[n], (sibling, *here))

    more = []
    for n, (dz, dr) in enumerate(DIRS):
        if dr == 0:
            continue
        z_src, z_dst = cuts(dz, 4, 4, 1 if dz else 4)
        near, away = ((5, 1), (4, 0)) if dr == 1 else ((2, 6), (3, 7))
        more.append((n, (z_src, every, both, pl.ds(away[0], 1)), (z_dst, every, both, pl.ds(away[1], 1))))
        if dz:
            part = pl.ds(0, 2) if dr == 1 else pl.ds(2, 2)
            more.append((n, (z_src, part, both, pl.ds(near[0], 1)), (z_dst, part, both, pl.ds(near[1], 1))))
        else:
            part = pl.ds(0, 1) if dr == 1 else pl.ds(3, 1)
            more.append((n, (z_src, part, both, pl.ds(near[0], 1)), (z_dst, part, both, pl.ds(near[1], 1))))
    for n, z_src, z_dst in ((0, 4, 0), (1, 7, 11)):
        box = (every, both, pl.ds(2, 4))
        more.append((n, (pl.ds(z_src, 1), *box), (pl.ds(z_dst, 1), *box)))
    more_dirs = [DIRS[n] for n, _, _ in more]

    def more_copy(q):
        n, src, dst = more[q]
        z, r, _ = at(*DIRS[n])
        return copy(
            co.at[(every, *src)], cw.at[(every, *dst)], g_send.at[q], g_recv.at[q], (tm, z, r)
        )

    def step_copy(n):
        z, r, _ = at(*DIRS[n])
        src, dst = fine_box(DIRS[n], 4, 4, (3, 3))
        return copy(sb.at[src], sb.at[dst], f_send.at[n], f_recv.at[n], (tm, z, r))

    def first_copy(n):
        z, r, _ = at(*DIRS[n])
        src, dst = fine_box(DIRS[n], 2, 4, (2, 4), blocks=2)
        return copy(bb.at[(0, *src)], bb.at[(0, *dst)], b_send.at[n], b_recv.at[n], (tm, z, r))

    def flat_guess_copy(n):
        z, r, _ = at(*DIRS[n])
        z_src, z_dst = cuts(DIRS[n][0], 3, 2, 2)
        return copy(e1.at[0, z_src], e1.at[0, z_dst], e_send.at[n], e_recv.at[n], (tm, z, r))

    def far_guess_copy(k):
        def make(n):
            z, r, _ = at(*TWO[n])
            z_src, z_dst = ((4, 0), (3, 7))[n]
            box = (both, pl.ds(0, 8) if k == 0 else pl.ds(2, 4))
            sem = 2 + 2 * k + n
            return copy(
                e1.at[(k, pl.ds(z_src, 1), *box)], e1.at[(k, pl.ds(z_dst, 1), *box)],
                e_send.at[sem], e_recv.at[sem], (tm, z, r),
            )

        return make

    def smooth_layer_copy(k):
        def make(n):
            z, r, _ = at(*DIRS[n])
            box = (every, both, pl.ds(1, 6))
            sem = 4 + 2 * k + n
            return copy(
                v1.at[(pl.ds(5, 2), *box)], vr.at[(k, pl.ds((1, 9)[n], 2), *box)],
                r_send.at[sem], r_recv.at[sem], (tm, z, r),
            )

        return make

    def guess_copy(n):
        z, r, _ = at(*DIRS[n])
        src, dst = coarse_box(DIRS[n], 2)
        return copy(
            e1.at[(1, *src)], e1.at[(1, *dst)], e_send.at[8 + n], e_recv.at[8 + n], (tm, z, r)
        )

    def last_guess_copy(n):
        if n == 8:
            box = (2, pl.ds(3, 2), both, pl.ds(2, 4))
            return copy(e1.at[box], e1.at[box], e_send.at[24], e_recv.at[24], (across, *here))
        z, r, _ = at(*DIRS[n])
        src, dst = coarse_box(DIRS[n], 1)
        return copy(
            e1.at[(2, *src)], e1.at[(2, *dst)], e_send.at[16 + n], e_recv.at[16 + n], (across, z, r)
        )

    def smooth_copy(n):
        z, r, _ = at(*DIRS[n])
        s_src, s_dst = (5, 1) if DIRS[n][1] == 1 else (2, 6)
        box = (pl.ds(3, 6), pl.ds(1 if DIRS[n][1] == 1 else 0, 3), both)
        return copy(
            v1.at[(*box, pl.ds(s_src, 1))], vr.at[(1, *box, pl.ds(s_dst, 1))],
            r_send.at[n], r_recv.at[n], (tm, z, r),
        )

    def jump_copy(field, n):
        z, r, _ = at(*DIRS[n])
        src, dst = fine_box(DIRS[n], 2, 2, (1, 1))
        return lambda target: copy(
            field.at[src], jj.at[(target, *dst)], r_send.at[n + 8], r_recv.at[n + 8 + 8 * target],
            ((sibling, z, r) if target == 0 else (tm, z, r)),
        )

    def start(make, order=range(8), dirs=DIRS):
        for n in order:
            _, _, there = at(*dirs[n])
            pl.when(there)(lambda n=n: make(n).start())

    def arrive(make, order=range(8), dirs=DIRS):
        for n in order:
            _, _, there = at(-dirs[n][0], -dirs[n][1])
            pl.when(there)(lambda n=n: make(n).wait_recv())

    def sent(make, order=range(8), dirs=DIRS):
        for n in order:
            _, _, there = at(*dirs[n])
            pl.when(there)(lambda n=n: make(n).wait_send())

    far = (4, 5, 6, 7, 2, 3, 0, 1)
    heavy = (0, 1, 4, 5, 6, 7, 2, 3)
    along = (0, 1)
    beside = (2, 3)

    @pl.when(is_lead)
    def _():
        start(coeff_copy, heavy)
        arrange(0)

    start(state_copy, heavy)
    swap.start()
    pl.when(jnp.logical_not(is_lead))(arrange_coeffs)

    window = copy(own, sx, m_send.at[0], m_recv.at[0], (across, *here))
    pl.when(tm == 2)(window.start)

    def zero(n):
        return jnp.zeros((4, 2, n, 128), jnp.float32)

    def loop(low, high, body, unroll=True):
        def wrapped(z, _):
            body(z)
            return 0

        lax.fori_loop(low, high, wrapped, 0, unroll=unroll)

    for edge, begin, begin_coarse in ((slab == 0, 0, 0), (slab == slabs - 1, 8, 5)):

        @pl.when(edge)
        def _():
            def clear(z):
                for m in range(4):
                    co[m, z] = zero(8)
                    cw[m, z] = zero(8)
                for field in (sa, sb, bb.at[0], vr.at[0], vr.at[1]):
                    field[z] = zero(8)

            loop(begin, begin + 4, clear)
            for k in range(3):
                for z in range(begin_coarse, begin_coarse + 3):
                    e1[k, z] = jnp.zeros((2, 8, 128), jnp.float32)
            for k in range(2):

                @pl.when(tm == 1 + 2 * k)
                def _():
                    for z in (2, 3) if begin == 0 else (8, 9):
                        jj[k, z] = zero(8)

    for edge, z in ((slab == 1, 0), (slab == slabs - 2, 7)):

        @pl.when(edge)
        def _():
            for k in range(2):
                e1[k, z] = jnp.zeros((2, 8, 128), jnp.float32)

    for edge, begin in ((coarse == 0, 0), (coarse == coarses - 1, 6)):

        @pl.when(edge)
        def _():
            s = pl.ds(begin, 2)

            def clear(z):
                for m in range(4):
                    co[m, z, :, :, s, :] = zero(2)
                    cw[m, z, :, :, s, :] = zero(2)
                for field in (sa, sb, bb.at[0]):
                    field[z, :, :, s, :] = zero(2)

            loop(0, 12, clear)
            for z in range(3, 9):
                vr[1, z, :, :, s, :] = zero(2)
            for k in range(2):

                @pl.when(tm == 1 + 2 * k)
                def _():
                    for z in range(2, 10):
                        jj[k, z, :, :, s, :] = zero(2)

            for k in (1, 2):
                for z in range(8):
                    e1[k, z, :, s, :] = jnp.zeros((2, 2, 128), jnp.float32)

    arrive(state_copy)
    swap.wait_recv()
    pl.when(is_lead)(lambda: arrive(coeff_copy))
    pl.when(jnp.logical_not(is_lead))(lambda: arrive(coeff_pass))

    scales, carries, tildes = chebyshev_coefficients(SECTIONS)

    def fine_step(begin, finish):
        def first(z):
            centre, spread, drift = operator(begin, co, z)
            ta[z] = centre + tildes[1] * (spread - drift)

        def later(degree, current, before, put):
            def body(z):
                centre, spread, drift = operator(current, co, z)
                put(
                    z,
                    scales[degree] * centre
                    + carries[degree] * before[z]
                    + tildes[degree] * (spread - drift),
                )

            return body

        def put_to(ref):
            def put(z, value):
                ref[z] = value

            return put

        loop(1, 11, first)
        loop(2, 10, later(2, ta, begin, put_to(ua)))
        loop(3, 9, later(3, ua, ta, put_to(ta)))
        loop(4, 8, later(4, ta, ua, finish))

    def to_own_rows(target, z, value):
        target[z, :, :, 2:6, :] = value[:, :, 2:6, :]

    def to_fe(z, value):
        fe[z - 4] = value

    fine_step(sa, lambda z, value: to_own_rows(sb, z, value))
    start(step_copy, far)

    @pl.when(is_lead)
    def _():
        for n in range(8):
            _, _, there = at(-DIRS[n][0], -DIRS[n][1])
            pl.when(there)(lambda n=n: coeff_pass(n).start())

    pl.when(tm == 1)(lambda: start(more_copy, range(len(more)), more_dirs))

    arrive(step_copy)
    fine_step(sb, to_fe)

    def weigh(z):
        weight[z] = RELAX / (1.0 + 12.0 * co[0, z])

    def halves(value):
        value = value[:, 0] + value[:, 1]
        return 0.125 * jnp.concatenate([value[0:1] + value[1:2], value[2:3] + value[3:4]], 0)

    def coarse_weigh(q):
        for m in range(4):
            mean = halves(co[m, 2 * q - 2] + co[m, 2 * q - 1])
            cco[m, q] = mean
            if m == 0:
                cweight[q] = RELAX / (1.0 + 3.0 * mean)

    def merge(low, high, first, last):
        def body(z):
            for m in range(4):
                for part, sub in ((every, 0), (every, 7), (first, 1), (last, 6)):
                    at_rows = (m, z, part, slice(None), pl.ds(sub, 1), slice(None))
                    co[at_rows] = cw[at_rows]

        for z in range(low, high):
            body(z)

    def weights():
        loop(2, 10, weigh)
        loop(1, 7, coarse_weigh)

    ends = copy(fe, fx, m_send.at[1], m_recv.at[1], (sibling, *here))
    ends_first = copy(fe, res, m_send.at[1], m_recv.at[1], (sibling, *here))
    jump = copy(
        jo.at[own_box(4)], jj.at[(0, *own_box(4))], m_send.at[2], m_recv.at[2], (sibling, *here)
    )
    jump_box = (1, pl.ds(2, 8), every, both, pl.ds(1, 6))
    last_jump = copy(jj.at[jump_box], jj.at[jump_box], m_send.at[4], m_recv.at[4], (across, *here))
    third = copy(res, res, m_send.at[3], m_recv.at[3], (sibling, *here))
    cross_boxes = (
        (2, pl.ds(3, 6), every, both, pl.ds(2, 4)),
        (2, pl.ds(3, 6), pl.ds(2, 2), both, pl.ds(1, 1)),
        (2, pl.ds(3, 6), pl.ds(0, 2), both, pl.ds(6, 1)),
        (2, pl.ds(2, 1), every, both, pl.ds(2, 4)),
        (2, pl.ds(9, 1), every, both, pl.ds(2, 4)),
    )
    cross = [
        copy(bb.at[box], bb.at[box], x_send.at[n], x_recv.at[n], (across, *here))
        for n, box in enumerate(cross_boxes)
    ]

    @pl.when(tm == 0)
    def _():
        window.wait_recv()
        for z in range(4):
            jo[z + 4] = fe[z] - sx[z]
        start(lambda n: jump_copy(jo, n)(0), far)
        jump.start()
        ends.start()
        ends_first.wait_recv()

    @pl.when(tm == 2)
    def _():
        ends.start()
        third.wait_recv()

    def solve_smooth(b, spans=((3, 9),)):
        def smooth(z):
            centre, spread, drift = operator(b, co, z)
            v1[z] = centre + (2.0 * weight[z]) * (spread - drift)

        for low, high in spans:
            loop(low, high, smooth)

    def solve_restrict(b, put):
        def restrict(q):
            total = None
            for z in (2 * q - 2, 2 * q - 1):
                centre, spread, drift = operator(v1, co, z)
                misfit = b[z] - centre + 2.0 * (spread - drift)
                total = misfit if total is None else total + misfit
            put(q, cweight[q] * halves(total))

        loop(3, 5, restrict)

    def solve_correct(e, base, reach):
        for q in range(3 - reach, 5 + reach):
            centre, spread, drift = operator(e, cco, q, fine=False)
            w = cweight[q]
            wide = spread_out((2.0 - w) * centre + w * (0.5 * spread - drift))
            for z in (2 * q - 2, 2 * q - 1):
                if z >= 4 - 2 * reach + (reach - 1) and z < 8 + 2 * reach - (reach - 1):
                    v2[z] = base(z) + wide

    def solve_finish(b, put, reach):
        def finish(z):
            centre, spread, drift = operator(v2, co, z)
            put(z, centre + weight[z] * (b[z] - centre + 2.0 * (spread - drift)))

        loop(4 - reach, 8 + reach, finish)

    def put_guess(k):
        def put(q, value):
            e1[k, q, :, 2:6, :] = value[:, 2:6, :]

        return put

    @pl.when(tm == 1)
    def _():
        b = bb.at[0]
        for z in range(4):
            b[z + 4, :, :, 2:6, :] = (fe[z] - own[z])[:, :, 2:6, :]
        start(first_copy, far)
        ends_first.start()
        arrive(more_copy, range(len(more)), more_dirs)
        merge(4, 8, pl.ds(0, 1), pl.ds(3, 1))
        for z in (3, 8):
            merge(z, z + 1, pl.ds(0, 2), pl.ds(2, 2))
        for z in (0, 11):
            for m in range(4):
                co[m, z, :, :, 2:6, :] = cw[m, z, :, :, 2:6, :]
        weights()
        arrive(first_copy)
        solve_smooth(b)
        start(smooth_layer_copy(0), along)

        def put_flat(q, value):
            e1[0, q] = value

        solve_restrict(b, put_flat)
        start(far_guess_copy(0), along, TWO)
        start(flat_guess_copy, along)
        arrive(smooth_layer_copy(0), along)
        arrive(flat_guess_copy, along)
        arrive(far_guess_copy(0), along, TWO)
        solve_correct(e1.at[0], lambda z: v1[z] if 3 <= z < 9 else vr[0, z], 2)
        arrive(lambda n: jump_copy(jo, n)(0))
        jump.wait_recv()
        b = bb.at[1]

        def put_first(z, value):
            bb[1, z] = value + jj[0, z]

        solve_finish(bb.at[0], put_first, 2)

        sent(smooth_layer_copy(0), along)
        solve_smooth(b)
        start(smooth_copy, beside)
        start(smooth_layer_copy(1), along)
        solve_restrict(b, put_guess(1))
        start(guess_copy, (4, 5, 6, 7, 2, 3))
        start(far_guess_copy(1), along, TWO)
        start(guess_copy, along)
        ends.wait_recv()
        for z in range(4):
            res[z] = fx[z] + (b[z + 4] - jj[0, z + 4])
        shape = (4, 2, 8, 128)
        i = lax.broadcasted_iota(jnp.int32, shape, 0)
        sub = lax.broadcasted_iota(jnp.int32, shape, 2)
        given = ((sub == 1) & (i > 0)) | ((sub == 6) & (i < 3))
        arrive(smooth_copy, beside)
        arrive(smooth_layer_copy(1), along)
        arrive(guess_copy)
        arrive(far_guess_copy(1), along, TWO)
        solve_correct(
            e1.at[1],
            lambda z: jnp.where(given, vr[1, z], v1[z]) if 3 <= z < 9 else vr[1, z],
            2,
        )
        last_jump.wait_recv()

        def put_second(z, value):
            bb[2, z] = value + jj[1, z]

        solve_finish(b, put_second, 2)

        b = bb.at[2]
        for part in cross:
            part.start()
        sent(smooth_copy, beside)
        sent(smooth_layer_copy(1), along)
        solve_smooth(b)
        solve_restrict(b, put_guess(2))
        start(last_guess_copy, far)
        last_guess_copy(8).start()

    @pl.when(tm == 3)
    def _():
        for z in range(4):
            value = fe[z] - own[z]
            jo[z + 4] = value
            to_own_rows(jj.at[1], z + 4, value)
        start(lambda n: jump_copy(jo, n)(1), far)
        weights()
        arrive(lambda n: jump_copy(jo, n)(1))
        last_jump.start()
        b = bb.at[2]
        for part in cross[:3]:
            part.wait_recv()
        for z in range(4):
            res[z] = b[z + 4] + own[z]
        third.start()
        solve_smooth(b, ((4, 8),))
        for part in cross[3:]:
            part.wait_recv()
        solve_smooth(b, ((3, 4), (8, 9)))
        arrive(last_guess_copy)
        last_guess_copy(8).wait_recv()
        solve_correct(e1.at[2], lambda z: v1[z], 1)
        ends.wait_recv()
        third.wait_send()

        def put_last(z, value):
            res[z - 4] = fx[z - 4] + value

        solve_finish(b, put_last, 0)

    for z in range(4):
        for p in range(2):
            for i in range(4):
                dealt[0, z, p, pl.ds(i, 4, stride=4), :] = res[z, i, p, 2:6, :]
        low_part, high_part = join_columns(dealt[0, z, 0], dealt[0, z, 1])
        o_ref[z, :, 0:128] = low_part
        o_ref[z, :, 128:256] = high_part

    sent(state_copy)
    swap.wait_send()
    sent(step_copy)

    @pl.when(is_lead)
    def _():
        sent(coeff_copy)
        for n in range(8):
            _, _, there = at(-DIRS[n][0], -DIRS[n][1])
            pl.when(there)(lambda n=n: coeff_pass(n).wait_send())

    @pl.when(tm == 0)
    def _():
        sent(lambda n: jump_copy(jo, n)(0))
        jump.wait_send()
        ends.wait_send()

    @pl.when(tm == 2)
    def _():
        window.wait_send()
        ends.wait_send()

    @pl.when(tm == 1)
    def _():
        sent(more_copy, range(len(more)), more_dirs)
        sent(first_copy)
        ends_first.wait_send()
        sent(flat_guess_copy, along)
        sent(far_guess_copy(0), along, TWO)
        sent(guess_copy)
        sent(far_guess_copy(1), along, TWO)
        sent(last_guess_copy)
        last_guess_copy(8).wait_send()
        for part in cross:
            part.wait_send()

    @pl.when(tm == 3)
    def _():
        sent(lambda n: jump_copy(jo, n)(1))
        last_jump.wait_send()


def per_device(states, diffusivity, velocity):
    def vmem(*shape):
        return pltpu.VMEM(shape + (8, 128), jnp.float32)

    dma = pltpu.SemaphoreType.DMA
    block = pl.BlockSpec(memory_space=pltpu.HBM)
    raw = (states[0], diffusivity, velocity)
    counts = (9, 8, 8, 14, 8, 8, 25, 24, 5, 5)
    out = pl.pallas_call(
        kernel,
        name="parareal",
        out_shape=jax.ShapeDtypeStruct(diffusivity.shape, jnp.float32),
        in_specs=[block] * 3,
        out_specs=pl.BlockSpec(memory_space=pltpu.VMEM),
        scratch_shapes=[pltpu.VMEM(array.shape, jnp.float32) for array in raw]
        + [
            vmem(4, 4, 2),
            vmem(4, 12, 4, 2),
            vmem(4, 12, 4, 2),
            vmem(12, 4, 2),
            vmem(12, 4, 2),
            vmem(12, 4, 2),
            vmem(12, 4, 2),
            vmem(12, 4, 2),
            vmem(4, 4, 2),
            vmem(12, 4, 2),
            vmem(2, 12, 4, 2),
            vmem(3, 12, 4, 2),
            vmem(12, 4, 2),
            vmem(12, 4, 2),
            vmem(2, 12, 4, 2),
            vmem(3, 8, 2),
            vmem(4, 8, 2),
            vmem(8, 2),
            vmem(4, 4, 2),
            vmem(4, 4, 2),
            vmem(4, 4, 2),
            vmem(4, 4, 2),
            pltpu.VMEM((5, 4, 2, 16, 128), jnp.float32),
            dma((3,)),
        ]
        + [dma((n,)) for n in counts for _ in range(2)],
        compiler_params=pltpu.CompilerParams(
            collective_id=0, has_side_effects=True, vmem_limit_bytes=55168 * 1024
        ),
    )(*raw)
    return out[None]


def solution(mesh):
    return jax.shard_map(
        per_device,
        mesh=mesh,
        in_specs=(
            P("tm", "slab", "coarse", None),
            P("slab", "coarse", None),
            P(None, "slab", "coarse", None),
        ),
        out_specs=P("tm", "slab", "coarse", None),
        check_vma=False,
    )
```

```python
import jax
import jax.numpy as jnp
from jax import lax
from jax.experimental import pallas as pl
from jax.experimental.pallas import tpu as pltpu
from jax.sharding import PartitionSpec as P

MESH = pl.DeviceIdType.MESH
SECTIONS = 4
RELAX = 0.8


def chebyshev_coefficients(sections):
    damping = 0.05
    centre_point = 1.0 + damping / (sections * sections)
    chebyshev = [1.0, centre_point]
    slopes = [0.0, 1.0]
    for degree in range(2, sections + 1):
        chebyshev.append(2.0 * centre_point * chebyshev[degree - 1] - chebyshev[degree - 2])
        slopes.append(
            2.0 * chebyshev[degree - 1]
            + 2.0 * centre_point * slopes[degree - 1]
            - slopes[degree - 2]
        )
    slope_ratio = chebyshev[sections] / slopes[sections]
    weights = [1.0 / entry for entry in chebyshev]
    scales = [0.0, 0.0]
    carries = [0.0, 0.0]
    tildes = [0.0, slope_ratio / centre_point]
    for degree in range(2, sections + 1):
        scales.append(2.0 * weights[degree] * centre_point / weights[degree - 1])
        carries.append(-weights[degree] / weights[degree - 2])
        tildes.append(2.0 * weights[degree] * slope_ratio / weights[degree - 1])
    return (scales, carries, tildes)


TWO = ((2, 0), (-2, 0))
DIRS = ((1, 0), (-1, 0), (0, 1), (0, -1), (1, 1), (1, -1), (-1, 1), (-1, -1))


def cuts(step, low, count, wide):
    if step == 0:
        return pl.ds(low, count), pl.ds(low, count)
    if step == 1:
        return pl.ds(low + count - wide, wide), pl.ds(low - wide, wide)
    return pl.ds(low, wide), pl.ds(low + count, wide)


def fine_box(d, deep, rows, corner, blocks=1):
    dz, dr = d
    hz, hr = corner if dz and dr else (deep, rows)
    z_src, z_dst = cuts(dz, 4, 4, hz)
    every = pl.ds(0, 2)
    if dr == 0:
        box = (pl.ds(0, 4), every, pl.ds(2, 4))
        return (z_src, *box), (z_dst, *box)
    rows_at = pl.ds(4 - hr, hr) if dr == 1 else pl.ds(0, hr)
    s_src, s_dst = (6 - blocks, 2 - blocks) if dr == 1 else (2, 6)
    return (
        (z_src, rows_at, every, pl.ds(s_src, blocks)),
        (z_dst, rows_at, every, pl.ds(s_dst, blocks)),
    )


def coarse_box(d, blocks):
    dz, dr = d
    z_src, z_dst = cuts(dz, 3, 2, 2)
    every = pl.ds(0, 2)
    if dr == 0:
        return (z_src, every, pl.ds(2, 4)), (z_dst, every, pl.ds(2, 4))
    blocks = 1 if dz else blocks
    s_src, s_dst = (6 - blocks, 2 - blocks) if dr == 1 else (2, 6)
    return (z_src, every, pl.ds(s_src, blocks)), (z_dst, every, pl.ds(s_dst, blocks))


def lanes(shape):
    return lax.broadcasted_iota(jnp.int32, shape, len(shape) - 1)


def around(centre, fine):
    axis = centre.ndim - 2
    row_after = jnp.concatenate([centre[1:], pltpu.roll(centre[:1], 7, axis)], 0)
    row_before = jnp.concatenate([pltpu.roll(centre[-1:], 1, axis), centre[:-1]], 0)
    if fine:
        even, odd = centre[:, 0], centre[:, 1]
    else:
        even, odd = centre, centre
    at = lanes(even.shape)
    last = even.ndim - 1
    shifted_up = jnp.where(at == 127, 0.0, pltpu.roll(even, 127, last))
    shifted_down = jnp.where(at == 0, 0.0, pltpu.roll(odd, 1, last))
    if not fine:
        return row_after, row_before, shifted_up, shifted_down
    return (
        row_after,
        row_before,
        jnp.stack([odd, shifted_up], 1),
        jnp.stack([shifted_down, even], 1),
    )


def operator(field, coeffs, z, fine=True):
    centre, after, before = field[z], field[z + 1], field[z - 1]
    ra, rb, ca, cb = around(centre, fine)
    spread = coeffs[0, z] * (after + before + ra + rb + ca + cb - 6.0 * centre)
    drift = coeffs[1, z] * (after - before) + coeffs[2, z] * (ra - rb) + coeffs[3, z] * (ca - cb)
    return centre, spread, drift


def spread_out(value):
    wide = jnp.concatenate([value[:1], value[:1], value[1:], value[1:]], 0)
    return jnp.stack([wide, wide], 1)


def gathered(value, index):
    return jnp.take_along_axis(value, index, axis=1, mode="promise_in_bounds")


def split_columns(rows):
    low, high = rows[:, :128], rows[:, 128:]
    at = lanes(low.shape)
    source = (2 * at) % 128
    first = at < 64
    even = jnp.where(first, gathered(low, source), gathered(high, source))
    odd = jnp.where(first, gathered(low, source + 1), gathered(high, source + 1))
    return even, odd


def join_columns(even, odd):
    at = lanes(even.shape)
    half = at // 2
    is_even = at % 2 == 0
    low = jnp.where(is_even, gathered(even, half), gathered(odd, half))
    high = jnp.where(is_even, gathered(even, half + 64), gathered(odd, half + 64))
    return low, high


def kernel(
    s_hbm, d_hbm, v_hbm, o_ref,
    s_ref, d_ref, v_ref,
    own, co, cw, sa, sb, ta, ua, weight, fe, jo, jj, bb, v1, v2, vr, e1, cco, cweight,
    fx, sx, xout, res, dealt,
    in_sem, s_send, s_recv, c_send, c_recv, w_send, w_recv, g_send, g_recv,
    f_send, f_recv, b_send, b_recv, e_send, e_recv, r_send, r_recv, x_send, x_recv,
    m_send, m_recv,
):
    tm, slab, coarse = (lax.axis_index(a) for a in ("tm", "slab", "coarse"))
    slabs, coarses = lax.axis_size("slab"), lax.axis_size("coarse")
    loads = [
        pltpu.make_async_copy(src, dst, in_sem.at[n])
        for n, (src, dst) in enumerate(((s_hbm, s_ref), (d_hbm, d_ref), (v_hbm, v_ref)))
    ]
    for load in loads:
        load.start()

    def at(dz, dr):
        z, r = slab + dz, coarse + dr
        return z, r, (z >= 0) & (z < slabs) & (r >= 0) & (r < coarses)

    core = lax.rem(tm, 2)
    is_lead = core == 1
    sibling = tm + 1 - 2 * core
    across = lax.rem(tm + 2, 4)
    here = (slab, coarse)

    barrier = pltpu.get_barrier_semaphore()
    count = jnp.int32(2)
    for dz, dr in DIRS:
        z, r, there = at(dz, dr)

        @pl.when(there)
        def _():
            for t in (tm, sibling):
                pl.semaphore_signal(barrier, inc=1, device_id=(t, z, r), device_id_type=MESH)

        count = count + 2 * there.astype(jnp.int32)
    for t in (across, sibling):
        pl.semaphore_signal(barrier, inc=1, device_id=(t, *here), device_id_type=MESH)

    def arrange(m):
        if m < 3:
            loads[m].wait()
        for z in range(4):
            source = (s_ref, d_ref, v_ref.at[0], v_ref.at[1], v_ref.at[2])[m]
            target = own.at[z] if m == 0 else co.at[m - 1, z + 4]
            for p, part in enumerate(split_columns(source[z])):
                dealt[m, z, p] = 0.5 * part if m > 1 else part
                for i in range(4):
                    target[i, p, 2:6, :] = dealt[m, z, p, pl.ds(i, 4, stride=4), :]

    def arrange_coeffs():
        for m in range(1, 5):
            arrange(m)

    pl.when(is_lead)(arrange_coeffs)
    pl.when(jnp.logical_not(is_lead))(lambda: arrange(0))
    pl.semaphore_wait(barrier, count)

    def copy(src, dst, send, recv, device):
        return pltpu.make_async_remote_copy(
            src_ref=src, dst_ref=dst, send_sem=send, recv_sem=recv, device_id=device, device_id_type=MESH
        )

    def own_box(z):
        return (pl.ds(z, 4), pl.ds(0, 4), pl.ds(0, 2), pl.ds(2, 4))

    every = pl.ds(0, 4)
    both = pl.ds(0, 2)

    def state_copy(n):
        z, r, _ = at(*DIRS[n])
        (zs, *src), dst = fine_box(DIRS[n], 4, 4, (3, 3))
        src = (pl.ds(zs.start - 4, zs.size), *src)
        return copy(own.at[src], sa.at[dst], s_send.at[n], s_recv.at[n], (sibling, z, r))

    swap = copy(
        own.at[own_box(0)], sa.at[own_box(4)], s_send.at[8], s_recv.at[8], (sibling, *here)
    )

    def coeff_copy(n):
        z, r, _ = at(*DIRS[n])
        src, dst = fine_box(DIRS[n], 3, 3, (2, 2))
        return copy(
            co.at[(every, *src)], co.at[(every, *dst)], c_send.at[n], c_recv.at[n], (tm, z, r)
        )

    def coeff_pass(n):
        box = (every, *fine_box(DIRS[n], 3, 3, (2, 2))[1])
        return copy(co.at[box], co.at[box], w_send.at[n], w_recv.at[n], (sibling, *here))

    more = []
    for n, (dz, dr) in enumerate(DIRS):
        if dr == 0:
            continue
        z_src, z_dst = cuts(dz, 4, 4, 1 if dz else 4)
        near, away = ((5, 1), (4, 0)) if dr == 1 else ((2, 6), (3, 7))
        more.append((n, (z_src, every, both, pl.ds(away[0], 1)), (z_dst, every, both, pl.ds(away[1], 1))))
        if dz:
            part = pl.ds(0, 2) if dr == 1 else pl.ds(2, 2)
            more.append((n, (z_src, part, both, pl.ds(near[0], 1)), (z_dst, part, both, pl.ds(near[1], 1))))
        else:
            part = pl.ds(0, 1) if dr == 1 else pl.ds(3, 1)
            more.append((n, (z_src, part, both, pl.ds(near[0], 1)), (z_dst, part, both, pl.ds(near[1], 1))))
    for n, z_src, z_dst in ((0, 4, 0), (1, 7, 11)):
        box = (every, both, pl.ds(2, 4))
        more.append((n, (pl.ds(z_src, 1), *box), (pl.ds(z_dst, 1), *box)))
    more_dirs = [DIRS[n] for n, _, _ in more]

    def more_copy(q):
        n, src, dst = more[q]
        z, r, _ = at(*DIRS[n])
        return copy(
            co.at[(every, *src)], cw.at[(every, *dst)], g_send.at[q], g_recv.at[q], (tm, z, r)
        )

    def step_copy(n):
        z, r, _ = at(*DIRS[n])
        src, dst = fine_box(DIRS[n], 4, 4, (3, 3))
        return copy(sb.at[src], sb.at[dst], f_send.at[n], f_recv.at[n], (tm, z, r))

    def first_copy(n):
        z, r, _ = at(*DIRS[n])
        src, dst = fine_box(DIRS[n], 2, 4, (2, 4), blocks=2)
        return copy(bb.at[(0, *src)], bb.at[(0, *dst)], b_send.at[n], b_recv.at[n], (tm, z, r))

    def flat_guess_copy(n):
        z, r, _ = at(*DIRS[n])
        z_src, z_dst = cuts(DIRS[n][0], 3, 2, 2)
        return copy(e1.at[0, z_src], e1.at[0, z_dst], e_send.at[n], e_recv.at[n], (tm, z, r))

    def far_guess_copy(k):
        def make(n):
            z, r, _ = at(*TWO[n])
            z_src, z_dst = ((4, 0), (3, 7))[n]
            box = (both, pl.ds(0, 8) if k == 0 else pl.ds(2, 4))
            sem = 2 + 2 * k + n
            return copy(
                e1.at[(k, pl.ds(z_src, 1), *box)], e1.at[(k, pl.ds(z_dst, 1), *box)],
                e_send.at[sem], e_recv.at[sem], (tm, z, r),
            )

        return make

    def smooth_layer_copy(k):
        def make(n):
            z, r, _ = at(*DIRS[n])
            box = (every, both, pl.ds(1, 6))
            sem = 4 + 2 * k + n
            return copy(
                v1.at[(pl.ds(5, 2), *box)], vr.at[(k, pl.ds((1, 9)[n], 2), *box)],
                r_send.at[sem], r_recv.at[sem], (tm, z, r),
            )

        return make

    def guess_copy(n):
        z, r, _ = at(*DIRS[n])
        src, dst = coarse_box(DIRS[n], 2)
        return copy(
            e1.at[(1, *src)], e1.at[(1, *dst)], e_send.at[8 + n], e_recv.at[8 + n], (tm, z, r)
        )

    def last_guess_copy(n):
        if n == 8:
            box = (2, pl.ds(3, 2), both, pl.ds(2, 4))
            return copy(e1.at[box], e1.at[box], e_send.at[24], e_recv.at[24], (across, *here))
        z, r, _ = at(*DIRS[n])
        src, dst = coarse_box(DIRS[n], 1)
        return copy(
            e1.at[(2, *src)], e1.at[(2, *dst)], e_send.at[16 + n], e_recv.at[16 + n], (across, z, r)
        )

    def smooth_copy(n):
        z, r, _ = at(*DIRS[n])
        s_src, s_dst = (5, 1) if DIRS[n][1] == 1 else (2, 6)
        box = (pl.ds(3, 6), pl.ds(1 if DIRS[n][1] == 1 else 0, 3), both)
        return copy(
            v1.at[(*box, pl.ds(s_src, 1))], vr.at[(1, *box, pl.ds(s_dst, 1))],
            r_send.at[n], r_recv.at[n], (tm, z, r),
        )

    def jump_copy(field, n):
        z, r, _ = at(*DIRS[n])
        src, dst = fine_box(DIRS[n], 2, 2, (1, 1))
        return lambda target: copy(
            field.at[src], jj.at[(target, *dst)], r_send.at[n + 8], r_recv.at[n + 8 + 8 * target],
            ((sibling, z, r) if target == 0 else (tm, z, r)),
        )

    def start(make, order=range(8), dirs=DIRS):
        for n in order:
            _, _, there = at(*dirs[n])
            pl.when(there)(lambda n=n: make(n).start())

    def arrive(make, order=range(8), dirs=DIRS):
        for n in order:
            _, _, there = at(-dirs[n][0], -dirs[n][1])
            pl.when(there)(lambda n=n: make(n).wait_recv())

    def sent(make, order=range(8), dirs=DIRS):
        for n in order:
            _, _, there = at(*dirs[n])
            pl.when(there)(lambda n=n: make(n).wait_send())

    far = (4, 5, 6, 7, 2, 3, 0, 1)
    heavy = (0, 1, 4, 5, 6, 7, 2, 3)
    along = (0, 1)
    beside = (2, 3)

    @pl.when(is_lead)
    def _():
        start(coeff_copy, heavy)
        arrange(0)

    start(state_copy, heavy)
    swap.start()
    pl.when(jnp.logical_not(is_lead))(arrange_coeffs)

    window = copy(own, sx, m_send.at[0], m_recv.at[0], (across, *here))
    pl.when(tm == 2)(window.start)

    def zero(n):
        return jnp.zeros((4, 2, n, 128), jnp.float32)

    def loop(low, high, body, unroll=True):
        def wrapped(z, _):
            body(z)
            return 0

        lax.fori_loop(low, high, wrapped, 0, unroll=unroll)

    for edge, begin, begin_coarse in ((slab == 0, 0, 0), (slab == slabs - 1, 8, 5)):

        @pl.when(edge)
        def _():
            def clear(z):
                for m in range(4):
                    co[m, z] = zero(8)
                    cw[m, z] = zero(8)
                for field in (sa, sb, bb.at[0], vr.at[0], vr.at[1]):
                    field[z] = zero(8)

            loop(begin, begin + 4, clear)
            for k in range(3):
                for z in range(begin_coarse, begin_coarse + 3):
                    e1[k, z] = jnp.zeros((2, 8, 128), jnp.float32)
            for k in range(2):

                @pl.when(tm == 1 + 2 * k)
                def _():
                    for z in (2, 3) if begin == 0 else (8, 9):
                        jj[k, z] = zero(8)

    for edge, z in ((slab == 1, 0), (slab == slabs - 2, 7)):

        @pl.when(edge)
        def _():
            for k in range(2):
                e1[k, z] = jnp.zeros((2, 8, 128), jnp.float32)

    for edge, begin in ((coarse == 0, 0), (coarse == coarses - 1, 6)):

        @pl.when(edge)
        def _():
            s = pl.ds(begin, 2)

            def clear(z):
                for m in range(4):
                    co[m, z, :, :, s, :] = zero(2)
                    cw[m, z, :, :, s, :] = zero(2)
                for field in (sa, sb, bb.at[0]):
                    field[z, :, :, s, :] = zero(2)

            loop(0, 12, clear)
            for z in range(3, 9):
                vr[1, z, :, :, s, :] = zero(2)
            for k in range(2):

                @pl.when(tm == 1 + 2 * k)
                def _():
                    for z in range(2, 10):
                        jj[k, z, :, :, s, :] = zero(2)

            for k in (1, 2):
                for z in range(8):
                    e1[k, z, :, s, :] = jnp.zeros((2, 2, 128), jnp.float32)

    arrive(state_copy)
    swap.wait_recv()
    pl.when(is_lead)(lambda: arrive(coeff_copy))
    pl.when(jnp.logical_not(is_lead))(lambda: arrive(coeff_pass))

    scales, carries, tildes = chebyshev_coefficients(SECTIONS)

    def fine_step(begin, finish):
        def first(z):
            centre, spread, drift = operator(begin, co, z)
            ta[z] = centre + tildes[1] * (spread - drift)

        def later(degree, current, before, put):
            def body(z):
                centre, spread, drift = operator(current, co, z)
                put(
                    z,
                    scales[degree] * centre
                    + carries[degree] * before[z]
                    + tildes[degree] * (spread - drift),
                )

            return body

        def put_to(ref):
            def put(z, value):
                ref[z] = value

            return put

        loop(1, 11, first)
        loop(2, 10, later(2, ta, begin, put_to(ua)))
        loop(3, 9, later(3, ua, ta, put_to(ta)))
        loop(4, 8, later(4, ta, ua, finish))

    def to_own_rows(target, z, value):
        target[z, :, :, 2:6, :] = value[:, :, 2:6, :]

    def to_fe(z, value):
        fe[z - 4] = value

    fine_step(sa, lambda z, value: to_own_rows(sb, z, value))
    start(step_copy, far)

    @pl.when(is_lead)
    def _():
        for n in range(8):
            _, _, there = at(-DIRS[n][0], -DIRS[n][1])
            pl.when(there)(lambda n=n: coeff_pass(n).start())

    pl.when(tm == 1)(lambda: start(more_copy, range(len(more)), more_dirs))

    arrive(step_copy)
    fine_step(sb, to_fe)

    def weigh(z):
        weight[z] = RELAX / (1.0 + 12.0 * co[0, z])

    def halves(value):
        value = value[:, 0] + value[:, 1]
        return 0.125 * jnp.concatenate([value[0:1] + value[1:2], value[2:3] + value[3:4]], 0)

    def coarse_weigh(q):
        for m in range(4):
            mean = halves(co[m, 2 * q - 2] + co[m, 2 * q - 1])
            cco[m, q] = mean
            if m == 0:
                cweight[q] = RELAX / (1.0 + 3.0 * mean)

    def merge(low, high, first, last):
        def body(z):
            for m in range(4):
                for part, sub in ((every, 0), (every, 7), (first, 1), (last, 6)):
                    at_rows = (m, z, part, slice(None), pl.ds(sub, 1), slice(None))
                    co[at_rows] = cw[at_rows]

        for z in range(low, high):
            body(z)

    def weights():
        loop(2, 10, weigh)
        loop(1, 7, coarse_weigh)

    ends = copy(fe, fx, m_send.at[1], m_recv.at[1], (sibling, *here))
    ends_first = copy(fe, res, m_send.at[1], m_recv.at[1], (sibling, *here))
    jump = copy(
        jo.at[own_box(4)], jj.at[(0, *own_box(4))], m_send.at[2], m_recv.at[2], (sibling, *here)
    )
    jump_box = (1, pl.ds(2, 8), every, both, pl.ds(1, 6))
    last_jump = copy(jj.at[jump_box], jj.at[jump_box], m_send.at[4], m_recv.at[4], (across, *here))
    third = copy(res, res, m_send.at[3], m_recv.at[3], (sibling, *here))
    cross_box = (2, *own_box(4))
    cross = [
        copy(a.at[box], a.at[box], x_send.at[n], x_recv.at[n], (across, *here))
        for n, (a, box) in enumerate(((bb, cross_box), (xout, own_box(0))))
    ]

    @pl.when(tm == 0)
    def _():
        window.wait_recv()
        for z in range(4):
            jo[z + 4] = fe[z] - sx[z]
        start(lambda n: jump_copy(jo, n)(0), far)
        jump.start()
        ends.start()
        ends_first.wait_recv()

    @pl.when(tm == 2)
    def _():
        ends.start()
        third.wait_recv()

    def solve_smooth(b):
        def smooth(z):
            centre, spread, drift = operator(b, co, z)
            v1[z] = centre + (2.0 * weight[z]) * (spread - drift)

        loop(3, 9, smooth)

    def solve_restrict(b, put, keep=False):
        def restrict(q):
            total = None
            for z in (2 * q - 2, 2 * q - 1):
                centre, spread, drift = operator(v1, co, z)
                misfit = b[z] - centre + 2.0 * (spread - drift)
                if keep:
                    xout[z - 4] = centre + weight[z] * misfit
                total = misfit if total is None else total + misfit
            put(q, cweight[q] * halves(total))

        loop(3, 5, restrict)

    def solve_correct(e, base, reach):
        for q in range(3 - reach, 5 + reach):
            centre, spread, drift = operator(e, cco, q, fine=False)
            w = cweight[q]
            wide = spread_out((2.0 - w) * centre + w * (0.5 * spread - drift))
            for z in (2 * q - 2, 2 * q - 1):
                if z >= 4 - 2 * reach + (reach - 1) and z < 8 + 2 * reach - (reach - 1):
                    v2[z] = base(z) + wide

    def solve_finish(b, put, reach):
        def finish(z):
            centre, spread, drift = operator(v2, co, z)
            put(z, centre + weight[z] * (b[z] - centre + 2.0 * (spread - drift)))

        loop(4 - reach, 8 + reach, finish)

    def put_guess(k):
        def put(q, value):
            e1[k, q, :, 2:6, :] = value[:, 2:6, :]

        return put

    @pl.when(tm == 1)
    def _():
        b = bb.at[0]
        for z in range(4):
            b[z + 4, :, :, 2:6, :] = (fe[z] - own[z])[:, :, 2:6, :]
        start(first_copy, far)
        ends_first.start()
        arrive(more_copy, range(len(more)), more_dirs)
        merge(4, 8, pl.ds(0, 1), pl.ds(3, 1))
        for z in (3, 8):
            merge(z, z + 1, pl.ds(0, 2), pl.ds(2, 2))
        for z in (0, 11):
            for m in range(4):
                co[m, z, :, :, 2:6, :] = cw[m, z, :, :, 2:6, :]
        weights()
        arrive(first_copy)
        solve_smooth(b)
        start(smooth_layer_copy(0), along)

        def put_flat(q, value):
            e1[0, q] = value

        solve_restrict(b, put_flat)
        start(far_guess_copy(0), along, TWO)
        start(flat_guess_copy, along)
        arrive(smooth_layer_copy(0), along)
        arrive(flat_guess_copy, along)
        arrive(far_guess_copy(0), along, TWO)
        solve_correct(e1.at[0], lambda z: v1[z] if 3 <= z < 9 else vr[0, z], 2)
        arrive(lambda n: jump_copy(jo, n)(0))
        jump.wait_recv()
        b = bb.at[1]

        def put_first(z, value):
            bb[1, z] = value + jj[0, z]

        solve_finish(bb.at[0], put_first, 2)

        sent(smooth_layer_copy(0), along)
        solve_smooth(b)
        start(smooth_copy, beside)
        start(smooth_layer_copy(1), along)
        solve_restrict(b, put_guess(1))
        start(guess_copy, (4, 5, 6, 7, 2, 3))
        start(far_guess_copy(1), along, TWO)
        start(guess_copy, along)
        ends.wait_recv()
        for z in range(4):
            res[z] = fx[z] + (b[z + 4] - jj[0, z + 4])
        shape = (4, 2, 8, 128)
        i = lax.broadcasted_iota(jnp.int32, shape, 0)
        sub = lax.broadcasted_iota(jnp.int32, shape, 2)
        given = ((sub == 1) & (i > 0)) | ((sub == 6) & (i < 3))
        arrive(smooth_copy, beside)
        arrive(smooth_layer_copy(1), along)
        arrive(guess_copy)
        arrive(far_guess_copy(1), along, TWO)
        solve_correct(
            e1.at[1],
            lambda z: jnp.where(given, vr[1, z], v1[z]) if 3 <= z < 9 else vr[1, z],
            2,
        )
        last_jump.wait_recv()

        def put_second(z, value):
            bb[2, z] = value + jj[1, z]

        solve_finish(b, put_second, 2)

        b = bb.at[2]
        cross[0].start()
        sent(smooth_copy, beside)
        sent(smooth_layer_copy(1), along)
        solve_smooth(b)
        solve_restrict(b, put_guess(2), keep=True)
        start(last_guess_copy, far)
        last_guess_copy(8).start()
        cross[1].start()

    @pl.when(tm == 3)
    def _():
        for z in range(4):
            value = fe[z] - own[z]
            jo[z + 4] = value
            to_own_rows(jj.at[1], z + 4, value)
        start(lambda n: jump_copy(jo, n)(1), far)
        weights()
        arrive(lambda n: jump_copy(jo, n)(1))
        last_jump.start()
        b = bb.at[2]
        cross[0].wait_recv()
        for z in range(4):
            res[z] = b[z + 4] + own[z]
        third.start()
        arrive(last_guess_copy)
        last_guess_copy(8).wait_recv()
        solve_correct(e1.at[2], lambda z: 0.0, 1)
        ends.wait_recv()
        cross[1].wait_recv()
        third.wait_send()
        for z in range(4, 8):
            centre, spread, drift = operator(v2, co, z)
            change = centre + weight[z] * (2.0 * (spread - drift) - centre)
            res[z - 4] = fx[z - 4] + xout[z - 4] + change

    for z in range(4):
        for p in range(2):
            for i in range(4):
                dealt[0, z, p, pl.ds(i, 4, stride=4), :] = res[z, i, p, 2:6, :]
        low_part, high_part = join_columns(dealt[0, z, 0], dealt[0, z, 1])
        o_ref[z, :, 0:128] = low_part
        o_ref[z, :, 128:256] = high_part

    sent(state_copy)
    swap.wait_send()
    sent(step_copy)

    @pl.when(is_lead)
    def _():
        sent(coeff_copy)
        for n in range(8):
            _, _, there = at(-DIRS[n][0], -DIRS[n][1])
            pl.when(there)(lambda n=n: coeff_pass(n).wait_send())

    @pl.when(tm == 0)
    def _():
        sent(lambda n: jump_copy(jo, n)(0))
        jump.wait_send()
        ends.wait_send()

    @pl.when(tm == 2)
    def _():
        window.wait_send()
        ends.wait_send()

    @pl.when(tm == 1)
    def _():
        sent(more_copy, range(len(more)), more_dirs)
        sent(first_copy)
        ends_first.wait_send()
        sent(flat_guess_copy, along)
        sent(far_guess_copy(0), along, TWO)
        sent(guess_copy)
        sent(far_guess_copy(1), along, TWO)
        sent(last_guess_copy)
        last_guess_copy(8).wait_send()
        for part in cross:
            part.wait_send()

    @pl.when(tm == 3)
    def _():
        sent(lambda n: jump_copy(jo, n)(1))
        last_jump.wait_send()


def per_device(states, diffusivity, velocity):
    def vmem(*shape):
        return pltpu.VMEM(shape + (8, 128), jnp.float32)

    dma = pltpu.SemaphoreType.DMA
    block = pl.BlockSpec(memory_space=pltpu.HBM)
    raw = (states[0], diffusivity, velocity)
    counts = (9, 8, 8, 14, 8, 8, 25, 24, 3, 5)
    out = pl.pallas_call(
        kernel,
        name="parareal",
        out_shape=jax.ShapeDtypeStruct(diffusivity.shape, jnp.float32),
        in_specs=[block] * 3,
        out_specs=pl.BlockSpec(memory_space=pltpu.VMEM),
        scratch_shapes=[pltpu.VMEM(array.shape, jnp.float32) for array in raw]
        + [
            vmem(4, 4, 2),
            vmem(4, 12, 4, 2),
            vmem(4, 12, 4, 2),
            vmem(12, 4, 2),
            vmem(12, 4, 2),
            vmem(12, 4, 2),
            vmem(12, 4, 2),
            vmem(12, 4, 2),
            vmem(4, 4, 2),
            vmem(12, 4, 2),
            vmem(2, 12, 4, 2),
            vmem(3, 12, 4, 2),
            vmem(12, 4, 2),
            vmem(12, 4, 2),
            vmem(2, 12, 4, 2),
            vmem(3, 8, 2),
            vmem(4, 8, 2),
            vmem(8, 2),
            vmem(4, 4, 2),
            vmem(4, 4, 2),
            vmem(4, 4, 2),
            vmem(4, 4, 2),
            pltpu.VMEM((5, 4, 2, 16, 128), jnp.float32),
            dma((3,)),
        ]
        + [dma((n,)) for n in counts for _ in range(2)],
        compiler_params=pltpu.CompilerParams(
            collective_id=0, has_side_effects=True, vmem_limit_bytes=55168 * 1024
        ),
    )(*raw)
    return out[None]


def solution(mesh):
    return jax.shard_map(
        per_device,
        mesh=mesh,
        in_specs=(
            P("tm", "slab", "coarse", None),
            P("slab", "coarse", None),
            P(None, "slab", "coarse", None),
        ),
        out_specs=P("tm", "slab", "coarse", None),
        check_vma=False,
    )
```
